32 devices in a mesh: section: 4 (over z), dp: 2 (over x), tensor: 4 (over y, core).
Axes of the slice: x: 2, y: 2, z: 4, core: 2. Of those that a mesh axis runs over, the one named last changes fastest.
Arguments:
- inputs: bfloat16 [4, 2, 256, 3584], P('section', 'dp', None, 'tensor'), may hold values from -8 to 8
- qkv_weight: bfloat16 [4, 3, 3584, 3584], P('section', None, 'dp', 'tensor')
- norm_gain: bfloat16 [4, 3584], P('section'), may hold values from 0.25 to 1.75
- preempted: int32 [4], P('section'), may hold values 0 or 1
Outputs:
- outputs: bfloat16 [4, 2, 256, 3584], P('section', 'dp', None, 'tensor')
The draws below stay inside these ranges and needn't reach their ends.
All inputs are finite; a program needn't handle non-finite values. No bound on the sum of `preempted` on one device may be relied on, other than what follows from the above.
Results may differ from the reference program's by a relative error of at most 0.008.
Values may be sent and summed in bfloat16 or wider, within the bound.
No kernel may reach another device: no remote copies, remote signals or barrier semaphores. Data moves between devices by JAX's collectives and lax.ppermute only.
A program may use at most 64 MiB of HBM per device.

```python
import math
import jax
import jax.numpy as jnp
from jax import lax

HEADS = 28
HD = 128
D = 3584
LEN = 256
SEQS = 2
SECTIONS = 4


def draw_inputs(key, part):
    key = jax.random.fold_in(key, 11)
    full_shape = (SECTIONS, SEQS, LEN, D)
    return jnp.clip(jax.random.normal(key, full_shape, jnp.float32), -6.0, 6.0).astype(jnp.bfloat16)


def draw_qkv_weight(key, part):
    key = jax.random.fold_in(key, 23)
    fan_scale = 1.0 / math.sqrt(D)

    def one_section(section_index):
        section_key = jax.random.fold_in(key, section_index)
        key_first = jax.random.fold_in(section_key, 0)
        return jnp.clip(jax.random.normal(key_first, (3, D, D), jnp.float32), -6.0, 6.0) * fan_scale
    return lax.map(one_section, jnp.arange(SECTIONS)).astype(jnp.bfloat16)


def plant(entries, rng, least, top_value):
    longest = entries.shape.index(max(entries.shape))
    spots = []
    for shift in (0, 1):
        where = [jax.random.randint(jax.random.fold_in(rng, axis), (), 0, length) for axis, length in enumerate(entries.shape)]
        where[longest] = (where[longest] + shift) % entries.shape[longest]
        spots.append(tuple(where))
    return entries.at[spots[0]].set(least).at[spots[1]].set(top_value)


def setup_inputs(seed: int = 0) -> dict:
    key_of = jax.random.split(jax.random.key(seed), 5)
    return {
        "inputs": draw_inputs(jax.random.fold_in(key_of[4], 71), 0),
        "qkv_weight": draw_qkv_weight(jax.random.fold_in(key_of[4], 71), 0),
        "norm_gain": jnp.clip(1.0 + 0.15 * jax.random.normal(key_of[2], (SECTIONS, D), jnp.float32), 0.25, 1.75).astype(jnp.bfloat16),
        "preempted": plant((jax.random.randint(key_of[3], (SECTIONS,), 0, 4) < 1).astype(jnp.int32), jax.random.fold_in(key_of[3], 1), 0, 1),
    }


def attention_layer(hidden_in, weight, gain_row):
    float_acts = hidden_in.astype(jnp.float32)
    inverse_rms = lax.rsqrt(lax.optimization_barrier(jnp.mean(float_acts * float_acts, axis=-1, keepdims=True)) + 1e-05)
    normed = (float_acts * inverse_rms * gain_row).astype(jnp.bfloat16)
    flat_rows = normed.reshape(-1, D)
    head_shape = (hidden_in.shape[0], LEN, HEADS, HD)
    queries = jnp.dot(flat_rows, weight[0], preferred_element_type=jnp.float32).astype(jnp.bfloat16).reshape(head_shape)
    key_rows = jnp.dot(flat_rows, weight[1], preferred_element_type=jnp.float32).astype(jnp.bfloat16).reshape(head_shape)
    values = jnp.dot(flat_rows, weight[2], preferred_element_type=jnp.float32).astype(jnp.bfloat16).reshape(head_shape)
    scores = jnp.einsum('sqhd,skhd->shqk', queries.astype(jnp.float32), key_rows.astype(jnp.float32)) / jnp.sqrt(jnp.float32(HD))
    causal = jnp.arange(LEN)[:, None] >= jnp.arange(LEN)[None, :]
    scores = jnp.where(causal, scores, jnp.float32(-1e+30))
    probability = jax.nn.softmax(scores, axis=-1).astype(jnp.bfloat16)
    mixture = jnp.einsum('shqk,skhd->sqhd', probability.astype(jnp.float32), values.astype(jnp.float32))
    return (float_acts + mixture.reshape(hidden_in.shape)).astype(jnp.bfloat16)

def reference(inputs, qkv_weight, norm_gain, preempted):
    own_out = lax.map(lambda section_item: attention_layer(section_item[0], section_item[1], section_item[2]), (inputs, qkv_weight, norm_gain))
    before = jnp.concatenate([jnp.zeros_like(own_out[:1]), own_out[:-1]], axis=0)
    shadow = lax.map(lambda section_item: attention_layer(section_item[0], section_item[1], section_item[2]), (before, qkv_weight, norm_gain))
    return jnp.where((preempted == 1)[:, None, None, None], shadow, own_out)
```

```python
import jax
import jax.numpy as jnp
from jax import lax
from jax.sharding import PartitionSpec as P

HD = 128
EPS = 1e-05
AXES = ("section", "dp", "tensor")
F32 = jnp.float32
BF16 = jnp.bfloat16


def permute(array, sections, hop):
    pairs = []
    for s in range(sections):
        for d in range(2):
            for y in range(2):
                for c in range(2):
                    to = hop(s, d, y, c)
                    if to is None or not 0 <= to[0] < sections:
                        continue
                    ts, td, ty, tc = to
                    pairs.append((s * 8 + d * 4 + y * 2 + c, ts * 8 + td * 4 + ty * 2 + tc))
    return lax.ppermute(array, AXES, pairs)


def ring(s, d, y, c):
    return (s, 1 - d, y, c) if d != y else (s, d, 1 - y, c)


def across(s, d, y, c):
    return (s, 1 - d, 1 - y, c) if d != y else None


def sibling(s, d, y, c):
    return (s, d, y, 1 - c)


def peer(s, d, y, c):
    return (s, 1 - d, y, c)


def onward(s, d, y, c):
    return (s + 1, d, y, c)


def chunks_of(heads):
    sizes = []
    while heads > 0:
        sizes.append(min(2, heads))
        heads -= sizes[-1]
    return sizes


def collect(block, sections, d, y, c):
    on_diagonal = d == y
    from_ring = permute(block, sections, ring)
    from_across = permute(block, sections, across)
    mine = jnp.where(on_diagonal, block, from_ring)
    other = jnp.where(on_diagonal, from_ring, from_across)
    both = jnp.stack([other, mine])
    theirs = permute(both, sections, sibling)
    return jnp.where(
        c == 0,
        jnp.concatenate([both, theirs], axis=-1),
        jnp.concatenate([theirs, both], axis=-1),
    )


def layer(block, weight, gain_half, sections, d, y, c):
    length, width = block.shape
    half = weight.shape[1]
    rows = collect(block, sections, d, y, c).astype(F32)
    squares = jnp.sum(rows * rows, axis=-1, keepdims=True)
    mean_half = squares / half
    normed = (rows * lax.rsqrt(mean_half + EPS) * gain_half).astype(BF16)
    peer_mean = permute(mean_half[0], sections, peer)
    inverse = lax.rsqrt((mean_half[1] + peer_mean) * 0.5 + EPS)
    scale_own = inverse * jnp.sqrt(mean_half[1] + EPS)
    scale_peer = inverse * jnp.sqrt(peer_mean + EPS)
    causal = jnp.arange(length)[:, None] >= jnp.arange(length)[None, :]
    outs = []
    start = 0
    for heads in chunks_of(width // HD):
        columns = slice(start * HD, (start + heads) * HD)
        start += heads
        part = weight[:, :, columns]
        sent = jnp.einsum("rd,kde->kre", normed[0], part, preferred_element_type=F32).astype(BF16)
        received = permute(sent, sections, peer)
        kept = jnp.einsum("rd,kde->kre", normed[1], part, preferred_element_type=F32)
        total = (kept * scale_own + received.astype(F32) * scale_peer).astype(BF16)
        queries, keys, values = total.reshape(3, length, heads, HD)
        scores = jnp.einsum("qhd,khd->hqk", queries, keys, preferred_element_type=F32) / jnp.sqrt(F32(HD))
        scores = jnp.where(causal, scores, F32(-1e30))
        probability = jax.nn.softmax(scores, axis=-1).astype(BF16)
        mixture = jnp.einsum("hqk,khd->qhd", probability, values, preferred_element_type=F32)
        outs.append((block[:, columns].astype(F32) + mixture.reshape(length, heads * HD)).astype(BF16))
    return jnp.concatenate(outs, axis=-1)


def solution(mesh):
    sections = mesh.shape["section"]

    def local(inputs, qkv_weight, norm_gain, preempted):
        d = lax.axis_index("dp")
        t = lax.axis_index("tensor")
        y, c = t // 2, t % 2
        weight = qkv_weight[0]
        half = weight.shape[1]
        gain_half = lax.dynamic_slice_in_dim(norm_gain[0], d * half, half)
        own = layer(inputs[0, 0], weight, gain_half, sections, d, y, c)
        before = permute(own, sections, onward)
        shadow = layer(before, weight, gain_half, sections, d, y, c)
        return jnp.where(preempted[0] == 1, shadow, own)[None, None]

    placed = (
        P("section", "dp", None, "tensor"),
        P("section", None, "dp", "tensor"),
        P("section", None),
        P("section"),
    )
    return jax.shard_map(
        local,
        mesh=mesh,
        in_specs=placed,
        out_specs=P("section", "dp", None, "tensor"),
        check_vma=False,
    )
```

```python
import functools
import math

import jax
import jax.numpy as jnp
from jax import lax
from jax.experimental import pallas as pl
from jax.experimental.pallas import tpu as pltpu
from jax.sharding import PartitionSpec as P

HD = 128
EPS = 1e-05
AXES = ("section", "dp", "tensor")
F32 = jnp.float32
BF16 = jnp.bfloat16
PARTS = 2
WIDE = 2 * HD
VMEM_BYTES = 40 * 1024 * 1024


def permute(array, sections, hop):
    pairs = []
    for s in range(sections):
        for d in range(2):
            for y in range(2):
                for c in range(2):
                    to = hop(s, d, y, c)
                    if to is None or not 0 <= to[0] < sections:
                        continue
                    ts, td, ty, tc = to
                    pairs.append((s * 8 + d * 4 + y * 2 + c, ts * 8 + td * 4 + ty * 2 + tc))
    return lax.ppermute(array, AXES, pairs)


def direct(s, d, y, c):
    return (s, d, y, c)


def ring(s, d, y, c):
    return (s, 1 - d, y, c) if d != y else (s, d, 1 - y, c)


def across(s, d, y, c):
    return (s, 1 - d, 1 - y, c) if d != y else None


def sibling(s, d, y, c):
    return (s, d, y, 1 - c)


def peer(s, d, y, c):
    return (s, 1 - d, y, c)


def onward(hop):
    def moved(s, d, y, c):
        to = hop(s, d, y, c)
        return None if to is None else (to[0] + 1, *to[1:])

    return moved


def cost(microseconds):
    return pl.CostEstimate(flops=0, bytes_accessed=int(microseconds * 3.69e4), transcendentals=0)


def any_spec():
    return pl.BlockSpec(memory_space=pl.ANY)


def pick_kernel(place, block, from_ring, from_across, *refs):
    both = refs[-1]

    @pl.when(place[2] == 1)
    def _():
        both[0] = from_ring[...]
        both[1] = block[...]

    @pl.when(place[2] == 0)
    def _():
        both[0] = from_across[...]
        both[1] = from_ring[...]


def pick(place, block, from_ring, from_across, after):
    in_smem = pl.BlockSpec(memory_space=pltpu.SMEM)
    in_vmem = pl.BlockSpec(memory_space=pltpu.VMEM)
    return pl.pallas_call(
        pick_kernel,
        in_specs=[in_smem, in_vmem, in_vmem, in_vmem] + [any_spec() for _ in after],
        out_shape=jax.ShapeDtypeStruct((2, *block.shape), BF16),
        cost_estimate=cost(0.8),
        name="pick",
    )(place, block, from_ring, from_across, *after)


def project_kernel(place, both, theirs, gain, weight, sent, kept, sent_mean, kept_mean, normed):
    rows, width = both.shape[1:]
    half = 2 * width

    @pl.when(pl.program_id(0) == 0)
    def _():
        core = place[0]
        first = pl.ds(pl.multiple_of(core * width, HD), width)
        second = pl.ds(pl.multiple_of((1 - core) * width, HD), width)
        for seq, mean_ref in ((0, sent_mean), (1, kept_mean)):
            mine = both[seq].astype(F32)
            their = theirs[seq].astype(F32)
            squares = jnp.sum(mine * mine, axis=-1, keepdims=True)
            squares += jnp.sum(their * their, axis=-1, keepdims=True)
            mean = squares * (1.0 / half)
            inverse = lax.rsqrt(mean + EPS)
            at = pl.ds(seq * rows, rows)
            normed[at, first] = (mine * inverse * gain[:, first].astype(F32)).astype(BF16)
            normed[at, second] = (their * inverse * gain[:, second].astype(F32)).astype(BF16)
            mean_ref[...] = jnp.transpose(jnp.broadcast_to(mean, (rows, HD)))[:8]

    for k in range(3):
        product = jnp.dot(normed[...], weight[0, k], preferred_element_type=F32)
        sent[k] = product[:rows].astype(BF16)
        kept[k] = product[rows:]


def project(place, both, theirs, gain, weight):
    rows, width = both.shape[1:]
    half = weight.shape[2]
    steps = pl.cdiv(width, WIDE)
    whole = lambda *shape: pl.BlockSpec(shape, lambda i, place: (0,) * len(shape))
    tall = pl.BlockSpec((3, rows, WIDE), lambda i, place: (0, 0, i))
    return pl.pallas_call(
        project_kernel,
        grid_spec=pltpu.PrefetchScalarGridSpec(
            num_scalar_prefetch=1,
            grid=(steps,),
            in_specs=[
                whole(2, rows, width),
                whole(2, rows, width),
                pl.BlockSpec((1, half), lambda i, place: (0, place[1])),
                pl.BlockSpec((1, 3, half, WIDE), lambda i, place: (0, 0, 0, i)),
            ],
            out_specs=[tall, tall, whole(8, rows), whole(8, rows)],
            scratch_shapes=[pltpu.VMEM((2 * rows, half), BF16)],
        ),
        out_shape=[
            jax.ShapeDtypeStruct((3, rows, width), BF16),
            jax.ShapeDtypeStruct((3, rows, width), F32),
            jax.ShapeDtypeStruct((8, rows), F32),
            jax.ShapeDtypeStruct((8, rows), F32),
        ],
        compiler_params=pltpu.CompilerParams(vmem_limit_bytes=VMEM_BYTES),
        cost_estimate=cost(3.5),
        name="project",
    )(place, both, theirs, gain, weight)


def column(row):
    return jnp.transpose(jnp.broadcast_to(row[:1], (HD, row.shape[1])))[:, :1]


def attend_kernel(chunk, last, flag, kept, received, kept_mean, peer_mean, block, own, *refs):
    earlier = refs[:chunk]
    out, pairs = refs[-2:]
    rows, width = block.shape
    mean_kept = column(kept_mean[...])
    mean_peer = column(peer_mean[...])
    inverse = lax.rsqrt((mean_kept + mean_peer) * 0.5 + EPS)
    scale_kept = inverse * jnp.sqrt(mean_kept + EPS)
    scale_peer = inverse * jnp.sqrt(mean_peer + EPS)
    causal = lax.broadcasted_iota(jnp.int32, (rows, rows), 0) >= lax.broadcasted_iota(
        jnp.int32, (rows, rows), 1
    )
    for head in range(width // HD):
        at = slice(head * HD, (head + 1) * HD)
        queries, keys, values = (
            (kept[k, :, at] * scale_kept + received[k, :, at].astype(F32) * scale_peer).astype(BF16)
            for k in range(3)
        )
        pairs[0, :, at] = keys
        pairs[1, :, at] = values
        held = [(ref[0, :, at], ref[1, :, at]) for ref in earlier] + [(keys, values)]
        scores = [
            lax.dot_general(queries, key, (((1,), (1,)), ((), ())), preferred_element_type=F32)
            * (1.0 / math.sqrt(HD))
            for key, _ in held
        ]
        scores[-1] = jnp.where(causal, scores[-1], F32(-1e30))
        top = functools.reduce(
            jnp.maximum, [jnp.max(score, axis=-1, keepdims=True) for score in scores]
        )
        raised = [jnp.exp(score - top) for score in scores]
        total = sum(jnp.sum(item, axis=-1, keepdims=True) for item in raised)
        over = 1.0 / total
        mixture = sum(
            jnp.dot((item * over).astype(BF16), value, preferred_element_type=F32)
            for item, (_, value) in zip(raised, held)
        )
        result = block[:, at].astype(F32) + mixture
        if last:
            result = jnp.where(flag[0] == 1, result, own[:, at].astype(F32))
        out[:, at] = result.astype(BF16)


def attend(last, flag, sums, block, own, earlier, after):
    rows, width = block.shape
    chunk = len(earlier)
    in_vmem = pl.BlockSpec(memory_space=pltpu.VMEM)
    return pl.pallas_call(
        functools.partial(attend_kernel, chunk, last),
        in_specs=[pl.BlockSpec(memory_space=pltpu.SMEM)]
        + [in_vmem] * (6 + chunk)
        + [any_spec() for _ in after],
        out_shape=[
            jax.ShapeDtypeStruct((rows, width), BF16),
            jax.ShapeDtypeStruct((2, rows, width), BF16),
        ],
        compiler_params=pltpu.CompilerParams(vmem_limit_bytes=VMEM_BYTES),
        cost_estimate=cost(2.5),
        name="attend",
    )(flag, *sums, block, own, *earlier, *after)


def solution(mesh):
    sections = mesh.shape["section"]

    def local(inputs, qkv_weight, norm_gain, preempted):
        d = lax.axis_index("dp")
        t = lax.axis_index("tensor")
        y, c = t // 2, t % 2
        place = jnp.stack([c, d, (d == y).astype(c.dtype)]).astype(jnp.int32)

        def partial(block, from_ring, from_across, after):
            both = pick(place, block, from_ring, from_across, after)
            theirs = permute(both, sections, sibling)
            sent, kept, sent_mean, kept_mean = project(place, both, theirs, norm_gain, qkv_weight)
            peer_mean = permute(sent_mean, sections, peer)
            received = permute(sent, sections, peer)
            return kept, received, kept_mean, peer_mean

        block = inputs[0, 0]
        rows = block.shape[0] // PARTS
        blocks = [block[i * rows : (i + 1) * rows] for i in range(PARTS)]
        moved = [(permute(part, sections, ring), permute(part, sections, across)) for part in blocks]
        sums = []
        after = []
        for part, pair in zip(blocks, moved):
            sums.append(partial(part, *pair, after))
            after = [sums[-1][2]]
        owns, befores, held = [], [], []
        for part, item in zip(blocks, sums):
            own, pairs = attend(False, preempted, item, part, part, held, after)
            held.append(pairs)
            owns.append(own)
            before = permute(own, sections, onward(direct))
            befores.append(
                (before, permute(own, sections, onward(ring)), permute(own, sections, onward(across)))
            )
            after = [before]
        sums, after = [], [owns[-1]]
        for three in befores:
            sums.append(partial(*three, after))
            after = [sums[-1][2]]
        outs, held = [], []
        for own, three, item in zip(owns, befores, sums):
            out, pairs = attend(True, preempted, item, three[0], own, held, after)
            held.append(pairs)
            outs.append(out)
        return jnp.concatenate(outs)[None, None]

    placed = (
        P("section", "dp", None, "tensor"),
        P("section", None, "dp", "tensor"),
        P("section", None),
        P("section"),
    )
    return jax.shard_map(
        local,
        mesh=mesh,
        in_specs=placed,
        out_specs=P("section", "dp", None, "tensor"),
        check_vma=False,
    )
```

```python
import functools
import math

import jax
import jax.numpy as jnp
from jax import lax
from jax.experimental import pallas as pl
from jax.experimental.pallas import tpu as pltpu
from jax.sharding import PartitionSpec as P

HD = 128
EPS = 1e-05
AXES = ("section", "dp", "tensor")
F32 = jnp.float32
BF16 = jnp.bfloat16
PARTS = 2
WIDE = 2 * HD
VMEM_BYTES = 16 * 1024 * 1024
STAT_ROWS = 16


def permute(array, sections, hop):
    pairs = []
    for s in range(sections):
        for d in range(2):
            for y in range(2):
                for c in range(2):
                    to = hop(s, d, y, c)
                    if to is None or not 0 <= to[0] < sections:
                        continue
                    ts, td, ty, tc = to
                    pairs.append((s * 8 + d * 4 + y * 2 + c, ts * 8 + td * 4 + ty * 2 + tc))
    return lax.ppermute(array, AXES, pairs)


def ring(s, d, y, c):
    return (s, 1 - d, y, c) if d != y else (s, d, 1 - y, c)


def cross(s, d, y, c):
    return (s, 1 - d, 1 - y, c) if d != y else (s, d, y, c)


def direct(s, d, y, c):
    return (s, d, y, c) if d != y else None


def sibling(s, d, y, c):
    return (s, d, y, 1 - c)


def peer(s, d, y, c):
    return (s, 1 - d, y, c)


def onward(hop):
    def moved(s, d, y, c):
        to = hop(s, d, y, c)
        return None if to is None else (to[0] + 1, *to[1:])

    return moved


def cost(microseconds):
    return pl.CostEstimate(flops=int(microseconds * 1.15e9), bytes_accessed=1000, transcendentals=0)


def any_spec():
    return pl.BlockSpec(memory_space=pl.ANY)


def vmem_spec():
    return pl.BlockSpec(memory_space=pltpu.VMEM)


def smem_spec():
    return pl.BlockSpec(memory_space=pltpu.SMEM)


def stage_kernel(weight, staged, semaphore):
    copy = pltpu.make_async_copy(weight, staged, semaphore)
    copy.start()
    copy.wait()


def stage(weight):
    return pl.pallas_call(
        stage_kernel,
        in_specs=[any_spec()],
        out_specs=vmem_spec(),
        out_shape=pltpu.VMEM(weight.shape, weight.dtype),
        scratch_shapes=[pltpu.SemaphoreType.DMA(())],
        compiler_params=pltpu.CompilerParams(vmem_limit_bytes=VMEM_BYTES),
        cost_estimate=cost(4),
        name="stage",
    )(weight)


def project_kernel(start, place, crossed, ringed, sib_crossed, sib_ringed, gain, weight, *refs):
    sent, kept, kept_mean, normed = refs[-4:]
    rows = normed.shape[0] // 2
    width = crossed.shape[1]
    half = 2 * width
    core, dp, diagonal = place[0], place[1], place[2]
    means = []
    for mine, theirs, offset in (
        (crossed, sib_crossed, diagonal),
        (ringed, sib_ringed, 1 - diagonal),
    ):
        at = pl.ds(pl.multiple_of(offset * rows, rows), rows)
        pieces = [ref[start : start + rows].astype(F32) for ref in (mine, theirs)]
        squares = sum(jnp.sum(piece * piece, axis=-1, keepdims=True) for piece in pieces)
        mean = squares * (1.0 / half)
        means.append(mean)
        inverse = lax.rsqrt(mean + EPS)
        for piece, order in zip(pieces, (core, 1 - core)):
            gains = gain[:, pl.ds(pl.multiple_of(dp * half + order * width, HD), width)]
            normed[at, pl.ds(pl.multiple_of(order * width, HD), width)] = (
                piece * inverse * gains.astype(F32)
            ).astype(BF16)
    on_diagonal = diagonal == 1
    sent_mean = jnp.where(on_diagonal, means[1], means[0])
    kept_mean[...] = jnp.where(on_diagonal, means[0], means[1])
    row = jnp.transpose(jnp.broadcast_to(sent_mean, (rows, HD)))[:STAT_ROWS]
    high = row.astype(BF16).astype(F32)
    mid = (row - high).astype(BF16).astype(F32)
    low = row - high - mid
    which = lax.broadcasted_iota(jnp.int32, row.shape, 0)
    stat = jnp.where(which == 0, high, jnp.where(which == 1, mid, low))
    for begin in range(0, width, rows):
        sent[3 * rows :, begin : begin + rows] = stat.astype(BF16)
    for begin in range(0, width, WIDE):
        at = slice(begin, min(begin + WIDE, width))
        for k in range(3):
            product = jnp.dot(normed[...], weight[0, k, :, at], preferred_element_type=F32)
            sent[k * rows : (k + 1) * rows, at] = product[:rows].astype(BF16)
            kept[k, :, at] = product[rows:]


def project(start, rows, place, four, gain, weight, after):
    width = four[0].shape[1]
    return pl.pallas_call(
        functools.partial(project_kernel, start),
        in_specs=[smem_spec()] + [vmem_spec()] * 6 + [any_spec() for _ in after],
        out_shape=[
            jax.ShapeDtypeStruct((3 * rows + STAT_ROWS, width), BF16),
            jax.ShapeDtypeStruct((3, rows, width), F32),
            jax.ShapeDtypeStruct((rows, 1), F32),
        ],
        scratch_shapes=[pltpu.VMEM((2 * rows, 2 * width), BF16)],
        compiler_params=pltpu.CompilerParams(vmem_limit_bytes=VMEM_BYTES),
        cost_estimate=cost(3.0),
        name="project",
    )(place, *four, gain, weight, *after)


def attend_kernel(
    chunk, last, place, flag, kept, received, kept_mean, crossed, block, own, *refs
):
    earlier = refs[:chunk]
    earlier_outs = refs[chunk : 2 * chunk] if last else ()
    out, pairs = refs[-2:]
    rows, width = own.shape
    out_start = rows * len(earlier_outs)
    for i, ref in enumerate(earlier_outs):
        out[i * rows : (i + 1) * rows] = ref[...]
    stat = received[3 * rows :, :rows].astype(F32)
    row = stat[0:1] + stat[1:2] + stat[2:3]
    mean_peer = jnp.transpose(jnp.broadcast_to(row, (HD, rows)))[:, :1]
    mean_kept = kept_mean[...]
    inverse = lax.rsqrt((mean_kept + mean_peer) * 0.5 + EPS)
    scale_kept = inverse * jnp.sqrt(mean_kept + EPS)
    scale_peer = inverse * jnp.sqrt(mean_peer + EPS)
    causal = lax.broadcasted_iota(jnp.int32, (rows, rows), 0) >= lax.broadcasted_iota(
        jnp.int32, (rows, rows), 1
    )
    for head in range(width // HD):
        at = slice(head * HD, (head + 1) * HD)
        queries, keys, values = (
            (
                kept[k, :, at] * scale_kept
                + received[k * rows : (k + 1) * rows, at].astype(F32) * scale_peer
            ).astype(BF16)
            for k in range(3)
        )
        pairs[0, :, at] = keys
        pairs[1, :, at] = values
        held = [(ref[0, :, at], ref[1, :, at]) for ref in earlier] + [(keys, values)]
        scores = [
            lax.dot_general(queries, key, (((1,), (1,)), ((), ())), preferred_element_type=F32)
            * (1.0 / math.sqrt(HD))
            for key, _ in held
        ]
        scores[-1] = jnp.where(causal, scores[-1], F32(-1e30))
        top = functools.reduce(
            jnp.maximum, [jnp.max(score, axis=-1, keepdims=True) for score in scores]
        )
        raised = [jnp.exp(score - top) for score in scores]
        total = sum(jnp.sum(item, axis=-1, keepdims=True) for item in raised)
        over = 1.0 / total
        mixture = sum(
            jnp.dot((item * over).astype(BF16), value, preferred_element_type=F32)
            for item, (_, value) in zip(raised, held)
        )
        residual = block[:, at].astype(F32)
        if last:
            residual = jnp.where(place[2] == 1, crossed[:, at].astype(F32), residual)
        result = residual + mixture
        if last:
            result = jnp.where(flag[0] == 1, result, own[:, at].astype(F32))
        out[out_start : out_start + rows, at] = result.astype(BF16)


def attend(last, place, flag, sums, crossed, block, own, earlier, outs, after):
    rows, width = own.shape
    chunk = len(earlier)
    return pl.pallas_call(
        functools.partial(attend_kernel, chunk, last),
        in_specs=[smem_spec()] * 2
        + [vmem_spec()] * (6 + chunk + len(outs))
        + [any_spec() for _ in after],
        out_shape=[
            jax.ShapeDtypeStruct(((len(outs) + 1) * rows, width), BF16),
            jax.ShapeDtypeStruct((2, rows, width), BF16),
        ],
        compiler_params=pltpu.CompilerParams(vmem_limit_bytes=VMEM_BYTES),
        cost_estimate=cost(250),
        name="attend",
    )(place, flag, *sums, crossed, block, own, *earlier, *outs, *after)


def solution(mesh):
    sections = mesh.shape["section"]

    def local(inputs, qkv_weight, norm_gain, preempted):
        d = lax.axis_index("dp")
        t = lax.axis_index("tensor")
        y, c = t // 2, t % 2
        place = jnp.stack([c, d, (d == y).astype(c.dtype)]).astype(jnp.int32)
        weight = stage(qkv_weight)

        def spread(crossed, ringed):
            return (
                crossed,
                ringed,
                permute(crossed, sections, sibling),
                permute(ringed, sections, sibling),
            )

        def partial(start, four, after):
            sent, kept, kept_mean = project(start, rows, place, four, norm_gain, weight, after)
            return kept, permute(sent, sections, peer), kept_mean

        block = inputs[0, 0]
        rows = block.shape[0] // PARTS
        starts = range(0, block.shape[0], rows)
        pair = permute(block, sections, cross), permute(block, sections, ring)
        *pair, weight = lax.optimization_barrier((*pair, weight))
        weight = pltpu.with_memory_space_constraint(weight, pltpu.VMEM)
        four = spread(*pair)
        sums, after = [], []
        for start in starts:
            sums.append(partial(start, four, after))
            after = [sums[-1][2]]
        owns, moved, held = [], [], []
        for start, item in zip(starts, sums):
            part = block[start : start + rows]
            own, pairs = attend(False, place, preempted, item, part, part, part, held, [], after)
            held.append(pairs)
            owns.append(own)
            crossed = permute(own, sections, onward(cross))
            ringed = permute(own, sections, onward(ring))
            moved.append(((crossed, ringed), permute(own, sections, onward(direct))))
            after = [crossed]
        sums, after = [], owns[-1]
        for i, (pair, _) in enumerate(moved):
            if i:
                pair = lax.optimization_barrier((*pair, after))[:2]
            four = spread(*pair)
            sums.append(partial(0, four, [after]))
            after = sums[-1][2]
        outs, held = [], []
        for own, (pair, before), item in zip(owns, moved, sums):
            out, pairs = attend(
                True, place, preempted, item, pair[0], before, own, held, outs, [after]
            )
            held.append(pairs)
            outs.append(out)
        return outs[-1][None, None]

    placed = (
        P("section", "dp", None, "tensor"),
        P("section", None, "dp", "tensor"),
        P("section", None),
        P("section"),
    )
    return jax.shard_map(
        local,
        mesh=mesh,
        in_specs=placed,
        out_specs=P("section", "dp", None, "tensor"),
        check_vma=False,
    )
```

```python
import functools
import math

import jax
import jax.numpy as jnp
from jax import lax
from jax.experimental import pallas as pl
from jax.experimental.pallas import tpu as pltpu
from jax.sharding import PartitionSpec as P

HD = 128
EPS = 1e-05
AXES = ("section", "dp", "tensor")
F32 = jnp.float32
BF16 = jnp.bfloat16
PARTS = 2
WIDE = 2 * HD
VMEM_BYTES = 16 * 1024 * 1024
STAT_ROWS = 16


def permute(array, sections, hop):
    pairs = []
    for s in range(sections):
        for d in range(2):
            for y in range(2):
                for c in range(2):
                    to = hop(s, d, y, c)
                    if to is None or not 0 <= to[0] < sections:
                        continue
                    ts, td, ty, tc = to
                    pairs.append((s * 8 + d * 4 + y * 2 + c, ts * 8 + td * 4 + ty * 2 + tc))
    return lax.ppermute(array, AXES, pairs)


def ring(s, d, y, c):
    return (s, 1 - d, y, c) if d != y else (s, d, 1 - y, c)


def cross(s, d, y, c):
    return (s, 1 - d, 1 - y, c) if d != y else (s, d, y, c)


def direct(s, d, y, c):
    return (s, d, y, c) if d != y else None


def across_y(s, d, y, c):
    return (s, d, 1 - y, c) if d != y else None


def across_x(s, d, y, c):
    return (s, 1 - d, y, c) if d == y else None


def sibling(s, d, y, c):
    return (s, d, y, 1 - c)


def peer(s, d, y, c):
    return (s, 1 - d, y, c)


def onward(hop):
    def moved(s, d, y, c):
        to = hop(s, d, y, c)
        return None if to is None else (to[0] + 1, *to[1:])

    return moved


def cost(microseconds):
    return pl.CostEstimate(flops=int(microseconds * 1.15e9), bytes_accessed=1000, transcendentals=0)


def any_spec():
    return pl.BlockSpec(memory_space=pl.ANY)


def vmem_spec():
    return pl.BlockSpec(memory_space=pltpu.VMEM)


def smem_spec():
    return pl.BlockSpec(memory_space=pltpu.SMEM)


def stage_kernel(place, weight, staged, semaphore):
    copy = pltpu.make_async_copy(weight, staged, semaphore)
    copy.start()
    copy.wait()


def stage(place, weight):
    return pl.pallas_call(
        stage_kernel,
        in_specs=[smem_spec(), any_spec()],
        out_specs=vmem_spec(),
        out_shape=pltpu.VMEM(weight.shape, weight.dtype),
        scratch_shapes=[pltpu.SemaphoreType.DMA(())],
        compiler_params=pltpu.CompilerParams(vmem_limit_bytes=VMEM_BYTES),
        cost_estimate=cost(4),
        name="stage",
    )(place, weight)


def project_kernel(place, crossed, ringed, sib_crossed, sib_ringed, gain, weight, *refs):
    sent, kept, kept_mean, normed = refs
    rows = normed.shape[0] // 2
    width = crossed.shape[1]
    half = 2 * width
    core, dp, diagonal = place[0], place[1], place[2]
    means = []
    for mine, theirs, offset in (
        (crossed, sib_crossed, diagonal),
        (ringed, sib_ringed, 1 - diagonal),
    ):
        at = pl.ds(pl.multiple_of(offset * rows, rows), rows)
        pieces = [ref[...].astype(F32) for ref in (mine, theirs)]
        squares = sum(jnp.sum(piece * piece, axis=-1, keepdims=True) for piece in pieces)
        mean = squares * (1.0 / half)
        means.append(mean)
        inverse = lax.rsqrt(mean + EPS)
        for piece, order in zip(pieces, (core, 1 - core)):
            gains = gain[:, pl.ds(pl.multiple_of(dp * half + order * width, HD), width)]
            normed[at, pl.ds(pl.multiple_of(order * width, HD), width)] = (
                piece * inverse * gains.astype(F32)
            ).astype(BF16)
    on_diagonal = diagonal == 1
    sent_mean = jnp.where(on_diagonal, means[1], means[0])
    kept_mean[...] = jnp.where(on_diagonal, means[0], means[1])
    row = jnp.transpose(jnp.broadcast_to(sent_mean, (rows, HD)))[:STAT_ROWS]
    high = row.astype(BF16).astype(F32)
    mid = (row - high).astype(BF16).astype(F32)
    low = row - high - mid
    which = lax.broadcasted_iota(jnp.int32, row.shape, 0)
    stat = jnp.where(which == 0, high, jnp.where(which == 1, mid, low))
    for begin in range(0, width, rows):
        sent[3 * rows :, begin : begin + rows] = stat.astype(BF16)
    for begin in range(0, width, WIDE):
        at = slice(begin, min(begin + WIDE, width))
        for k in range(3):
            product = jnp.dot(normed[...], weight[0, k, :, at], preferred_element_type=F32)
            sent[k * rows : (k + 1) * rows, at] = product[:rows].astype(BF16)
            kept[k, :, at] = product[rows:]


def project(rows, place, four, gain, weight, estimate):
    width = four[0].shape[1]
    return pl.pallas_call(
        project_kernel,
        in_specs=[smem_spec()] + [vmem_spec()] * 6,
        out_shape=[
            jax.ShapeDtypeStruct((3 * rows + STAT_ROWS, width), BF16),
            jax.ShapeDtypeStruct((3, rows, width), F32),
            jax.ShapeDtypeStruct((rows, 1), F32),
        ],
        scratch_shapes=[pltpu.VMEM((2 * rows, 2 * width), BF16)],
        compiler_params=pltpu.CompilerParams(vmem_limit_bytes=VMEM_BYTES),
        cost_estimate=cost(estimate),
        name="project",
    )(place, *four, gain, weight)


def attend_kernel(
    chunk, last, place, flag, kept, received, kept_mean, crossed, block, own, *refs
):
    earlier = refs[:chunk]
    earlier_outs = refs[chunk : 2 * chunk] if last else ()
    out, pairs = refs[-2:]
    rows, width = own.shape
    out_start = rows * len(earlier_outs)
    for i, ref in enumerate(earlier_outs):
        out[i * rows : (i + 1) * rows] = ref[...]
    stat = received[3 * rows :, :rows].astype(F32)
    row = stat[0:1] + stat[1:2] + stat[2:3]
    mean_peer = jnp.transpose(jnp.broadcast_to(row, (HD, rows)))[:, :1]
    mean_kept = kept_mean[...]
    inverse = lax.rsqrt((mean_kept + mean_peer) * 0.5 + EPS)
    scale_kept = inverse * jnp.sqrt(mean_kept + EPS)
    scale_peer = inverse * jnp.sqrt(mean_peer + EPS)
    causal = lax.broadcasted_iota(jnp.int32, (rows, rows), 0) >= lax.broadcasted_iota(
        jnp.int32, (rows, rows), 1
    )
    for head in range(width // HD):
        at = slice(head * HD, (head + 1) * HD)
        queries, keys, values = (
            (
                kept[k, :, at] * scale_kept
                + received[k * rows : (k + 1) * rows, at].astype(F32) * scale_peer
            ).astype(BF16)
            for k in range(3)
        )
        pairs[0, :, at] = keys
        pairs[1, :, at] = values
        held = [(ref[0, :, at], ref[1, :, at]) for ref in earlier] + [(keys, values)]
        scores = [
            lax.dot_general(queries, key, (((1,), (1,)), ((), ())), preferred_element_type=F32)
            * (1.0 / math.sqrt(HD))
            for key, _ in held
        ]
        scores[-1] = jnp.where(causal, scores[-1], F32(-1e30))
        top = functools.reduce(
            jnp.maximum, [jnp.max(score, axis=-1, keepdims=True) for score in scores]
        )
        raised = [jnp.exp(score - top) for score in scores]
        total = sum(jnp.sum(item, axis=-1, keepdims=True) for item in raised)
        over = 1.0 / total
        mixture = sum(
            jnp.dot((item * over).astype(BF16), value, preferred_element_type=F32)
            for item, (_, value) in zip(raised, held)
        )
        residual = block[:, at].astype(F32)
        if last:
            residual = jnp.where(place[2] == 1, crossed[:, at].astype(F32), residual)
        result = residual + mixture
        if last:
            result = jnp.where(flag[0] == 1, result, own[:, at].astype(F32))
        out[out_start : out_start + rows, at] = result.astype(BF16)


def attend(last, place, flag, sums, crossed, block, own, earlier, outs, after):
    rows, width = own.shape
    chunk = len(earlier)
    return pl.pallas_call(
        functools.partial(attend_kernel, chunk, last),
        in_specs=[smem_spec()] * 2
        + [vmem_spec()] * (6 + chunk + len(outs))
        + [any_spec() for _ in after],
        out_shape=[
            jax.ShapeDtypeStruct(((len(outs) + 1) * rows, width), BF16),
            jax.ShapeDtypeStruct((2, rows, width), BF16),
        ],
        compiler_params=pltpu.CompilerParams(vmem_limit_bytes=VMEM_BYTES),
        cost_estimate=cost(250),
        name="attend",
    )(place, flag, *sums, crossed, block, own, *earlier, *outs, *after)


def solution(mesh):
    sections = mesh.shape["section"]

    def local(inputs, qkv_weight, norm_gain, preempted):
        d = lax.axis_index("dp")
        t = lax.axis_index("tensor")
        y, c = t // 2, t % 2
        place = jnp.stack([c, d, (d == y).astype(c.dtype)]).astype(jnp.int32)
        place, diagonal, weight = lax.optimization_barrier((place, d == y, qkv_weight))
        weight = stage(place, weight)

        def spread(crossed, ringed):
            return (
                crossed,
                ringed,
                permute(crossed, sections, sibling),
                permute(ringed, sections, sibling),
            )

        def partial(four, estimate):
            sent, kept, kept_mean = project(rows, place, four, norm_gain, weight, estimate)
            return kept, permute(sent, sections, peer), kept_mean

        block = inputs[0, 0]
        rows = block.shape[0] // PARTS
        parts = [block[i * rows : (i + 1) * rows] for i in range(PARTS)]
        pair = permute(parts[0], sections, cross), permute(parts[0], sections, ring)
        relayed = permute(parts[1], sections, across_y)
        ringed = permute(parts[1], sections, ring)
        *pair, weight = lax.optimization_barrier((*pair, weight))
        weight = pltpu.with_memory_space_constraint(weight, pltpu.VMEM)
        sums = [partial(spread(*pair), 3)]
        crossed = jnp.where(diagonal, parts[1], permute(relayed, sections, across_x))
        crossed, ringed, _ = lax.optimization_barrier((crossed, ringed, sums[0][2]))
        sums.append(partial(spread(crossed, ringed), 3))
        owns, held, moved = [], [], []
        after = [sums[1][2]]
        seconds = []
        for part, item in zip(parts, sums):
            own, pairs = attend(False, place, preempted, item, part, part, part, held, [], after)
            held.append(pairs)
            owns.append(own)
            pair = permute(own, sections, onward(cross)), permute(own, sections, onward(ring))
            moved.append((pair[0], permute(own, sections, onward(direct))))
            if seconds:
                pair = lax.optimization_barrier((*pair, seconds[0][2]))[:2]
            seconds.append(partial(spread(*pair), 0.001))
            after = [seconds[0][2]]
        sums, after = seconds, seconds[1][2]
        outs, held = [], []
        for own, (crossed, before), item in zip(owns, moved, sums):
            out, pairs = attend(
                True, place, preempted, item, crossed, before, own, held, outs, [after]
            )
            held.append(pairs)
            outs.append(out)
        return outs[-1][None, None]

    placed = (
        P("section", "dp", None, "tensor"),
        P("section", None, "dp", "tensor"),
        P("section", None),
        P("section"),
    )
    return jax.shard_map(
        local,
        mesh=mesh,
        in_specs=placed,
        out_specs=P("section", "dp", None, "tensor"),
        check_vma=False,
    )
```

```python
import functools
import math

import jax
import jax.numpy as jnp
from jax import lax
from jax.experimental import pallas as pl
from jax.experimental.pallas import tpu as pltpu
from jax.sharding import PartitionSpec as P

HD = 128
EPS = 1e-05
AXES = ("section", "dp", "tensor")
F32 = jnp.float32
BF16 = jnp.bfloat16
PARTS = 2
VMEM_BYTES = 16 * 1024 * 1024
STAT_ROWS = 16


def permute(array, sections, hop):
    pairs = []
    for s in range(sections):
        for d in range(2):
            for y in range(2):
                for c in range(2):
                    to = hop(s, d, y, c)
                    if to is None or not 0 <= to[0] < sections:
                        continue
                    ts, td, ty, tc = to
                    pairs.append((s * 8 + d * 4 + y * 2 + c, ts * 8 + td * 4 + ty * 2 + tc))
    return lax.ppermute(array, AXES, pairs)


def ring(s, d, y, c):
    return (s, 1 - d, y, c) if d != y else (s, d, 1 - y, c)


def cross(s, d, y, c):
    return (s, 1 - d, 1 - y, c) if d != y else (s, d, y, c)


def direct(s, d, y, c):
    return (s, d, y, c) if d != y else None


def across_y(s, d, y, c):
    return (s, d, 1 - y, c) if d != y else None


def across_x(s, d, y, c):
    return (s, 1 - d, y, c) if d == y else None


def sibling(s, d, y, c):
    return (s, d, y, 1 - c)


def peer(s, d, y, c):
    return (s, 1 - d, y, c)


def onward(hop):
    def moved(s, d, y, c):
        to = hop(s, d, y, c)
        return None if to is None else (to[0] + 1, *to[1:])

    return moved


def cost(microseconds):
    return pl.CostEstimate(flops=int(microseconds * 1.15e9), bytes_accessed=1000, transcendentals=0)


def any_spec():
    return pl.BlockSpec(memory_space=pl.ANY)


def vmem_spec():
    return pl.BlockSpec(memory_space=pltpu.VMEM)


def smem_spec():
    return pl.BlockSpec(memory_space=pltpu.SMEM)


def stage_kernel(place, weight, staged, semaphore):
    copy = pltpu.make_async_copy(weight, staged, semaphore)
    copy.start()
    copy.wait()


def stage(place, weight):
    return pl.pallas_call(
        stage_kernel,
        in_specs=[smem_spec(), any_spec()],
        out_specs=vmem_spec(),
        out_shape=pltpu.VMEM(weight.shape, weight.dtype),
        scratch_shapes=[pltpu.SemaphoreType.DMA(())],
        compiler_params=pltpu.CompilerParams(vmem_limit_bytes=VMEM_BYTES),
        cost_estimate=cost(4),
        name="stage",
    )(place, weight)


def project_kernel(place, crossed, ringed, sib_crossed, sib_ringed, gain, weight, *refs):
    sent, kept, kept_mean, normed = refs
    rows = normed.shape[0] // 2
    width = crossed.shape[1]
    half = 2 * width
    core, dp, diagonal = place[0], place[1], place[2]
    means = []
    for mine, theirs, offset in (
        (crossed, sib_crossed, diagonal),
        (ringed, sib_ringed, 1 - diagonal),
    ):
        at = pl.ds(pl.multiple_of(offset * rows, rows), rows)
        pieces = [ref[...].astype(F32) for ref in (mine, theirs)]
        squares = sum(jnp.sum(piece * piece, axis=-1, keepdims=True) for piece in pieces)
        mean = squares * (1.0 / half)
        means.append(mean)
        inverse = lax.rsqrt(mean + EPS)
        for piece, order in zip(pieces, (core, 1 - core)):
            gains = gain[:, pl.ds(pl.multiple_of(dp * half + order * width, HD), width)]
            normed[at, pl.ds(pl.multiple_of(order * width, HD), width)] = (
                piece * inverse * gains.astype(F32)
            ).astype(BF16)
    on_diagonal = diagonal == 1
    sent_mean = jnp.where(on_diagonal, means[1], means[0])
    kept_mean[...] = jnp.where(on_diagonal, means[0], means[1])
    row = jnp.transpose(jnp.broadcast_to(sent_mean, (rows, HD)))[:STAT_ROWS]
    high = row.astype(BF16).astype(F32)
    mid = (row - high).astype(BF16).astype(F32)
    low = row - high - mid
    which = lax.broadcasted_iota(jnp.int32, row.shape, 0)
    stat = jnp.where(which == 0, high, jnp.where(which == 1, mid, low))
    for begin in range(0, width, rows):
        sent[3 * rows :, begin : begin + rows] = stat.astype(BF16)
    for k in range(3):
        product = jnp.dot(normed[...], weight[0, k], preferred_element_type=F32)
        sent[k * rows : (k + 1) * rows] = product[:rows].astype(BF16)
        kept[k] = product[rows:]


def project(rows, place, four, gain, weight, estimate):
    width = four[0].shape[1]
    return pl.pallas_call(
        project_kernel,
        in_specs=[smem_spec()] + [vmem_spec()] * 6,
        out_shape=[
            pltpu.VMEM((3 * rows + STAT_ROWS, width), BF16),
            pltpu.VMEM((3, rows, width), F32),
            pltpu.VMEM((rows, 1), F32),
        ],
        scratch_shapes=[pltpu.VMEM((2 * rows, 2 * width), BF16)],
        compiler_params=pltpu.CompilerParams(vmem_limit_bytes=VMEM_BYTES),
        cost_estimate=cost(estimate),
        name="project",
    )(place, *four, gain, weight)


def mix(kept, received, kept_mean, earlier, pairs, put):
    rows, width = kept.shape[1:]
    stat = received[3 * rows :, :rows].astype(F32)
    row = stat[0:1] + stat[1:2] + stat[2:3]
    mean_peer = jnp.transpose(jnp.broadcast_to(row, (HD, rows)))[:, :1]
    mean_kept = kept_mean[...]
    inverse = lax.rsqrt((mean_kept + mean_peer) * 0.5 + EPS)
    scale_kept = inverse * jnp.sqrt(mean_kept + EPS)
    scale_peer = inverse * jnp.sqrt(mean_peer + EPS)
    causal = lax.broadcasted_iota(jnp.int32, (rows, rows), 0) >= lax.broadcasted_iota(
        jnp.int32, (rows, rows), 1
    )
    heads = [slice(begin, begin + HD) for begin in range(0, width, HD)]
    held, scores = [], []
    for at in heads:
        queries, keys, values = (
            (
                kept[k, :, at] * scale_kept
                + received[k * rows : (k + 1) * rows, at].astype(F32) * scale_peer
            ).astype(BF16)
            for k in range(3)
        )
        pairs[0, :, at] = keys
        pairs[1, :, at] = values
        held.append([(ref[0, :, at], ref[1, :, at]) for ref in earlier] + [(keys, values)])
        scores.append(
            [
                lax.dot_general(queries, key, (((1,), (1,)), ((), ())), preferred_element_type=F32)
                * (1.0 / math.sqrt(HD))
                for key, _ in held[-1]
            ]
        )
        scores[-1][-1] = jnp.where(causal, scores[-1][-1], F32(-1e30))
    tops = [
        functools.reduce(jnp.maximum, [jnp.max(item, axis=-1, keepdims=True) for item in score])
        for score in scores
    ]
    raised = [[jnp.exp(item - top) for item in score] for score, top in zip(scores, tops)]
    overs = [1.0 / sum(jnp.sum(item, axis=-1, keepdims=True) for item in items) for items in raised]
    for at, items, over, pair in zip(heads, raised, overs, held):
        mixture = sum(
            jnp.dot((item * over).astype(BF16), value, preferred_element_type=F32)
            for item, (_, value) in zip(items, pair)
        )
        put(at, mixture)


def attend_kernel(kept, received, kept_mean, block, *refs):
    earlier, (out, pairs) = refs[:-2], refs[-2:]

    def put(at, mixture):
        out[:, at] = (block[:, at].astype(F32) + mixture).astype(BF16)

    mix(kept, received, kept_mean, earlier, pairs, put)


def hold_kernel(kept, received, kept_mean, *refs):
    owns, (held, pairs, whole) = refs[:-3], refs[-3:]
    rows = kept.shape[1]

    def put(at, mixture):
        held[:, at] = mixture

    mix(kept, received, kept_mean, (), pairs, put)
    for i, own in enumerate(owns):
        whole[i * rows : (i + 1) * rows] = own[...]


def final_kernel(
    place, flag, kept, received, kept_mean, earlier, held, first, second, before, own, out, pairs
):
    rows = kept.shape[1]
    diagonal, shadow = place[2] == 1, flag[0] == 1

    def settle(start, crossed, at, mixture):
        here = slice(start, start + rows)
        residual = jnp.where(diagonal, crossed[:, at].astype(F32), before[here, at].astype(F32))
        result = jnp.where(shadow, residual + mixture, own[here, at].astype(F32))
        out[here, at] = result.astype(BF16)

    def put(at, mixture):
        settle(rows, second, at, mixture)

    settle(0, first, slice(None), held[...])
    mix(kept, received, kept_mean, (earlier,), pairs, put)


def call_attend(kernel, name, scalars, arrays, out_shape):
    return pl.pallas_call(
        kernel,
        in_specs=[smem_spec() for _ in scalars] + [vmem_spec() for _ in arrays],
        out_shape=out_shape,
        compiler_params=pltpu.CompilerParams(vmem_limit_bytes=VMEM_BYTES),
        cost_estimate=cost(250),
        name=name,
    )(*scalars, *arrays)


def solution(mesh):
    sections = mesh.shape["section"]

    def local(inputs, qkv_weight, norm_gain, preempted):
        d = lax.axis_index("dp")
        t = lax.axis_index("tensor")
        y, c = t // 2, t % 2
        place = jnp.stack([c, d, (d == y).astype(c.dtype)]).astype(jnp.int32)
        place, diagonal, weight = lax.optimization_barrier((place, d == y, qkv_weight))
        weight = stage(place, weight)

        def spread(crossed, ringed):
            return (
                crossed,
                ringed,
                permute(crossed, sections, sibling),
                permute(ringed, sections, sibling),
            )

        def partial(four, estimate):
            sent, kept, kept_mean = project(rows, place, four, norm_gain, weight, estimate)
            return kept, permute(sent, sections, peer), kept_mean

        block = inputs[0, 0]
        rows = block.shape[0] // PARTS
        parts = [block[i * rows : (i + 1) * rows] for i in range(PARTS)]
        pair = permute(parts[0], sections, cross), permute(parts[0], sections, ring)
        relayed = permute(parts[1], sections, across_y)
        ringed = permute(parts[1], sections, ring)
        *pair, weight = lax.optimization_barrier((*pair, weight))
        weight = pltpu.with_memory_space_constraint(weight, pltpu.VMEM)
        sums = [partial(spread(*pair), 3)]
        crossed = jnp.where(diagonal, parts[1], permute(relayed, sections, across_x))
        crossed, ringed, _ = lax.optimization_barrier((crossed, ringed, sums[0][2]))
        sums.append(partial(spread(crossed, ringed), 3))
        width = block.shape[1]
        rows_of = pltpu.VMEM((rows, width), BF16)
        pairs_of = pltpu.VMEM((2, rows, width), BF16)
        owns, held, moved, seconds = [], [], [], []
        for part, item in zip(parts, sums):
            if seconds:
                part = lax.optimization_barrier((part, seconds[0][2]))[0]
            own, pairs = call_attend(
                attend_kernel, "attend", [], [*item, part, *held], [rows_of, pairs_of]
            )
            held.append(pairs)
            owns.append(own)
            pair = permute(own, sections, onward(cross)), permute(own, sections, onward(ring))
            moved.append(pair[0])
            if seconds:
                pair = lax.optimization_barrier((*pair, seconds[0][2]))[:2]
            seconds.append(partial(spread(*pair), 0.001))
        mixture, pairs, own = call_attend(
            hold_kernel,
            "hold",
            [],
            [*seconds[0], *owns],
            [pltpu.VMEM((rows, width), F32), pairs_of, pltpu.VMEM(block.shape, BF16)],
        )
        before = permute(own, sections, onward(direct))
        out, _ = call_attend(
            final_kernel,
            "final",
            [place, preempted],
            [*seconds[1], pairs, mixture, *moved, before, own],
            [jax.ShapeDtypeStruct(block.shape, BF16), pairs_of],
        )
        return out[None, None]

    placed = (
        P("section", "dp", None, "tensor"),
        P("section", None, "dp", "tensor"),
        P("section", None),
        P("section"),
    )
    return jax.shard_map(
        local,
        mesh=mesh,
        in_specs=placed,
        out_specs=P("section", "dp", None, "tensor"),
        check_vma=False,
    )
```

```python
import functools
import math

import jax
import jax.numpy as jnp
from jax import lax
from jax.experimental import pallas as pl
from jax.experimental.pallas import tpu as pltpu
from jax.sharding import PartitionSpec as P

HD = 128
EPS = 1e-05
AXES = ("section", "dp", "tensor")
F32 = jnp.float32
BF16 = jnp.bfloat16
PARTS = 2
VMEM_BYTES = 16 * 1024 * 1024
STAT_ROWS = 16


def permute(array, sections, hop):
    pairs = []
    for s in range(sections):
        for d in range(2):
            for y in range(2):
                for c in range(2):
                    to = hop(s, d, y, c)
                    if to is None or not 0 <= to[0] < sections:
                        continue
                    ts, td, ty, tc = to
                    pairs.append((s * 8 + d * 4 + y * 2 + c, ts * 8 + td * 4 + ty * 2 + tc))
    return lax.ppermute(array, AXES, pairs)


def ring(s, d, y, c):
    return (s, 1 - d, y, c) if d != y else (s, d, 1 - y, c)


def cross(s, d, y, c):
    return (s, 1 - d, 1 - y, c) if d != y else (s, d, y, c)


def direct(s, d, y, c):
    return (s, d, y, c) if d != y else None


def forward(s, d, y, c):
    return (s, d, 1 - y, c) if d == y else None


def swap(s, d, y, c):
    return (s, d, 1 - y, c)


def sibling(s, d, y, c):
    return (s, d, y, 1 - c)


def peer(s, d, y, c):
    return (s, 1 - d, y, c)


def onward(hop):
    def moved(s, d, y, c):
        to = hop(s, d, y, c)
        return None if to is None else (to[0] + 1, *to[1:])

    return moved


def cost(microseconds):
    return pl.CostEstimate(flops=int(microseconds * 1.15e9), bytes_accessed=1000, transcendentals=0)


def any_spec():
    return pl.BlockSpec(memory_space=pl.ANY)


def vmem_spec():
    return pl.BlockSpec(memory_space=pltpu.VMEM)


def smem_spec():
    return pl.BlockSpec(memory_space=pltpu.SMEM)


def stage_kernel(place, weight, arrived, staged, semaphore):
    copy = pltpu.make_async_copy(weight, staged, semaphore)
    copy.start()
    copy.wait()


def stage(place, weight, arrived):
    return pl.pallas_call(
        stage_kernel,
        in_specs=[smem_spec(), any_spec(), any_spec()],
        out_specs=vmem_spec(),
        out_shape=pltpu.VMEM(weight.shape, weight.dtype),
        scratch_shapes=[pltpu.SemaphoreType.DMA(())],
        compiler_params=pltpu.CompilerParams(vmem_limit_bytes=VMEM_BYTES),
        cost_estimate=cost(250),
        name="stage",
    )(place, pltpu.with_memory_space_constraint(weight, pltpu.HBM), arrived)


def project_kernel(
    place, crossed, ringed, sib_crossed, sib_ringed, gain, weight, sent, kept, kept_mean, *scratch
):
    normed, out, semaphores = scratch
    rows, width = crossed.shape
    half = 2 * width
    first_core, diagonal = place[0] == 0, place[2] == 1
    gains = gain[:, pl.ds(pl.multiple_of(place[1] * half, HD), half)].astype(F32)
    means = []
    for i, (mine, theirs) in enumerate(((crossed, sib_crossed), (ringed, sib_ringed))):
        mine, theirs = mine[...].astype(F32), theirs[...].astype(F32)
        pieces = jnp.where(first_core, mine, theirs), jnp.where(first_core, theirs, mine)
        squares = sum(jnp.sum(piece * piece, axis=-1, keepdims=True) for piece in pieces)
        mean = squares * (1.0 / half)
        means.append(mean)
        inverse = lax.rsqrt(mean + EPS)
        for j, piece in enumerate(pieces):
            at = slice(j * width, (j + 1) * width)
            normed[i * rows : (i + 1) * rows, at] = (piece * inverse * gains[:, at]).astype(BF16)
    sent_mean = jnp.where(diagonal, means[1], means[0])
    kept_mean[...] = jnp.where(diagonal, means[0], means[1])
    row = jnp.transpose(jnp.broadcast_to(sent_mean, (rows, HD)))[:STAT_ROWS]
    high = row.astype(BF16).astype(F32)
    mid = (row - high).astype(BF16).astype(F32)
    low = row - high - mid
    which = lax.broadcasted_iota(jnp.int32, row.shape, 0)
    stat = jnp.where(which == 0, high, jnp.where(which == 1, mid, low)).astype(BF16)
    for begin in range(0, width, rows):
        out[:STAT_ROWS, begin : begin + rows] = stat
    copies = []
    for k in range(3):
        product = jnp.dot(normed[...], weight[0, k], preferred_element_type=F32)
        crossed_sums, ringed_sums = product[:rows], product[rows:]
        begin = STAT_ROWS + k * rows
        out[begin : begin + rows] = jnp.where(diagonal, ringed_sums, crossed_sums).astype(BF16)
        kept[k] = jnp.where(diagonal, crossed_sums, ringed_sums)
        at = pl.ds(begin, rows) if k else pl.ds(0, begin + rows)
        copies.append(pltpu.make_async_copy(out.at[at], sent.at[at], semaphores.at[k]))
        copies[-1].start()
    for copy in copies:
        copy.wait()


def project(rows, place, four, gain, weight, estimate):
    width = four[0].shape[1]
    sent_shape = (3 * rows + STAT_ROWS, width)
    return pl.pallas_call(
        project_kernel,
        in_specs=[smem_spec()] + [vmem_spec()] * 6,
        out_specs=[any_spec(), vmem_spec(), vmem_spec()],
        out_shape=[
            jax.ShapeDtypeStruct(sent_shape, BF16),
            pltpu.VMEM((3, rows, width), F32),
            pltpu.VMEM((rows, 1), F32),
        ],
        scratch_shapes=[
            pltpu.VMEM((2 * rows, 2 * width), BF16),
            pltpu.VMEM(sent_shape, BF16),
            pltpu.SemaphoreType.DMA((3,)),
        ],
        compiler_params=pltpu.CompilerParams(vmem_limit_bytes=VMEM_BYTES),
        cost_estimate=cost(estimate),
        name="project",
    )(place, *four, gain, weight)


def mix(kept, received, kept_mean, earlier, pairs, put):
    rows, width = kept.shape[1:]
    stat = received[:STAT_ROWS, :rows].astype(F32)
    row = stat[0:1] + stat[1:2] + stat[2:3]
    mean_peer = jnp.transpose(jnp.broadcast_to(row, (HD, rows)))[:, :1]
    mean_kept = kept_mean[...]
    inverse = lax.rsqrt((mean_kept + mean_peer) * 0.5 + EPS)
    scale_kept = inverse * jnp.sqrt(mean_kept + EPS)
    scale_peer = inverse * jnp.sqrt(mean_peer + EPS)
    causal = lax.broadcasted_iota(jnp.int32, (rows, rows), 0) >= lax.broadcasted_iota(
        jnp.int32, (rows, rows), 1
    )
    heads = [slice(begin, begin + HD) for begin in range(0, width, HD)]
    held, scores = [], []
    for at in heads:
        queries, keys, values = (
            (
                kept[k, :, at] * scale_kept
                + received[STAT_ROWS + k * rows : STAT_ROWS + (k + 1) * rows, at].astype(F32)
                * scale_peer
            ).astype(BF16)
            for k in range(3)
        )
        pairs[0, :, at] = keys
        pairs[1, :, at] = values
        held.append([(ref[0, :, at], ref[1, :, at]) for ref in earlier] + [(keys, values)])
        scores.append(
            [
                lax.dot_general(queries, key, (((1,), (1,)), ((), ())), preferred_element_type=F32)
                * (1.0 / math.sqrt(HD))
                for key, _ in held[-1]
            ]
        )
        scores[-1][-1] = jnp.where(causal, scores[-1][-1], F32(-1e30))
    tops = [
        functools.reduce(jnp.maximum, [jnp.max(item, axis=-1, keepdims=True) for item in score])
        for score in scores
    ]
    raised = [[jnp.exp(item - top) for item in score] for score, top in zip(scores, tops)]
    overs = [1.0 / sum(jnp.sum(item, axis=-1, keepdims=True) for item in items) for items in raised]
    for at, items, over, pair in zip(heads, raised, overs, held):
        mixture = sum(
            jnp.dot((item * over).astype(BF16), value, preferred_element_type=F32)
            for item, (_, value) in zip(items, pair)
        )
        put(at, mixture)


def attend_kernel(kept, received, kept_mean, block, *refs):
    earlier, (out, pairs) = refs[:-2], refs[-2:]

    def put(at, mixture):
        out[:, at] = (block[:, at].astype(F32) + mixture).astype(BF16)

    mix(kept, received, kept_mean, earlier, pairs, put)


def hold_kernel(kept, received, kept_mean, *refs):
    owns, (held, pairs, whole) = refs[:-3], refs[-3:]
    rows = kept.shape[1]

    def put(at, mixture):
        held[:, at] = mixture

    mix(kept, received, kept_mean, (), pairs, put)
    for i, own in enumerate(owns):
        whole[i * rows : (i + 1) * rows] = own[...]


def final_kernel(
    place, flag, kept, received, kept_mean, earlier, held, first, second, before, own, out, pairs
):
    rows = kept.shape[1]
    diagonal, shadow = place[2] == 1, flag[0] == 1

    def settle(start, crossed, at, mixture):
        here = slice(start, start + rows)
        residual = jnp.where(diagonal, crossed[:, at].astype(F32), before[here, at].astype(F32))
        result = jnp.where(shadow, residual + mixture, own[here, at].astype(F32))
        out[here, at] = result.astype(BF16)

    def put(at, mixture):
        settle(rows, second, at, mixture)

    settle(0, first, slice(None), held[...])
    mix(kept, received, kept_mean, (earlier,), pairs, put)


def call_attend(kernel, name, scalars, arrays, out_shape):
    return pl.pallas_call(
        kernel,
        in_specs=[smem_spec() for _ in scalars] + [vmem_spec() for _ in arrays],
        out_shape=out_shape,
        compiler_params=pltpu.CompilerParams(vmem_limit_bytes=VMEM_BYTES),
        cost_estimate=cost(250),
        name=name,
    )(*scalars, *arrays)


def solution(mesh):
    sections = mesh.shape["section"]

    def local(inputs, qkv_weight, norm_gain, preempted):
        d = lax.axis_index("dp")
        t = lax.axis_index("tensor")
        y, c = t // 2, t % 2
        place = jnp.stack([c, d, (d == y).astype(c.dtype)]).astype(jnp.int32)
        place, diagonal = lax.optimization_barrier((place, d == y))

        def spread(crossed, ringed):
            return (
                crossed,
                ringed,
                permute(crossed, sections, sibling),
                permute(ringed, sections, sibling),
            )

        def partial(four, estimate):
            sent, kept, kept_mean = project(rows, place, four, norm_gain, weight, estimate)
            return kept, permute(sent, sections, peer), kept_mean

        block = inputs[0, 0]
        rows = block.shape[0] // PARTS
        parts = [block[i * rows : (i + 1) * rows] for i in range(PARTS)]
        ringed = [permute(part, sections, ring) for part in parts]
        weight = stage(place, qkv_weight, ringed[0])
        forwarded = permute(ringed[0], sections, forward)
        crossed = jnp.where(diagonal, parts[0], forwarded)
        crossed, weight = lax.optimization_barrier((crossed, weight))
        weight = pltpu.with_memory_space_constraint(weight, pltpu.VMEM)
        sums = [partial(spread(crossed, ringed[0]), 3)]
        late, _ = lax.optimization_barrier((ringed[1], weight))
        forwarded = permute(late, sections, forward)
        forwarded, late, part, _ = lax.optimization_barrier(
            (forwarded, late, parts[1], sums[0][2])
        )
        sums.append(partial(spread(jnp.where(diagonal, part, forwarded), late), 1))
        width = block.shape[1]
        rows_of = pltpu.VMEM((rows, width), BF16)
        pairs_of = pltpu.VMEM((2, rows, width), BF16)
        owns, held, moved, seconds = [], [], [], []
        for part, item in zip(parts, sums):
            if seconds:
                part = lax.optimization_barrier((part, seconds[0][2]))[0]
            own, pairs = call_attend(
                attend_kernel, "attend", [], [*item, part, *held], [rows_of, pairs_of]
            )
            held.append(pairs)
            owns.append(own)
            moved.append(permute(own, sections, onward(cross)))
            if seconds:
                crossed = lax.optimization_barrier((moved[-1], seconds[0][2]))[0]
                pair = crossed, permute(crossed, sections, swap)
            else:
                pair = moved[-1], permute(own, sections, onward(ring))
            seconds.append(partial(spread(*pair), 0.001))
        mixture, pairs, own = call_attend(
            hold_kernel,
            "hold",
            [],
            [*seconds[0], *owns],
            [pltpu.VMEM((rows, width), F32), pairs_of, pltpu.VMEM(block.shape, BF16)],
        )
        before = permute(own, sections, onward(direct))
        out, _ = call_attend(
            final_kernel,
            "final",
            [place, preempted],
            [*seconds[1], pairs, mixture, *moved, before, own],
            [jax.ShapeDtypeStruct(block.shape, BF16), pairs_of],
        )
        return out[None, None]

    placed = (
        P("section", "dp", None, "tensor"),
        P("section", None, "dp", "tensor"),
        P("section", None),
        P("section"),
    )
    return jax.shard_map(
        local,
        mesh=mesh,
        in_specs=placed,
        out_specs=P("section", "dp", None, "tensor"),
        check_vma=False,
    )
```

```python
import functools
import math

import jax
import jax.numpy as jnp
from jax import lax
from jax.experimental import pallas as pl
from jax.experimental.pallas import tpu as pltpu
from jax.sharding import PartitionSpec as P

HD = 128
EPS = 1e-05
AXES = ("section", "dp", "tensor")
F32 = jnp.float32
BF16 = jnp.bfloat16
PARTS = 2
VMEM_BYTES = 16 * 1024 * 1024
STAT_ROWS = 16


def permute(array, sections, hop):
    pairs = []
    for s in range(sections):
        for d in range(2):
            for y in range(2):
                for c in range(2):
                    to = hop(s, d, y, c)
                    if to is None or not 0 <= to[0] < sections:
                        continue
                    ts, td, ty, tc = to
                    pairs.append((s * 8 + d * 4 + y * 2 + c, ts * 8 + td * 4 + ty * 2 + tc))
    return lax.ppermute(array, AXES, pairs)


def ring(s, d, y, c):
    return (s, 1 - d, y, c) if d != y else (s, d, 1 - y, c)


def cross(s, d, y, c):
    return (s, 1 - d, 1 - y, c) if d != y else (s, d, y, c)


def direct(s, d, y, c):
    return (s, d, y, c) if d != y else None


def across_y(s, d, y, c):
    return (s, d, 1 - y, c) if d != y else None


def across_x(s, d, y, c):
    return (s, 1 - d, y, c) if d == y else None


def swap(s, d, y, c):
    return (s, d, 1 - y, c)


def sibling(s, d, y, c):
    return (s, d, y, 1 - c)


def peer(s, d, y, c):
    return (s, 1 - d, y, c)


def onward(hop):
    def moved(s, d, y, c):
        to = hop(s, d, y, c)
        return None if to is None else (to[0] + 1, *to[1:])

    return moved


def cost(microseconds):
    return pl.CostEstimate(flops=int(microseconds * 1.15e9), bytes_accessed=1000, transcendentals=0)


def any_spec():
    return pl.BlockSpec(memory_space=pl.ANY)


def vmem_spec():
    return pl.BlockSpec(memory_space=pltpu.VMEM)


def smem_spec():
    return pl.BlockSpec(memory_space=pltpu.SMEM)


def stage_kernel(place, weight, staged, semaphore):
    copy = pltpu.make_async_copy(weight, staged, semaphore)
    copy.start()
    copy.wait()


def stage(place, weight):
    return pl.pallas_call(
        stage_kernel,
        in_specs=[smem_spec(), any_spec()],
        out_specs=vmem_spec(),
        out_shape=pltpu.VMEM(weight.shape, weight.dtype),
        scratch_shapes=[pltpu.SemaphoreType.DMA(())],
        compiler_params=pltpu.CompilerParams(vmem_limit_bytes=VMEM_BYTES),
        cost_estimate=cost(4),
        name="stage",
    )(place, pltpu.with_memory_space_constraint(weight, pltpu.HBM))


def project_kernel(place, crossed, ringed, sib_crossed, sib_ringed, gain, weight, *refs):
    sent, kept, kept_mean, normed, out, semaphores = refs
    rows = normed.shape[0] // 2
    width = crossed.shape[1]
    half = 2 * width
    core, dp, diagonal = place[0], place[1], place[2]
    means = []
    for mine, theirs, offset in (
        (crossed, sib_crossed, diagonal),
        (ringed, sib_ringed, 1 - diagonal),
    ):
        at = pl.ds(pl.multiple_of(offset * rows, rows), rows)
        pieces = [ref[...].astype(F32) for ref in (mine, theirs)]
        squares = sum(jnp.sum(piece * piece, axis=-1, keepdims=True) for piece in pieces)
        mean = squares * (1.0 / half)
        means.append(mean)
        inverse = lax.rsqrt(mean + EPS)
        for piece, order in zip(pieces, (core, 1 - core)):
            gains = gain[:, pl.ds(pl.multiple_of(dp * half + order * width, HD), width)]
            normed[at, pl.ds(pl.multiple_of(order * width, HD), width)] = (
                piece * inverse * gains.astype(F32)
            ).astype(BF16)
    on_diagonal = diagonal == 1
    sent_mean = jnp.where(on_diagonal, means[1], means[0])
    kept_mean[...] = jnp.where(on_diagonal, means[0], means[1])
    row = jnp.transpose(jnp.broadcast_to(sent_mean, (rows, HD)))[:STAT_ROWS]
    high = row.astype(BF16).astype(F32)
    mid = (row - high).astype(BF16).astype(F32)
    low = row - high - mid
    which = lax.broadcasted_iota(jnp.int32, row.shape, 0)
    stat = jnp.where(which == 0, high, jnp.where(which == 1, mid, low)).astype(BF16)
    for begin in range(0, width, rows):
        out[:STAT_ROWS, begin : begin + rows] = stat
    split = width // (2 * HD) * HD + HD
    copies = []
    for i, (k, begin, end) in enumerate(
        ((0, 0, width), (1, 0, width), (2, 0, split), (2, split, width))
    ):
        columns = slice(begin, end)
        product = jnp.dot(normed[...], weight[0, k, :, columns], preferred_element_type=F32)
        top = STAT_ROWS + k * rows
        out[top : top + rows, columns] = product[:rows].astype(BF16)
        kept[k, :, columns] = product[rows:]
        at = (slice(top if k else 0, top + rows), columns)
        copies.append(pltpu.make_async_copy(out.at[at], sent.at[at], semaphores.at[i]))
        copies[-1].start()
    for copy in copies:
        copy.wait()


def project(rows, place, four, gain, weight, estimate):
    width = four[0].shape[1]
    sent_shape = (3 * rows + STAT_ROWS, width)
    return pl.pallas_call(
        project_kernel,
        in_specs=[smem_spec()] + [vmem_spec()] * 6,
        out_specs=[any_spec(), vmem_spec(), vmem_spec()],
        out_shape=[
            jax.ShapeDtypeStruct(sent_shape, BF16),
            pltpu.VMEM((3, rows, width), F32),
            pltpu.VMEM((rows, 1), F32),
        ],
        scratch_shapes=[
            pltpu.VMEM((2 * rows, 2 * width), BF16),
            pltpu.VMEM(sent_shape, BF16),
            pltpu.SemaphoreType.DMA((4,)),
        ],
        compiler_params=pltpu.CompilerParams(vmem_limit_bytes=VMEM_BYTES),
        cost_estimate=cost(estimate),
        name="project",
    )(place, *four, gain, weight)


def mix(kept, received, kept_mean, earlier, pairs, put):
    rows, width = kept.shape[1:]
    stat = received[:STAT_ROWS, :rows].astype(F32)
    row = stat[0:1] + stat[1:2] + stat[2:3]
    mean_peer = jnp.transpose(jnp.broadcast_to(row, (HD, rows)))[:, :1]
    mean_kept = kept_mean[...]
    inverse = lax.rsqrt((mean_kept + mean_peer) * 0.5 + EPS)
    scale_kept = inverse * jnp.sqrt(mean_kept + EPS)
    scale_peer = inverse * jnp.sqrt(mean_peer + EPS)
    causal = lax.broadcasted_iota(jnp.int32, (rows, rows), 0) >= lax.broadcasted_iota(
        jnp.int32, (rows, rows), 1
    )
    heads = [slice(begin, begin + HD) for begin in range(0, width, HD)]
    held, scores = [], []
    for at in heads:
        queries, keys, values = (
            (
                kept[k, :, at] * scale_kept
                + received[STAT_ROWS + k * rows : STAT_ROWS + (k + 1) * rows, at].astype(F32)
                * scale_peer
            ).astype(BF16)
            for k in range(3)
        )
        pairs[0, :, at] = keys
        pairs[1, :, at] = values
        held.append([(ref[0, :, at], ref[1, :, at]) for ref in earlier] + [(keys, values)])
        scores.append(
            [
                lax.dot_general(queries, key, (((1,), (1,)), ((), ())), preferred_element_type=F32)
                * (1.0 / math.sqrt(HD))
                for key, _ in held[-1]
            ]
        )
        scores[-1][-1] = jnp.where(causal, scores[-1][-1], F32(-1e30))
    tops = [
        functools.reduce(jnp.maximum, [jnp.max(item, axis=-1, keepdims=True) for item in score])
        for score in scores
    ]
    raised = [[jnp.exp(item - top) for item in score] for score, top in zip(scores, tops)]
    overs = [1.0 / sum(jnp.sum(item, axis=-1, keepdims=True) for item in items) for items in raised]
    for at, items, over, pair in zip(heads, raised, overs, held):
        mixture = sum(
            jnp.dot((item * over).astype(BF16), value, preferred_element_type=F32)
            for item, (_, value) in zip(items, pair)
        )
        put(at, mixture)


def attend_kernel(kept, received, kept_mean, block, *refs):
    earlier, (out, pairs) = refs[:-2], refs[-2:]

    def put(at, mixture):
        out[:, at] = (block[:, at].astype(F32) + mixture).astype(BF16)

    mix(kept, received, kept_mean, earlier, pairs, put)


def hold_kernel(kept, received, kept_mean, *refs):
    owns, (held, pairs, whole) = refs[:-3], refs[-3:]
    rows = kept.shape[1]

    def put(at, mixture):
        held[:, at] = mixture

    mix(kept, received, kept_mean, (), pairs, put)
    for i, own in enumerate(owns):
        whole[i * rows : (i + 1) * rows] = own[...]


def final_kernel(
    place, flag, kept, received, kept_mean, earlier, held, first, second, before, own, out, pairs
):
    rows = kept.shape[1]
    diagonal, shadow = place[2] == 1, flag[0] == 1

    def settle(start, crossed, at, mixture):
        here = slice(start, start + rows)
        residual = jnp.where(diagonal, crossed[:, at].astype(F32), before[here, at].astype(F32))
        result = jnp.where(shadow, residual + mixture, own[here, at].astype(F32))
        out[here, at] = result.astype(BF16)

    def put(at, mixture):
        settle(rows, second, at, mixture)

    settle(0, first, slice(None), held[...])
    mix(kept, received, kept_mean, (earlier,), pairs, put)


def call_attend(kernel, name, scalars, arrays, out_shape):
    return pl.pallas_call(
        kernel,
        in_specs=[smem_spec() for _ in scalars] + [vmem_spec() for _ in arrays],
        out_shape=out_shape,
        compiler_params=pltpu.CompilerParams(vmem_limit_bytes=VMEM_BYTES),
        cost_estimate=cost(250),
        name=name,
    )(*scalars, *arrays)


def solution(mesh):
    sections = mesh.shape["section"]

    def local(inputs, qkv_weight, norm_gain, preempted):
        d = lax.axis_index("dp")
        t = lax.axis_index("tensor")
        y, c = t // 2, t % 2
        place = jnp.stack([c, d, (d == y).astype(c.dtype)]).astype(jnp.int32)
        place, diagonal, weight = lax.optimization_barrier((place, d == y, qkv_weight))
        weight = stage(place, weight)

        def spread(crossed, ringed):
            return (
                crossed,
                ringed,
                permute(crossed, sections, sibling),
                permute(ringed, sections, sibling),
            )

        def partial(four, estimate):
            sent, kept, kept_mean = project(rows, place, four, norm_gain, weight, estimate)
            return kept, permute(sent, sections, peer), kept_mean

        block = inputs[0, 0]
        rows = block.shape[0] // PARTS
        parts = [block[i * rows : (i + 1) * rows] for i in range(PARTS)]
        pair = permute(parts[0], sections, cross), permute(parts[0], sections, ring)
        relayed = permute(parts[1], sections, across_y)
        ringed = permute(parts[1], sections, ring)
        *pair, weight = lax.optimization_barrier((*pair, weight))
        weight = pltpu.with_memory_space_constraint(weight, pltpu.VMEM)
        sums = [partial(spread(*pair), 3)]
        crossed = jnp.where(diagonal, parts[1], permute(relayed, sections, across_x))
        crossed, ringed, _ = lax.optimization_barrier((crossed, ringed, sums[0][2]))
        sums.append(partial(spread(crossed, ringed), 3))
        width = block.shape[1]
        rows_of = pltpu.VMEM((rows, width), BF16)
        pairs_of = pltpu.VMEM((2, rows, width), BF16)

        def attend(part, item, held):
            return call_attend(
                attend_kernel, "attend", [], [*item, part, *held], [rows_of, pairs_of]
            )

        def carry(own):
            return permute(own, sections, onward(cross))

        first, pairs = attend(parts[0], sums[0], [])
        moved = [carry(first)]
        four = spread(moved[0], permute(moved[0], sections, swap))
        part = lax.optimization_barrier((parts[1], *four))[0]
        second, _ = attend(part, sums[1], [pairs])
        owns = [first, second]
        moved.append(carry(second))
        *four, _ = lax.optimization_barrier((*four, second))
        seconds = [partial(four, 3)]
        crossed, _ = lax.optimization_barrier((moved[1], seconds[0][2]))
        seconds.append(partial(spread(crossed, permute(crossed, sections, swap)), 1))
        mixture, pairs, own = call_attend(
            hold_kernel,
            "hold",
            [],
            [*seconds[0], *owns],
            [pltpu.VMEM((rows, width), F32), pairs_of, pltpu.VMEM(block.shape, BF16)],
        )
        before = permute(own, sections, onward(direct))
        out, _ = call_attend(
            final_kernel,
            "final",
            [place, preempted],
            [*seconds[1], pairs, mixture, *moved, before, own],
            [jax.ShapeDtypeStruct(block.shape, BF16), pairs_of],
        )
        return out[None, None]

    placed = (
        P("section", "dp", None, "tensor"),
        P("section", None, "dp", "tensor"),
        P("section", None),
        P("section"),
    )
    return jax.shard_map(
        local,
        mesh=mesh,
        in_specs=placed,
        out_specs=P("section", "dp", None, "tensor"),
        check_vma=False,
    )
```

```python
import functools
import math

import jax
import jax.numpy as jnp
from jax import lax
from jax.experimental import pallas as pl
from jax.experimental.pallas import tpu as pltpu
from jax.sharding import PartitionSpec as P

HD = 128
EPS = 1e-05
AXES = ("section", "dp", "tensor")
F32 = jnp.float32
BF16 = jnp.bfloat16
PARTS = 2
VMEM_BYTES = 16 * 1024 * 1024
STAT_ROWS = 16


def permute(array, sections, hop):
    pairs = []
    for s in range(sections):
        for d in range(2):
            for y in range(2):
                for c in range(2):
                    to = hop(s, d, y, c)
                    if to is None or not 0 <= to[0] < sections:
                        continue
                    ts, td, ty, tc = to
                    pairs.append((s * 8 + d * 4 + y * 2 + c, ts * 8 + td * 4 + ty * 2 + tc))
    return lax.ppermute(array, AXES, pairs)


def ring(s, d, y, c):
    return (s, 1 - d, y, c) if d != y else (s, d, 1 - y, c)


def cross(s, d, y, c):
    return (s, 1 - d, 1 - y, c) if d != y else (s, d, y, c)


def direct(s, d, y, c):
    return (s, d, y, c) if d != y else None


def forward(s, d, y, c):
    return (s, d, 1 - y, c) if d == y else None


def swap(s, d, y, c):
    return (s, d, 1 - y, c)


def sibling(s, d, y, c):
    return (s, d, y, 1 - c)


def peer(s, d, y, c):
    return (s, 1 - d, y, c)


def onward(hop):
    def moved(s, d, y, c):
        to = hop(s, d, y, c)
        return None if to is None else (to[0] + 1, *to[1:])

    return moved


def cost(microseconds):
    return pl.CostEstimate(flops=int(microseconds * 1.15e9), bytes_accessed=1000, transcendentals=0)


def any_spec():
    return pl.BlockSpec(memory_space=pl.ANY)


def vmem_spec():
    return pl.BlockSpec(memory_space=pltpu.VMEM)


def smem_spec():
    return pl.BlockSpec(memory_space=pltpu.SMEM)


def stage_kernel(place, weight, staged, semaphore):
    copy = pltpu.make_async_copy(weight, staged, semaphore)
    copy.start()
    copy.wait()


def stage(place, weight):
    return pl.pallas_call(
        stage_kernel,
        in_specs=[smem_spec(), any_spec()],
        out_specs=vmem_spec(),
        out_shape=pltpu.VMEM(weight.shape, weight.dtype),
        scratch_shapes=[pltpu.SemaphoreType.DMA(())],
        compiler_params=pltpu.CompilerParams(vmem_limit_bytes=VMEM_BYTES),
        cost_estimate=cost(4),
        name="stage",
    )(place, pltpu.with_memory_space_constraint(weight, pltpu.HBM))


def project_kernel(place, crossed, ringed, sib_crossed, sib_ringed, gain, weight, *refs):
    sent, kept, kept_mean, normed = refs[:4]
    out, semaphores = refs[4:] or (sent, None)
    rows = normed.shape[0] // 2
    width = crossed.shape[1]
    half = 2 * width
    core, dp, diagonal = place[0], place[1], place[2]
    means = []
    for mine, theirs, offset in (
        (crossed, sib_crossed, diagonal),
        (ringed, sib_ringed, 1 - diagonal),
    ):
        at = pl.ds(pl.multiple_of(offset * rows, rows), rows)
        pieces = [ref[...].astype(F32) for ref in (mine, theirs)]
        squares = sum(jnp.sum(piece * piece, axis=-1, keepdims=True) for piece in pieces)
        mean = squares * (1.0 / half)
        means.append(mean)
        inverse = lax.rsqrt(mean + EPS)
        for piece, order in zip(pieces, (core, 1 - core)):
            gains = gain[:, pl.ds(pl.multiple_of(dp * half + order * width, HD), width)]
            normed[at, pl.ds(pl.multiple_of(order * width, HD), width)] = (
                piece * inverse * gains.astype(F32)
            ).astype(BF16)
    on_diagonal = diagonal == 1
    sent_mean = jnp.where(on_diagonal, means[1], means[0])
    kept_mean[...] = jnp.where(on_diagonal, means[0], means[1])
    row = jnp.transpose(jnp.broadcast_to(sent_mean, (rows, HD)))[:STAT_ROWS]
    high = row.astype(BF16).astype(F32)
    mid = (row - high).astype(BF16).astype(F32)
    low = row - high - mid
    which = lax.broadcasted_iota(jnp.int32, row.shape, 0)
    stat = jnp.where(which == 0, high, jnp.where(which == 1, mid, low)).astype(BF16)
    for begin in range(0, width, rows):
        out[:STAT_ROWS, begin : begin + rows] = stat
    split = width // (2 * HD) * HD + HD
    copies = []
    for i, (k, begin, end) in enumerate(
        ((0, 0, width), (1, 0, width), (2, 0, split), (2, split, width))
    ):
        columns = slice(begin, end)
        product = jnp.dot(normed[...], weight[0, k, :, columns], preferred_element_type=F32)
        top = STAT_ROWS + k * rows
        out[top : top + rows, columns] = product[:rows].astype(BF16)
        kept[k, :, columns] = product[rows:]
        if semaphores is None:
            continue
        at = (slice(top if k else 0, top + rows), columns)
        copies.append(pltpu.make_async_copy(out.at[at], sent.at[at], semaphores.at[i]))
        copies[-1].start()
    for copy in copies:
        copy.wait()


def project(rows, place, four, gain, weight, apart, estimate):
    width = four[0].shape[1]
    sent_shape = (3 * rows + STAT_ROWS, width)
    return pl.pallas_call(
        project_kernel,
        in_specs=[smem_spec()] + [vmem_spec()] * 6,
        out_specs=[any_spec() if apart else vmem_spec(), vmem_spec(), vmem_spec()],
        out_shape=[
            (pltpu.HBM if apart else pltpu.VMEM)(sent_shape, BF16),
            pltpu.VMEM((3, rows, width), F32),
            pltpu.VMEM((rows, 1), F32),
        ],
        scratch_shapes=[pltpu.VMEM((2 * rows, 2 * width), BF16)]
        + [pltpu.VMEM(sent_shape, BF16), pltpu.SemaphoreType.DMA((4,))] * apart,
        compiler_params=pltpu.CompilerParams(vmem_limit_bytes=VMEM_BYTES),
        cost_estimate=cost(estimate),
        name="project",
    )(place, *four, gain, weight)


def mix(kept, received, kept_mean, earlier, pairs, put):
    rows, width = kept.shape[1:]
    stat = received[:STAT_ROWS, :rows].astype(F32)
    row = stat[0:1] + stat[1:2] + stat[2:3]
    mean_peer = jnp.transpose(jnp.broadcast_to(row, (HD, rows)))[:, :1]
    mean_kept = kept_mean[...]
    inverse = lax.rsqrt((mean_kept + mean_peer) * 0.5 + EPS)
    scale_kept = inverse * jnp.sqrt(mean_kept + EPS)
    scale_peer = inverse * jnp.sqrt(mean_peer + EPS)
    causal = lax.broadcasted_iota(jnp.int32, (rows, rows), 0) >= lax.broadcasted_iota(
        jnp.int32, (rows, rows), 1
    )
    heads = [slice(begin, begin + HD) for begin in range(0, width, HD)]
    held, scores = [], []
    for at in heads:
        queries, keys, values = (
            (
                kept[k, :, at] * scale_kept
                + received[STAT_ROWS + k * rows : STAT_ROWS + (k + 1) * rows, at].astype(F32)
                * scale_peer
            ).astype(BF16)
            for k in range(3)
        )
        pairs[0, :, at] = keys
        pairs[1, :, at] = values
        held.append([(ref[0, :, at], ref[1, :, at]) for ref in earlier] + [(keys, values)])
        scores.append(
            [
                lax.dot_general(queries, key, (((1,), (1,)), ((), ())), preferred_element_type=F32)
                * (1.0 / math.sqrt(HD))
                for key, _ in held[-1]
            ]
        )
        scores[-1][-1] = jnp.where(causal, scores[-1][-1], F32(-1e30))
    tops = [
        functools.reduce(jnp.maximum, [jnp.max(item, axis=-1, keepdims=True) for item in score])
        for score in scores
    ]
    raised = [[jnp.exp(item - top) for item in score] for score, top in zip(scores, tops)]
    overs = [1.0 / sum(jnp.sum(item, axis=-1, keepdims=True) for item in items) for items in raised]
    for at, items, over, pair in zip(heads, raised, overs, held):
        mixture = sum(
            jnp.dot((item * over).astype(BF16), value, preferred_element_type=F32)
            for item, (_, value) in zip(items, pair)
        )
        put(at, mixture)


def attend_kernel(kept, received, kept_mean, block, *refs):
    earlier, (out, pairs) = refs[:-2], refs[-2:]

    def put(at, mixture):
        out[:, at] = (block[:, at].astype(F32) + mixture).astype(BF16)

    mix(kept, received, kept_mean, earlier, pairs, put)


def hold_kernel(kept, received, kept_mean, *refs):
    owns, (held, pairs, whole) = refs[:-3], refs[-3:]
    rows = kept.shape[1]

    def put(at, mixture):
        held[:, at] = mixture

    mix(kept, received, kept_mean, (), pairs, put)
    for i, own in enumerate(owns):
        whole[i * rows : (i + 1) * rows] = own[...]


def final_kernel(
    place, flag, kept, received, kept_mean, earlier, held, first, second, before, own, out, pairs
):
    rows = kept.shape[1]
    diagonal, shadow = place[2] == 1, flag[0] == 1

    def settle(start, crossed, at, mixture):
        here = slice(start, start + rows)
        residual = jnp.where(diagonal, crossed[:, at].astype(F32), before[here, at].astype(F32))
        result = jnp.where(shadow, residual + mixture, own[here, at].astype(F32))
        out[here, at] = result.astype(BF16)

    def put(at, mixture):
        settle(rows, second, at, mixture)

    settle(0, first, slice(None), held[...])
    mix(kept, received, kept_mean, (earlier,), pairs, put)


def call_attend(kernel, name, scalars, arrays, out_shape):
    return pl.pallas_call(
        kernel,
        in_specs=[smem_spec() for _ in scalars] + [vmem_spec() for _ in arrays],
        out_shape=out_shape,
        compiler_params=pltpu.CompilerParams(vmem_limit_bytes=VMEM_BYTES),
        cost_estimate=cost(250),
        name=name,
    )(*scalars, *arrays)


def solution(mesh):
    sections = mesh.shape["section"]

    def local(inputs, qkv_weight, norm_gain, preempted):
        d = lax.axis_index("dp")
        t = lax.axis_index("tensor")
        y, c = t // 2, t % 2
        place = jnp.stack([c, d, (d == y).astype(c.dtype)]).astype(jnp.int32)
        place, diagonal, weight = lax.optimization_barrier((place, d == y, qkv_weight))
        weight = stage(place, weight)

        def spread(crossed, ringed):
            return (
                crossed,
                ringed,
                permute(crossed, sections, sibling),
                permute(ringed, sections, sibling),
            )

        def partial(four, apart, estimate):
            sent, kept, kept_mean = project(rows, place, four, norm_gain, weight, apart, estimate)
            return kept, permute(sent, sections, peer), kept_mean

        block = inputs[0, 0]
        rows = block.shape[0] // PARTS
        parts = [block[i * rows : (i + 1) * rows] for i in range(PARTS)]
        ringed = [permute(part, sections, ring) for part in parts]
        crossed = permute(parts[0], sections, cross)
        ringed[0], crossed, weight = lax.optimization_barrier((ringed[0], crossed, weight))
        weight = pltpu.with_memory_space_constraint(weight, pltpu.VMEM)
        sums = [partial(spread(crossed, ringed[0]), False, 3)]
        late, _ = lax.optimization_barrier((ringed[1], sums[0][2]))
        forwarded = permute(late, sections, forward)
        crossed = jnp.where(diagonal, parts[1], forwarded)
        sums.append(partial(spread(crossed, late), True, 0.001))
        width = block.shape[1]
        rows_of = pltpu.VMEM((rows, width), BF16)
        pairs_of = pltpu.VMEM((2, rows, width), BF16)

        def attend(part, item, held):
            return call_attend(
                attend_kernel, "attend", [], [*item, part, *held], [rows_of, pairs_of]
            )

        def carry(own):
            return permute(own, sections, onward(cross))

        first, pairs = attend(parts[0], sums[0], [])
        moved = [carry(first)]
        swapped = permute(moved[0], sections, swap)
        beside = permute(moved[0], sections, sibling)
        part = lax.optimization_barrier((parts[1], beside))[0]
        second, _ = attend(part, sums[1], [pairs])
        owns = [first, second]
        moved.append(carry(second))
        swapped, _ = lax.optimization_barrier((swapped, second))
        four = moved[0], swapped, beside, permute(swapped, sections, sibling)
        seconds = [partial(four, False, 3)]
        crossed, _ = lax.optimization_barrier((moved[1], seconds[0][2]))
        swapped = permute(crossed, sections, swap)
        seconds.append(partial(spread(crossed, swapped), True, 1))
        mixture, pairs, own = call_attend(
            hold_kernel,
            "hold",
            [],
            [*seconds[0], *owns],
            [pltpu.VMEM((rows, width), F32), pairs_of, pltpu.VMEM(block.shape, BF16)],
        )
        before = permute(own, sections, onward(direct))
        out, _ = call_attend(
            final_kernel,
            "final",
            [place, preempted],
            [*seconds[1], pairs, mixture, *moved, before, own],
            [jax.ShapeDtypeStruct(block.shape, BF16), pairs_of],
        )
        return out[None, None]

    placed = (
        P("section", "dp", None, "tensor"),
        P("section", None, "dp", "tensor"),
        P("section", None),
        P("section"),
    )
    return jax.shard_map(
        local,
        mesh=mesh,
        in_specs=placed,
        out_specs=P("section", "dp", None, "tensor"),
        check_vma=False,
    )
```

```python
import functools
import math

import jax
import jax.numpy as jnp
from jax import lax
from jax.experimental import pallas as pl
from jax.experimental.pallas import tpu as pltpu
from jax.sharding import PartitionSpec as P

HD = 128
EPS = 1e-05
AXES = ("section", "dp", "tensor")
F32 = jnp.float32
BF16 = jnp.bfloat16
VMEM_BYTES = 16 * 1024 * 1024
STAT_ROWS = 16


def chunk_rows(length):
    return [length * 7 // 16, length * 5 // 16, length // 4]


def permute(array, sections, hop):
    pairs = []
    for s in range(sections):
        for d in range(2):
            for y in range(2):
                for c in range(2):
                    to = hop(s, d, y, c)
                    if to is None or not 0 <= to[0] < sections:
                        continue
                    ts, td, ty, tc = to
                    pairs.append((s * 8 + d * 4 + y * 2 + c, ts * 8 + td * 4 + ty * 2 + tc))
    return lax.ppermute(array, AXES, pairs)


def ring(s, d, y, c):
    return (s, 1 - d, y, c) if d != y else (s, d, 1 - y, c)


def cross(s, d, y, c):
    return (s, 1 - d, 1 - y, c) if d != y else (s, d, y, c)


def direct(s, d, y, c):
    return (s, d, y, c) if d != y else None


def forward(s, d, y, c):
    return (s, d, 1 - y, c) if d == y else None


def swap(s, d, y, c):
    return (s, d, 1 - y, c)


def sibling(s, d, y, c):
    return (s, d, y, 1 - c)


def peer(s, d, y, c):
    return (s, 1 - d, y, c)


def onward(hop):
    def moved(s, d, y, c):
        to = hop(s, d, y, c)
        return None if to is None else (to[0] + 1, *to[1:])

    return moved


def cost(microseconds):
    return pl.CostEstimate(flops=int(microseconds * 1.15e9), bytes_accessed=1000, transcendentals=0)


def any_spec():
    return pl.BlockSpec(memory_space=pl.ANY)


def vmem_spec():
    return pl.BlockSpec(memory_space=pltpu.VMEM)


def smem_spec():
    return pl.BlockSpec(memory_space=pltpu.SMEM)


def stage_kernel(place, weight, staged, semaphore):
    copy = pltpu.make_async_copy(weight, staged, semaphore)
    copy.start()
    copy.wait()


def stage(place, weight):
    return pl.pallas_call(
        stage_kernel,
        in_specs=[smem_spec(), any_spec()],
        out_specs=vmem_spec(),
        out_shape=pltpu.VMEM(weight.shape, weight.dtype),
        scratch_shapes=[pltpu.SemaphoreType.DMA(())],
        compiler_params=pltpu.CompilerParams(vmem_limit_bytes=VMEM_BYTES),
        cost_estimate=cost(4),
        name="stage",
    )(place, pltpu.with_memory_space_constraint(weight, pltpu.HBM))


def project_kernel(start, place, crossed, ringed, sib_crossed, sib_ringed, gain, weight, *refs):
    sent, kept, kept_mean, normed = refs[:4]
    out, semaphores = refs[4:] or (sent, None)
    rows = normed.shape[0] // 2
    width = crossed.shape[1]
    half = 2 * width
    core, dp, diagonal = place[0], place[1], place[2]
    means = []
    for mine, theirs, offset in (
        (crossed, sib_crossed, diagonal),
        (ringed, sib_ringed, 1 - diagonal),
    ):
        at = pl.ds(pl.multiple_of(offset * rows, rows), rows)
        pieces = [ref[start : start + rows].astype(F32) for ref in (mine, theirs)]
        squares = sum(jnp.sum(piece * piece, axis=-1, keepdims=True) for piece in pieces)
        mean = squares * (1.0 / half)
        means.append(mean)
        inverse = lax.rsqrt(mean + EPS)
        for piece, order in zip(pieces, (core, 1 - core)):
            gains = gain[:, pl.ds(pl.multiple_of(dp * half + order * width, HD), width)]
            normed[at, pl.ds(pl.multiple_of(order * width, HD), width)] = (
                piece * inverse * gains.astype(F32)
            ).astype(BF16)
    on_diagonal = diagonal == 1
    sent_mean = jnp.where(on_diagonal, means[1], means[0])
    kept_mean[...] = jnp.where(on_diagonal, means[0], means[1])
    wide = jnp.broadcast_to(sent_mean, (rows, HD))
    if rows < HD:
        wide = jnp.concatenate([wide, jnp.zeros((HD - rows, HD), F32)])
    row = jnp.transpose(wide)[:STAT_ROWS]
    high = row.astype(BF16).astype(F32)
    mid = (row - high).astype(BF16).astype(F32)
    low = row - high - mid
    which = lax.broadcasted_iota(jnp.int32, row.shape, 0)
    stat = jnp.where(which == 0, high, jnp.where(which == 1, mid, low)).astype(BF16)
    for begin in range(0, width, HD):
        out[:STAT_ROWS, begin : begin + HD] = stat
    split = width // (2 * HD) * HD + HD
    copies = []
    for i, (k, begin, end) in enumerate(
        ((0, 0, width), (1, 0, width), (2, 0, split), (2, split, width))
    ):
        columns = slice(begin, end)
        product = jnp.dot(normed[...], weight[0, k, :, columns], preferred_element_type=F32)
        top = STAT_ROWS + k * rows
        out[top : top + rows, columns] = product[:rows].astype(BF16)
        kept[k, :, columns] = product[rows:]
        if semaphores is None:
            continue
        at = (slice(top if k else 0, top + rows), columns)
        copies.append(pltpu.make_async_copy(out.at[at], sent.at[at], semaphores.at[i]))
        copies[-1].start()
    for copy in copies:
        copy.wait()


def project(start, rows, place, four, gain, weight, apart, estimate):
    width = four[0].shape[1]
    sent_shape = (3 * rows + STAT_ROWS, width)
    return pl.pallas_call(
        functools.partial(project_kernel, start),
        in_specs=[smem_spec()] + [vmem_spec()] * 6,
        out_specs=[any_spec() if apart else vmem_spec(), vmem_spec(), vmem_spec()],
        out_shape=[
            (pltpu.HBM if apart else pltpu.VMEM)(sent_shape, BF16),
            pltpu.VMEM((3, rows, width), F32),
            pltpu.VMEM((rows, 1), F32),
        ],
        scratch_shapes=[pltpu.VMEM((2 * rows, 2 * width), BF16)]
        + [pltpu.VMEM(sent_shape, BF16), pltpu.SemaphoreType.DMA((4,))] * apart,
        compiler_params=pltpu.CompilerParams(vmem_limit_bytes=VMEM_BYTES),
        cost_estimate=cost(estimate),
        name="project",
    )(place, *four, gain, weight)


def mix(kept, received, kept_mean, earlier, pairs, put):
    rows, width = kept.shape[1:]
    stat = received[:STAT_ROWS, :HD].astype(F32)
    row = stat[0:1] + stat[1:2] + stat[2:3]
    mean_peer = jnp.transpose(jnp.broadcast_to(row, (HD, HD)))[:rows, :1]
    mean_kept = kept_mean[...]
    inverse = lax.rsqrt((mean_kept + mean_peer) * 0.5 + EPS)
    scale_kept = inverse * jnp.sqrt(mean_kept + EPS)
    scale_peer = inverse * jnp.sqrt(mean_peer + EPS)
    start = sum(ref.shape[1] for ref in earlier)
    padding = -(start + rows) % HD
    shape = (rows, start + rows + padding)
    causal = lax.broadcasted_iota(jnp.int32, shape, 0) + start >= lax.broadcasted_iota(
        jnp.int32, shape, 1
    )

    def together(k, at, last):
        pieces = [ref[k, :, at] for ref in earlier] + [last]
        if padding:
            pieces.append(jnp.zeros((padding, HD), BF16))
        return jnp.concatenate(pieces) if len(pieces) > 1 else last

    heads = [slice(begin, begin + HD) for begin in range(0, width, HD)]
    held, scores = [], []
    for at in heads:
        queries, keys, values = (
            (
                kept[k, :, at] * scale_kept
                + received[STAT_ROWS + k * rows : STAT_ROWS + (k + 1) * rows, at].astype(F32)
                * scale_peer
            ).astype(BF16)
            for k in range(3)
        )
        pairs[0, :, at] = keys
        pairs[1, :, at] = values
        held.append(together(1, at, values))
        score = lax.dot_general(
            queries, together(0, at, keys), (((1,), (1,)), ((), ())), preferred_element_type=F32
        )
        scores.append(jnp.where(causal, score * (1.0 / math.sqrt(HD)), F32(-1e30)))
    tops = [jnp.max(score, axis=-1, keepdims=True) for score in scores]
    raised = [jnp.exp(score - top) for score, top in zip(scores, tops)]
    overs = [1.0 / jnp.sum(item, axis=-1, keepdims=True) for item in raised]
    for at, item, over, values in zip(heads, raised, overs, held):
        put(at, jnp.dot((item * over).astype(BF16), values, preferred_element_type=F32))


def attend_kernel(kept, received, kept_mean, block, *refs):
    earlier, (out, pairs) = refs[:-2], refs[-2:]

    def put(at, mixture):
        out[:, at] = (block[:, at].astype(F32) + mixture).astype(BF16)

    mix(kept, received, kept_mean, earlier, pairs, put)


def hold_kernel(count, kept, received, kept_mean, *refs):
    earlier = refs[:count]
    if count:
        owns, (held, pairs) = (), refs[count:]
    else:
        owns, (held, pairs, whole) = refs[:-3], refs[-3:]

    def put(at, mixture):
        held[:, at] = mixture

    mix(kept, received, kept_mean, earlier, pairs, put)
    begin = 0
    for own in owns:
        whole[begin : begin + own.shape[0]] = own[...]
        begin += own.shape[0]


def final_kernel(count, place, flag, kept, received, kept_mean, *refs):
    earlier, mixtures, crossed = refs[:count], refs[count : 2 * count], refs[2 * count : -4]
    before, own, out, pairs = refs[-4:]
    diagonal, shadow = place[2] == 1, flag[0] == 1

    def settle(start, arrived, at, mixture):
        here = slice(start, start + arrived.shape[0])
        residual = jnp.where(diagonal, arrived[:, at].astype(F32), before[here, at].astype(F32))
        result = jnp.where(shadow, residual + mixture, own[here, at].astype(F32))
        out[here, at] = result.astype(BF16)

    begin = 0
    for arrived, mixture in zip(crossed, mixtures):
        settle(begin, arrived, slice(None), mixture[...])
        begin += arrived.shape[0]

    def put(at, mixture):
        settle(begin, crossed[-1], at, mixture)

    mix(kept, received, kept_mean, earlier, pairs, put)


def call_attend(kernel, name, scalars, arrays, out_shape):
    return pl.pallas_call(
        kernel,
        in_specs=[smem_spec() for _ in scalars] + [vmem_spec() for _ in arrays],
        out_shape=out_shape,
        compiler_params=pltpu.CompilerParams(vmem_limit_bytes=VMEM_BYTES),
        cost_estimate=cost(250),
        name=name,
    )(*scalars, *arrays)


def solution(mesh):
    sections = mesh.shape["section"]

    def local(inputs, qkv_weight, norm_gain, preempted):
        d = lax.axis_index("dp")
        t = lax.axis_index("tensor")
        y, c = t // 2, t % 2
        place = jnp.stack([c, d, (d == y).astype(c.dtype)]).astype(jnp.int32)
        place, diagonal, weight = lax.optimization_barrier((place, d == y, qkv_weight))
        weight = stage(place, weight)

        def spread(crossed, ringed):
            return (
                crossed,
                ringed,
                permute(crossed, sections, sibling),
                permute(ringed, sections, sibling),
            )

        def partial(start, rows, four, apart, estimate):
            sent, kept, kept_mean = project(
                start, rows, place, four, norm_gain, weight, apart, estimate
            )
            return kept, permute(sent, sections, peer), kept_mean

        block = inputs[0, 0]
        length, width = block.shape
        sizes = chunk_rows(length)
        begins = [sum(sizes[:i]) for i in range(len(sizes))]
        parts = [block[begin : begin + size] for begin, size in zip(begins, sizes)]
        ringed = permute(parts[0], sections, ring)
        crossed = permute(parts[0], sections, cross)
        others = block[sizes[0] :]
        late = permute(others, sections, ring)
        crossed, ringed, weight = lax.optimization_barrier((crossed, ringed, weight))
        weight = pltpu.with_memory_space_constraint(weight, pltpu.VMEM)
        sums = [partial(0, sizes[0], spread(crossed, ringed), False, 3)]
        late, _ = lax.optimization_barrier((late, sums[0][2]))
        crossed = jnp.where(diagonal, others, permute(late, sections, forward))
        four = spread(crossed, late)
        for begin, size in zip(begins[1:-1], sizes[1:-1]):
            *four, _ = lax.optimization_barrier((*four, sums[-1][2]))
            sums.append(partial(begin - sizes[0], size, four, True, 0.001))

        def pairs_of(size):
            return pltpu.VMEM((2, size, width), BF16)

        def attend(i, part, held):
            return call_attend(
                attend_kernel,
                "attend",
                [],
                [*sums[i], part, *held],
                [pltpu.VMEM((sizes[i], width), BF16), pairs_of(sizes[i])],
            )

        part, _ = lax.optimization_barrier((parts[0], sums[-1][2]))
        own, pairs = attend(0, part, [])
        owns, held = [own], [pairs]
        moved = [permute(own, sections, onward(cross))]
        *four, _ = lax.optimization_barrier((*four, own))
        sums.append(partial(begins[-1] - sizes[0], sizes[-1], four, True, 0.001))

        mixtures, mixed, seconds = [], [], []

        def hold(i, after):
            shapes = [pltpu.VMEM((sizes[i], width), F32), pairs_of(sizes[i])]
            if not i:
                shapes.append(pltpu.VMEM(block.shape, BF16))
            kept, received, kept_mean = seconds[i]
            kept, _ = lax.optimization_barrier((kept, after))
            mixture, pairs, *first = call_attend(
                functools.partial(hold_kernel, i),
                "hold",
                [],
                [kept, received, kept_mean, *mixed, *(owns if not i else [])],
                shapes,
            )
            mixtures.append(mixture)
            mixed.append(pairs)
            return first

        for i, size in enumerate(sizes):
            crossed = moved[i]
            last = i + 1 == len(sizes)
            if not i:
                crossed, _ = lax.optimization_barrier((crossed, sums[-1][2]))
            else:
                if last:
                    (whole,) = hold(0, seconds[-1][2])
                    after = mixtures[0]
                else:
                    part, _ = lax.optimization_barrier((parts[i + 1], seconds[-1][2]))
                    own, pairs = attend(i + 1, part, held)
                    after = own
                crossed, _ = lax.optimization_barrier((crossed, after))
            swapped = permute(crossed, sections, swap)
            beside = permute(crossed, sections, sibling)
            if not i:
                part, _, _ = lax.optimization_barrier((parts[1], beside, sums[-1][2]))
                own, pairs = attend(1, part, held)
            if not last:
                owns.append(own)
                held.append(pairs)
                on_its_way, _ = lax.optimization_barrier((own, beside))
                moved.append(permute(on_its_way, sections, onward(cross)))
                swapped, _ = lax.optimization_barrier((swapped, own))
            four = crossed, swapped, beside, permute(swapped, sections, sibling)
            seconds.append(partial(0, size, four, bool(i), 0.001 if i else 3))
        for i in range(1, len(sizes) - 1):
            hold(i, seconds[-1][2])
        before = permute(whole, sections, onward(direct))
        out, _ = call_attend(
            functools.partial(final_kernel, len(mixtures)),
            "final",
            [place, preempted],
            [*seconds[-1], *mixed, *mixtures, *moved, before, whole],
            [jax.ShapeDtypeStruct(block.shape, BF16), pairs_of(sizes[-1])],
        )
        return out[None, None]

    placed = (
        P("section", "dp", None, "tensor"),
        P("section", None, "dp", "tensor"),
        P("section", None),
        P("section"),
    )
    return jax.shard_map(
        local,
        mesh=mesh,
        in_specs=placed,
        out_specs=P("section", "dp", None, "tensor"),
        check_vma=False,
    )
```

```python
import functools
import math

import jax
import jax.numpy as jnp
from jax import lax
from jax.experimental import pallas as pl
from jax.experimental.pallas import tpu as pltpu
from jax.sharding import PartitionSpec as P

HD = 128
EPS = 1e-05
AXES = ("section", "dp", "tensor")
F32 = jnp.float32
BF16 = jnp.bfloat16
PARTS = 2
VMEM_BYTES = 16 * 1024 * 1024
STAT_ROWS = 16


def permute(array, sections, hop):
    pairs = []
    for s in range(sections):
        for d in range(2):
            for y in range(2):
                for c in range(2):
                    to = hop(s, d, y, c)
                    if to is None or not 0 <= to[0] < sections:
                        continue
                    ts, td, ty, tc = to
                    pairs.append((s * 8 + d * 4 + y * 2 + c, ts * 8 + td * 4 + ty * 2 + tc))
    return lax.ppermute(array, AXES, pairs)


def ring(s, d, y, c):
    return (s, 1 - d, y, c) if d != y else (s, d, 1 - y, c)


def cross(s, d, y, c):
    return (s, 1 - d, 1 - y, c) if d != y else (s, d, y, c)


def direct(s, d, y, c):
    return (s, d, y, c) if d != y else None


def across_y(s, d, y, c):
    return (s, d, 1 - y, c) if d != y else None


def across_x(s, d, y, c):
    return (s, 1 - d, y, c) if d == y else None


def swap(s, d, y, c):
    return (s, d, 1 - y, c)


def sibling(s, d, y, c):
    return (s, d, y, 1 - c)


def peer(s, d, y, c):
    return (s, 1 - d, y, c)


def onward(hop):
    def moved(s, d, y, c):
        to = hop(s, d, y, c)
        return None if to is None else (to[0] + 1, *to[1:])

    return moved


def cost(microseconds):
    return pl.CostEstimate(flops=int(microseconds * 1.15e9), bytes_accessed=1000, transcendentals=0)


def any_spec():
    return pl.BlockSpec(memory_space=pl.ANY)


def vmem_spec():
    return pl.BlockSpec(memory_space=pltpu.VMEM)


def smem_spec():
    return pl.BlockSpec(memory_space=pltpu.SMEM)


def stage_kernel(place, weight, staged, semaphore):
    copy = pltpu.make_async_copy(weight, staged, semaphore)
    copy.start()
    copy.wait()


def stage(place, weight):
    return pl.pallas_call(
        stage_kernel,
        in_specs=[smem_spec(), any_spec()],
        out_specs=vmem_spec(),
        out_shape=pltpu.VMEM(weight.shape, weight.dtype),
        scratch_shapes=[pltpu.SemaphoreType.DMA(())],
        compiler_params=pltpu.CompilerParams(vmem_limit_bytes=VMEM_BYTES),
        cost_estimate=cost(4),
        name="stage",
    )(place, pltpu.with_memory_space_constraint(weight, pltpu.HBM))


def project_kernel(
    cuts, apart, place, crossed, ringed, sib_crossed, sib_ringed, gain, weight, *refs
):
    count = len(cuts)
    sents, (kept, kept_mean, normed) = refs[:count], refs[count : count + 3]
    outs = refs[count + 3 : -1] if apart else sents
    rows = normed.shape[0] // 2
    width = crossed.shape[1]
    half = 2 * width
    core, dp, diagonal = place[0], place[1], place[2]
    means = []
    for mine, theirs, offset in (
        (crossed, sib_crossed, diagonal),
        (ringed, sib_ringed, 1 - diagonal),
    ):
        at = pl.ds(pl.multiple_of(offset * rows, rows), rows)
        pieces = [ref[...].astype(F32) for ref in (mine, theirs)]
        squares = sum(jnp.sum(piece * piece, axis=-1, keepdims=True) for piece in pieces)
        mean = squares * (1.0 / half)
        means.append(mean)
        inverse = lax.rsqrt(mean + EPS)
        for piece, order in zip(pieces, (core, 1 - core)):
            gains = gain[:, pl.ds(pl.multiple_of(dp * half + order * width, HD), width)]
            normed[at, pl.ds(pl.multiple_of(order * width, HD), width)] = (
                piece * inverse * gains.astype(F32)
            ).astype(BF16)
    on_diagonal = diagonal == 1
    sent_mean = jnp.where(on_diagonal, means[1], means[0])
    kept_mean[...] = jnp.where(on_diagonal, means[0], means[1])
    row = jnp.transpose(jnp.broadcast_to(sent_mean, (rows, HD)))[:STAT_ROWS]
    high = row.astype(BF16).astype(F32)
    mid = (row - high).astype(BF16).astype(F32)
    low = row - high - mid
    which = lax.broadcasted_iota(jnp.int32, row.shape, 0)
    stat = jnp.where(which == 0, high, jnp.where(which == 1, mid, low)).astype(BF16)
    copies = []
    for (begin, end), out, sent in zip(cuts, outs, sents):
        for column in range(0, end - begin, rows):
            out[:STAT_ROWS, column : column + rows] = stat
        for k in range(3):
            product = jnp.dot(normed[...], weight[0, k, :, begin:end], preferred_element_type=F32)
            top = STAT_ROWS + k * rows
            out[top : top + rows] = product[:rows].astype(BF16)
            kept[k, :, begin:end] = product[rows:]
            if apart:
                at = pl.ds(top, rows) if k else pl.ds(0, top + rows)
                copies.append(
                    pltpu.make_async_copy(out.at[at], sent.at[at], refs[-1].at[len(copies)])
                )
                copies[-1].start()
    for copy in copies:
        copy.wait()


def project(rows, place, four, gain, weight, cuts, apart, estimate):
    width = four[0].shape[1]
    shapes = [(3 * rows + STAT_ROWS, end - begin) for begin, end in cuts]
    scratch = [pltpu.VMEM((2 * rows, 2 * width), BF16)]
    if apart:
        scratch += [pltpu.VMEM(shape, BF16) for shape in shapes]
        scratch.append(pltpu.SemaphoreType.DMA((3 * len(cuts),)))
    return pl.pallas_call(
        functools.partial(project_kernel, cuts, apart),
        in_specs=[smem_spec()] + [vmem_spec()] * 6,
        out_specs=[any_spec() if apart else vmem_spec() for _ in cuts] + [vmem_spec()] * 2,
        out_shape=[(pltpu.HBM if apart else pltpu.VMEM)(shape, BF16) for shape in shapes]
        + [pltpu.VMEM((3, rows, width), F32), pltpu.VMEM((rows, 1), F32)],
        scratch_shapes=scratch,
        compiler_params=pltpu.CompilerParams(vmem_limit_bytes=VMEM_BYTES),
        cost_estimate=cost(estimate),
        name="project",
    )(place, *four, gain, weight)


def mix(kept, received, kept_mean, earlier, pairs, put, first=0):
    rows = kept.shape[1]
    last = first + received.shape[1]
    stat = received[:STAT_ROWS, :rows].astype(F32)
    row = stat[0:1] + stat[1:2] + stat[2:3]
    mean_peer = jnp.transpose(jnp.broadcast_to(row, (HD, rows)))[:, :1]
    mean_kept = kept_mean[...]
    inverse = lax.rsqrt((mean_kept + mean_peer) * 0.5 + EPS)
    scale_kept = inverse * jnp.sqrt(mean_kept + EPS)
    scale_peer = inverse * jnp.sqrt(mean_peer + EPS)
    causal = lax.broadcasted_iota(jnp.int32, (rows, rows), 0) >= lax.broadcasted_iota(
        jnp.int32, (rows, rows), 1
    )
    heads = [slice(begin, begin + HD) for begin in range(first, last, HD)]
    held, scores = [], []
    for at in heads:
        queries, keys, values = (
            (
                kept[k, :, at] * scale_kept
                + received[
                    STAT_ROWS + k * rows : STAT_ROWS + (k + 1) * rows,
                    at.start - first : at.stop - first,
                ].astype(F32)
                * scale_peer
            ).astype(BF16)
            for k in range(3)
        )
        if pairs is not None:
            pairs[0, :, at] = keys
            pairs[1, :, at] = values
        held.append([(ref[0, :, at], ref[1, :, at]) for ref in earlier] + [(keys, values)])
        scores.append(
            [
                lax.dot_general(queries, key, (((1,), (1,)), ((), ())), preferred_element_type=F32)
                * (1.0 / math.sqrt(HD))
                for key, _ in held[-1]
            ]
        )
        scores[-1][-1] = jnp.where(causal, scores[-1][-1], F32(-1e30))
    tops = [
        functools.reduce(jnp.maximum, [jnp.max(item, axis=-1, keepdims=True) for item in score])
        for score in scores
    ]
    raised = [[jnp.exp(item - top) for item in score] for score, top in zip(scores, tops)]
    overs = [1.0 / sum(jnp.sum(item, axis=-1, keepdims=True) for item in items) for items in raised]
    for at, items, over, pair in zip(heads, raised, overs, held):
        mixture = sum(
            jnp.dot((item * over).astype(BF16), value, preferred_element_type=F32)
            for item, (_, value) in zip(items, pair)
        )
        put(at, mixture)


def attend_kernel(kept, received, kept_mean, block, *refs):
    earlier, (out, again, pairs) = refs[:-3], refs[-3:]

    def put(at, mixture):
        out[:, at] = (block[:, at].astype(F32) + mixture).astype(BF16)
        again[:, at] = out[:, at]

    mix(kept, received, kept_mean, earlier, pairs, put)


def hold_kernel(kept, received, kept_mean, *refs):
    owns, (held, pairs, whole) = refs[:-3], refs[-3:]
    rows = kept.shape[1]

    def put(at, mixture):
        held[:, at] = mixture

    mix(kept, received, kept_mean, (), pairs, put)
    for i, own in enumerate(owns):
        whole[i * rows : (i + 1) * rows] = own[...]


def part_kernel(kept, received, kept_mean, earlier, held):
    def put(at, mixture):
        held[:, at] = mixture

    mix(kept, received, kept_mean, (earlier,), None, put)


def final_kernel(
    place, flag, kept, received, kept_mean, earlier, held, part, first, second, before, own, out
):
    rows = kept.shape[1]
    diagonal, shadow = place[2] == 1, flag[0] == 1

    def settle(start, crossed, at, mixture):
        here = slice(start, start + rows)
        residual = jnp.where(diagonal, crossed[:, at].astype(F32), before[here, at].astype(F32))
        result = jnp.where(shadow, residual + mixture, own[here, at].astype(F32))
        out[here, at] = result.astype(BF16)

    def put(at, mixture):
        settle(rows, second, at, mixture)

    done = part.shape[1]
    settle(0, first, slice(None), held[...])
    settle(rows, second, slice(0, done), part[...])
    mix(kept, received, kept_mean, (earlier,), None, put, done)


def call_attend(kernel, name, scalars, arrays, out_shape):
    return pl.pallas_call(
        kernel,
        in_specs=[smem_spec() for _ in scalars] + [vmem_spec() for _ in arrays],
        out_shape=out_shape,
        compiler_params=pltpu.CompilerParams(vmem_limit_bytes=VMEM_BYTES),
        cost_estimate=cost(250),
        name=name,
    )(*scalars, *arrays)


def solution(mesh):
    sections = mesh.shape["section"]

    def local(inputs, qkv_weight, norm_gain, preempted):
        d = lax.axis_index("dp")
        t = lax.axis_index("tensor")
        y, c = t // 2, t % 2
        place = jnp.stack([c, d, (d == y).astype(c.dtype)]).astype(jnp.int32)
        place, diagonal, weight = lax.optimization_barrier((place, d == y, qkv_weight))
        weight = stage(place, weight)

        def spread(crossed, ringed):
            return (
                crossed,
                ringed,
                permute(crossed, sections, sibling),
                permute(ringed, sections, sibling),
            )

        def partial(four, apart, estimate, cuts=None):
            width = four[0].shape[1]
            *sents, kept, kept_mean = project(
                rows, place, four, norm_gain, weight, cuts or [(0, width)], apart, estimate
            )
            received = [permute(sent, sections, peer) for sent in sents]
            return kept, received if cuts else received[0], kept_mean

        block = inputs[0, 0]
        rows = block.shape[0] // PARTS
        parts = [block[i * rows : (i + 1) * rows] for i in range(PARTS)]
        ringed = permute(parts[0], sections, ring)
        crossed = permute(parts[0], sections, cross)
        relayed = permute(parts[1], sections, across_y)
        ringed, crossed, weight = lax.optimization_barrier((ringed, crossed, weight))
        weight = pltpu.with_memory_space_constraint(weight, pltpu.VMEM)
        sums = [partial(spread(crossed, ringed), False, 3)]
        crossed = jnp.where(diagonal, parts[1], permute(relayed, sections, across_x))
        crossed, _ = lax.optimization_barrier((crossed, sums[0][2]))
        swapped = permute(crossed, sections, swap)
        sums.append(partial(spread(crossed, swapped), True, 0.001))
        width = block.shape[1]
        rows_of = pltpu.VMEM((rows, width), BF16)
        pairs_of = pltpu.VMEM((2, rows, width), BF16)

        def attend(part, item, held):
            return call_attend(
                attend_kernel,
                "attend",
                [],
                [*item, part, *held],
                [rows_of, pltpu.HBM((rows, width), BF16), pairs_of],
            )

        def carry(own):
            return permute(own, sections, onward(cross))

        first, first_again, pairs = attend(parts[0], sums[0], [])
        moved = [carry(first)]
        swapped = permute(moved[0], sections, swap)
        beside = permute(moved[0], sections, sibling)
        part = lax.optimization_barrier((parts[1], beside))[0]
        second, second_again, _ = attend(part, sums[1], [pairs])
        owns = [first_again, second_again]
        moved.append(carry(second))
        swapped, _ = lax.optimization_barrier((swapped, second))
        four = moved[0], swapped, beside, permute(swapped, sections, sibling)
        seconds = [partial(four, False, 3)]
        crossed, _ = lax.optimization_barrier((moved[1], seconds[0][2]))
        swapped = permute(crossed, sections, swap)
        cut = (width // HD + 1) // 2 * HD
        cuts = [(0, cut), (cut, width)]
        kept, received, kept_mean = partial(spread(crossed, swapped), True, 1, cuts)
        mixture, pairs, own = call_attend(
            hold_kernel,
            "hold",
            [],
            [*seconds[0], *owns],
            [pltpu.VMEM((rows, width), F32), pairs_of, pltpu.VMEM(block.shape, BF16)],
        )
        before = permute(own, sections, onward(direct))
        (part,) = call_attend(
            part_kernel,
            "part",
            [],
            [kept, received[0], kept_mean, pairs],
            [pltpu.VMEM((rows, cut), F32)],
        )
        (out,) = call_attend(
            final_kernel,
            "final",
            [place, preempted],
            [kept, received[1], kept_mean, pairs, mixture, part, *moved, before, own],
            [jax.ShapeDtypeStruct(block.shape, BF16)],
        )
        return out[None, None]

    placed = (
        P("section", "dp", None, "tensor"),
        P("section", None, "dp", "tensor"),
        P("section", None),
        P("section"),
    )
    return jax.shard_map(
        local,
        mesh=mesh,
        in_specs=placed,
        out_specs=P("section", "dp", None, "tensor"),
        check_vma=False,
    )
```

```python
import functools
import math

import jax
import jax.numpy as jnp
from jax import lax
from jax.experimental import pallas as pl
from jax.experimental.pallas import tpu as pltpu
from jax.sharding import PartitionSpec as P

HD = 128
EPS = 1e-05
AXES = ("section", "dp", "tensor")
F32 = jnp.float32
BF16 = jnp.bfloat16
PARTS = 2
VMEM_BYTES = 16 * 1024 * 1024
STAT_ROWS = 16


def permute(array, sections, hop):
    pairs = []
    for s in range(sections):
        for d in range(2):
            for y in range(2):
                for c in range(2):
                    to = hop(s, d, y, c)
                    if to is None or not 0 <= to[0] < sections:
                        continue
                    ts, td, ty, tc = to
                    pairs.append((s * 8 + d * 4 + y * 2 + c, ts * 8 + td * 4 + ty * 2 + tc))
    return lax.ppermute(array, AXES, pairs)


def ring(s, d, y, c):
    return (s, 1 - d, y, c) if d != y else (s, d, 1 - y, c)


def cross(s, d, y, c):
    return (s, 1 - d, 1 - y, c) if d != y else (s, d, y, c)


def direct(s, d, y, c):
    return (s, d, y, c)


def forward(s, d, y, c):
    return (s, d, 1 - y, c) if d == y else None


def swap(s, d, y, c):
    return (s, d, 1 - y, c)


def sibling(s, d, y, c):
    return (s, d, y, 1 - c)


def peer(s, d, y, c):
    return (s, 1 - d, y, c)


def onward(hop):
    def moved(s, d, y, c):
        to = hop(s, d, y, c)
        return None if to is None else (to[0] + 1, *to[1:])

    return moved


def cost(microseconds):
    return pl.CostEstimate(flops=int(microseconds * 1.15e9), bytes_accessed=1000, transcendentals=0)


def any_spec():
    return pl.BlockSpec(memory_space=pl.ANY)


def vmem_spec():
    return pl.BlockSpec(memory_space=pltpu.VMEM)


def smem_spec():
    return pl.BlockSpec(memory_space=pltpu.SMEM)


def stage_kernel(place, weight, staged, semaphore):
    copy = pltpu.make_async_copy(weight, staged, semaphore)
    copy.start()
    copy.wait()


def stage(place, weight):
    return pl.pallas_call(
        stage_kernel,
        in_specs=[smem_spec(), any_spec()],
        out_specs=vmem_spec(),
        out_shape=pltpu.VMEM(weight.shape, weight.dtype),
        scratch_shapes=[pltpu.SemaphoreType.DMA(())],
        compiler_params=pltpu.CompilerParams(vmem_limit_bytes=VMEM_BYTES),
        cost_estimate=cost(4),
        name="stage",
    )(place, pltpu.with_memory_space_constraint(weight, pltpu.HBM))


def project_kernel(
    cuts, apart, owned, place, crossed, ringed, sib_crossed, sib_ringed, gain, weight, *refs
):
    count = len(cuts)
    semaphores = refs[-1]
    owns, refs = refs[:owned], refs[owned:-1]
    sents, (kept, kept_mean, *whole), (normed, *outs) = (
        refs[:count],
        refs[count : count + 2 + bool(owned)],
        refs[count + 2 + bool(owned) :],
    )
    copies = []

    def copy(source, target):
        copies.append(pltpu.make_async_copy(source, target, semaphores.at[len(copies)]))
        copies[-1].start()

    begin = 0
    for own in owns:
        copy(own, whole[0].at[pl.ds(begin, own.shape[0])])
        begin += own.shape[0]
    outs = outs if apart else sents
    rows = normed.shape[0] // 2
    width = crossed.shape[1]
    half = 2 * width
    core, dp, diagonal = place[0], place[1], place[2]
    means = []
    for mine, theirs, offset in (
        (crossed, sib_crossed, diagonal),
        (ringed, sib_ringed, 1 - diagonal),
    ):
        at = pl.ds(pl.multiple_of(offset * rows, rows), rows)
        pieces = [ref[...].astype(F32) for ref in (mine, theirs)]
        squares = sum(jnp.sum(piece * piece, axis=-1, keepdims=True) for piece in pieces)
        mean = squares * (1.0 / half)
        means.append(mean)
        inverse = lax.rsqrt(mean + EPS)
        for piece, order in zip(pieces, (core, 1 - core)):
            gains = gain[:, pl.ds(pl.multiple_of(dp * half + order * width, HD), width)]
            normed[at, pl.ds(pl.multiple_of(order * width, HD), width)] = (
                piece * inverse * gains.astype(F32)
            ).astype(BF16)
    on_diagonal = diagonal == 1
    sent_mean = jnp.where(on_diagonal, means[1], means[0])
    kept_mean[...] = jnp.where(on_diagonal, means[0], means[1])
    row = jnp.transpose(jnp.broadcast_to(sent_mean, (rows, HD)))[:STAT_ROWS]
    high = row.astype(BF16).astype(F32)
    mid = (row - high).astype(BF16).astype(F32)
    low = row - high - mid
    which = lax.broadcasted_iota(jnp.int32, row.shape, 0)
    stat = jnp.where(which == 0, high, jnp.where(which == 1, mid, low)).astype(BF16)
    for (begin, end), out, sent in zip(cuts, outs, sents):
        for column in range(0, end - begin, rows):
            out[:STAT_ROWS, column : column + rows] = stat
        for k in range(3):
            product = jnp.dot(normed[...], weight[0, k, :, begin:end], preferred_element_type=F32)
            top = STAT_ROWS + k * rows
            out[top : top + rows] = product[:rows].astype(BF16)
            kept[k, :, begin:end] = product[rows:]
            if apart:
                at = pl.ds(top, rows) if k else pl.ds(0, top + rows)
                copy(out.at[at], sent.at[at])
    for item in copies:
        item.wait()


def project(rows, place, four, gain, weight, cuts, apart, owns, estimate):
    width = four[0].shape[1]
    shapes = [(3 * rows + STAT_ROWS, end - begin) for begin, end in cuts]
    scratch = [pltpu.VMEM((2 * rows, 2 * width), BF16)]
    if apart:
        scratch += [pltpu.VMEM(shape, BF16) for shape in shapes]
    scratch.append(pltpu.SemaphoreType.DMA((3 * len(cuts) + len(owns),)))
    whole = (sum(own.shape[0] for own in owns), width)
    return pl.pallas_call(
        functools.partial(project_kernel, cuts, apart, len(owns)),
        in_specs=[smem_spec()] + [vmem_spec() for _ in range(6 + len(owns))],
        out_specs=[any_spec() if apart else vmem_spec() for _ in cuts]
        + [vmem_spec()] * 2
        + [any_spec()] * bool(owns),
        out_shape=[(pltpu.HBM if apart else pltpu.VMEM)(shape, BF16) for shape in shapes]
        + [pltpu.VMEM((3, rows, width), F32), pltpu.VMEM((rows, 1), F32)]
        + [pltpu.HBM(whole, BF16)] * bool(owns),
        scratch_shapes=scratch,
        compiler_params=pltpu.CompilerParams(vmem_limit_bytes=VMEM_BYTES),
        cost_estimate=cost(estimate),
        name="project",
    )(place, *four, gain, weight, *owns)


def mix(kept, received, kept_mean, earlier, pairs, put, first=0):
    rows = kept.shape[1]
    last = first + received.shape[1]
    stat = received[:STAT_ROWS, :rows].astype(F32)
    row = stat[0:1] + stat[1:2] + stat[2:3]
    mean_peer = jnp.transpose(jnp.broadcast_to(row, (HD, rows)))[:, :1]
    mean_kept = kept_mean[...]
    inverse = lax.rsqrt((mean_kept + mean_peer) * 0.5 + EPS)
    scale_kept = inverse * jnp.sqrt(mean_kept + EPS)
    scale_peer = inverse * jnp.sqrt(mean_peer + EPS)
    causal = lax.broadcasted_iota(jnp.int32, (rows, rows), 0) >= lax.broadcasted_iota(
        jnp.int32, (rows, rows), 1
    )
    heads = [slice(begin, begin + HD) for begin in range(first, last, HD)]
    held, scores = [], []
    for at in heads:
        queries, keys, values = (
            (
                kept[k, :, at] * scale_kept
                + received[
                    STAT_ROWS + k * rows : STAT_ROWS + (k + 1) * rows,
                    at.start - first : at.stop - first,
                ].astype(F32)
                * scale_peer
            ).astype(BF16)
            for k in range(3)
        )
        if pairs is not None:
            pairs[0, :, at] = keys
            pairs[1, :, at] = values
        held.append([(ref[0, :, at], ref[1, :, at]) for ref in earlier] + [(keys, values)])
        scores.append(
            [
                lax.dot_general(queries, key, (((1,), (1,)), ((), ())), preferred_element_type=F32)
                * (1.0 / math.sqrt(HD))
                for key, _ in held[-1]
            ]
        )
        scores[-1][-1] = jnp.where(causal, scores[-1][-1], F32(-1e30))
    tops = [
        functools.reduce(jnp.maximum, [jnp.max(item, axis=-1, keepdims=True) for item in score])
        for score in scores
    ]
    raised = [[jnp.exp(item - top) for item in score] for score, top in zip(scores, tops)]
    overs = [1.0 / sum(jnp.sum(item, axis=-1, keepdims=True) for item in items) for items in raised]
    for at, items, over, pair in zip(heads, raised, overs, held):
        mixture = sum(
            jnp.dot((item * over).astype(BF16), value, preferred_element_type=F32)
            for item, (_, value) in zip(items, pair)
        )
        put(at, mixture)


def attend_kernel(first, kept, received, kept_mean, block, *refs):
    earlier, out, pairs = ((), *refs) if first else (refs[:1], refs[1], None)

    def put(at, mixture):
        out[:, at] = (block[:, at].astype(F32) + mixture).astype(BF16)

    mix(kept, received, kept_mean, earlier, pairs, put)


def hold_kernel(kept, received, kept_mean, held, pairs):
    def put(at, mixture):
        held[:, at] = mixture

    mix(kept, received, kept_mean, (), pairs, put)


def part_kernel(kept, received, kept_mean, earlier, held):
    def put(at, mixture):
        held[:, at] = mixture

    mix(kept, received, kept_mean, (earlier,), None, put)


def settle_kernel(flag, held, part, before, own, out, rest, rest_own):
    rows, done = part.shape
    shadow = flag[0] == 1

    def settle(here, at, mixture):
        result = jnp.where(
            shadow, before[here, at].astype(F32) + mixture, own[here, at].astype(F32)
        )
        out[here, at] = result.astype(BF16)

    upper, lower = slice(0, rows), slice(rows, 2 * rows)
    settle(upper, slice(None), held[...])
    settle(lower, slice(0, done), part[...])
    out[lower, done:] = own[lower, done:]
    rest[...] = before[lower, done:]
    rest_own[...] = own[lower, done:]


def final_kernel(
    flag, kept, received, kept_mean, earlier, rest, rest_own, settled, out, piece, semaphore
):
    rows, width = kept.shape[1:]
    done = width - rest.shape[1]
    shadow = flag[0] == 1

    def put(at, mixture):
        here = slice(at.start - done, at.stop - done)
        result = rest[:, here].astype(F32) + mixture
        piece[:, here] = jnp.where(shadow, result, rest_own[:, here].astype(F32)).astype(BF16)

    mix(kept, received, kept_mean, (earlier,), None, put, done)
    copy = pltpu.make_async_copy(
        piece, out.at[pl.ds(rows, rows), pl.ds(done, width - done)], semaphore
    )
    copy.start()
    copy.wait()


def call_attend(kernel, name, scalars, arrays, out_shape):
    return pl.pallas_call(
        kernel,
        in_specs=[smem_spec() for _ in scalars] + [vmem_spec() for _ in arrays],
        out_shape=out_shape,
        compiler_params=pltpu.CompilerParams(vmem_limit_bytes=VMEM_BYTES),
        cost_estimate=cost(250),
        name=name,
    )(*scalars, *arrays)


def solution(mesh):
    sections = mesh.shape["section"]

    def local(inputs, qkv_weight, norm_gain, preempted):
        d = lax.axis_index("dp")
        t = lax.axis_index("tensor")
        y, c = t // 2, t % 2
        place = jnp.stack([c, d, (d == y).astype(c.dtype)]).astype(jnp.int32)
        place, diagonal, weight = lax.optimization_barrier((place, d == y, qkv_weight))
        weight = stage(place, weight)

        def spread(crossed, ringed):
            return (
                crossed,
                ringed,
                permute(crossed, sections, sibling),
                permute(ringed, sections, sibling),
            )

        def partial(four, apart, estimate, cuts=None, owns=()):
            width = four[0].shape[1]
            cuts_in = cuts or [(0, width)]
            results = project(
                rows, place, four, norm_gain, weight, cuts_in, apart, owns, estimate
            )
            received = [permute(sent, sections, peer) for sent in results[: len(cuts_in)]]
            kept, kept_mean, *whole = results[len(cuts_in) :]
            return (kept, received if cuts else received[0], kept_mean, *whole)

        block = inputs[0, 0]
        rows = block.shape[0] // PARTS
        parts = [block[i * rows : (i + 1) * rows] for i in range(PARTS)]
        ringed = [permute(part, sections, ring) for part in parts]
        crossed = permute(parts[0], sections, cross)
        ringed[0], crossed, weight = lax.optimization_barrier((ringed[0], crossed, weight))
        weight = pltpu.with_memory_space_constraint(weight, pltpu.VMEM)
        sums = [partial(spread(crossed, ringed[0]), False, 3)]
        late, _ = lax.optimization_barrier((ringed[1], sums[0][2]))
        forwarded = permute(late, sections, forward)
        crossed = jnp.where(diagonal, parts[1], forwarded)
        sums.append(partial(spread(crossed, late), True, 0.001))
        width = block.shape[1]
        rows_of = pltpu.VMEM((rows, width), BF16)
        pairs_of = pltpu.VMEM((2, rows, width), BF16)

        def attend(part, item, held):
            return call_attend(
                functools.partial(attend_kernel, not held),
                "attend",
                [],
                [*item, part, *held],
                [rows_of] if held else [rows_of, pairs_of],
            )

        def carry(own):
            return permute(own, sections, onward(cross))

        first, pairs = attend(parts[0], sums[0], [])
        moved = [carry(first)]
        swapped = permute(moved[0], sections, swap)
        beside = permute(moved[0], sections, sibling)
        part = lax.optimization_barrier((parts[1], beside))[0]
        (second,) = attend(part, sums[1], [pairs])
        moved.append(carry(second))
        swapped, _ = lax.optimization_barrier((swapped, second))
        four = moved[0], swapped, beside, permute(swapped, sections, sibling)
        *upper, own = partial(four, False, 3, None, [first, second])
        crossed, _ = lax.optimization_barrier((moved[1], upper[2]))
        swapped = permute(crossed, sections, swap)
        cut = (width // HD + 1) // 2 * HD
        cuts = [(0, cut), (cut, width)]
        kept, received, kept_mean = partial(spread(crossed, swapped), True, 1, cuts)
        mixture, pairs = call_attend(
            hold_kernel, "hold", [], upper, [pltpu.VMEM((rows, width), F32), pairs_of]
        )
        own, _ = lax.optimization_barrier((own, mixture))
        before = permute(own, sections, onward(direct))
        (part,) = call_attend(
            part_kernel,
            "part",
            [],
            [kept, received[0], kept_mean, pairs],
            [pltpu.VMEM((rows, cut), F32)],
        )
        rest_of = pltpu.VMEM((rows, width - cut), BF16)
        out, *rest = call_attend(
            settle_kernel,
            "settle",
            [preempted],
            [mixture, part, before, own],
            [jax.ShapeDtypeStruct(block.shape, BF16), rest_of, rest_of],
        )
        last = [kept, received[1], kept_mean, pairs, *rest]
        out = pl.pallas_call(
            final_kernel,
            in_specs=[smem_spec()] + [vmem_spec() for _ in last] + [any_spec()],
            out_specs=any_spec(),
            out_shape=jax.ShapeDtypeStruct(block.shape, BF16),
            input_output_aliases={1 + len(last): 0},
            scratch_shapes=[
                pltpu.VMEM((rows, width - cut), BF16),
                pltpu.SemaphoreType.DMA(()),
            ],
            compiler_params=pltpu.CompilerParams(vmem_limit_bytes=VMEM_BYTES),
            cost_estimate=cost(250),
            name="final",
        )(preempted, *last, out)
        return out[None, None]

    placed = (
        P("section", "dp", None, "tensor"),
        P("section", None, "dp", "tensor"),
        P("section", None),
        P("section"),
    )
    return jax.shard_map(
        local,
        mesh=mesh,
        in_specs=placed,
        out_specs=P("section", "dp", None, "tensor"),
        check_vma=False,
    )
```

```python
import functools
import math

import jax
import jax.numpy as jnp
from jax import lax
from jax.experimental import pallas as pl
from jax.experimental.pallas import tpu as pltpu
from jax.sharding import PartitionSpec as P

HD = 128
EPS = 1e-05
AXES = ("section", "dp", "tensor")
F32 = jnp.float32
BF16 = jnp.bfloat16
VMEM_BYTES = 16 * 1024 * 1024
STAT_ROWS = 16


def chunk_rows(length):
    first = length * 9 // 16
    return [first, length - first]


def permute(array, sections, hop):
    pairs = []
    for s in range(sections):
        for d in range(2):
            for y in range(2):
                for c in range(2):
                    to = hop(s, d, y, c)
                    if to is None or not 0 <= to[0] < sections:
                        continue
                    ts, td, ty, tc = to
                    pairs.append((s * 8 + d * 4 + y * 2 + c, ts * 8 + td * 4 + ty * 2 + tc))
    return lax.ppermute(array, AXES, pairs)


def ring(s, d, y, c):
    return (s, 1 - d, y, c) if d != y else (s, d, 1 - y, c)


def cross(s, d, y, c):
    return (s, 1 - d, 1 - y, c) if d != y else (s, d, y, c)


def direct(s, d, y, c):
    return (s, d, y, c)


def forward(s, d, y, c):
    return (s, d, 1 - y, c) if d == y else None


def swap(s, d, y, c):
    return (s, d, 1 - y, c)


def sibling(s, d, y, c):
    return (s, d, y, 1 - c)


def peer(s, d, y, c):
    return (s, 1 - d, y, c)


def onward(hop):
    def moved(s, d, y, c):
        to = hop(s, d, y, c)
        return None if to is None else (to[0] + 1, *to[1:])

    return moved


def cost(microseconds):
    return pl.CostEstimate(flops=int(microseconds * 1.15e9), bytes_accessed=1000, transcendentals=0)


def any_spec():
    return pl.BlockSpec(memory_space=pl.ANY)


def vmem_spec():
    return pl.BlockSpec(memory_space=pltpu.VMEM)


def smem_spec():
    return pl.BlockSpec(memory_space=pltpu.SMEM)


def stage_kernel(place, weight, staged, semaphore):
    copy = pltpu.make_async_copy(weight, staged, semaphore)
    copy.start()
    copy.wait()


def stage(place, weight):
    return pl.pallas_call(
        stage_kernel,
        in_specs=[smem_spec(), any_spec()],
        out_specs=vmem_spec(),
        out_shape=pltpu.VMEM(weight.shape, weight.dtype),
        scratch_shapes=[pltpu.SemaphoreType.DMA(())],
        compiler_params=pltpu.CompilerParams(vmem_limit_bytes=VMEM_BYTES),
        cost_estimate=cost(4),
        name="stage",
    )(place, pltpu.with_memory_space_constraint(weight, pltpu.HBM))


def to_lanes(column):
    rows = column.shape[0]
    wide = jnp.broadcast_to(column, (rows, HD))
    if rows % HD:
        wide = jnp.concatenate([wide, jnp.zeros((-rows % HD, HD), F32)])
    tiles = [jnp.transpose(wide[i : i + HD])[:STAT_ROWS] for i in range(0, wide.shape[0], HD)]
    return jnp.concatenate(tiles, axis=1) if len(tiles) > 1 else tiles[0]


def to_column(row, rows):
    tiles = [
        jnp.transpose(jnp.broadcast_to(row[:, i : i + HD], (HD, HD)))
        for i in range(0, row.shape[1], HD)
    ]
    column = jnp.concatenate(tiles) if len(tiles) > 1 else tiles[0]
    return column[:rows, :1]


def project_kernel(
    cuts, apart, owned, place, crossed, ringed, sib_crossed, sib_ringed, gain, weight, *refs
):
    count = len(cuts)
    semaphores = refs[-1]
    owns, refs = refs[:owned], refs[owned:-1]
    sents, (kept, kept_mean, *whole), (normed, *outs) = (
        refs[:count],
        refs[count : count + 2 + bool(owned)],
        refs[count + 2 + bool(owned) :],
    )
    copies = []

    def copy(source, target):
        copies.append(pltpu.make_async_copy(source, target, semaphores.at[len(copies)]))
        copies[-1].start()

    begin = 0
    for own in owns:
        copy(own, whole[0].at[pl.ds(begin, own.shape[0])])
        begin += own.shape[0]
    outs = outs if apart else sents
    rows = normed.shape[0] // 2
    width = crossed.shape[1]
    half = 2 * width
    core, dp, diagonal = place[0], place[1], place[2]
    means = []
    for mine, theirs, offset in (
        (crossed, sib_crossed, diagonal),
        (ringed, sib_ringed, 1 - diagonal),
    ):
        at = pl.ds(pl.multiple_of(offset * rows, rows), rows)
        pieces = [ref[...].astype(F32) for ref in (mine, theirs)]
        squares = sum(jnp.sum(piece * piece, axis=-1, keepdims=True) for piece in pieces)
        mean = squares * (1.0 / half)
        means.append(mean)
        inverse = lax.rsqrt(mean + EPS)
        for piece, order in zip(pieces, (core, 1 - core)):
            gains = gain[:, pl.ds(pl.multiple_of(dp * half + order * width, HD), width)]
            normed[at, pl.ds(pl.multiple_of(order * width, HD), width)] = (
                piece * inverse * gains.astype(F32)
            ).astype(BF16)
    on_diagonal = diagonal == 1
    sent_mean = jnp.where(on_diagonal, means[1], means[0])
    kept_mean[...] = jnp.where(on_diagonal, means[0], means[1])
    row = to_lanes(sent_mean)
    high = row.astype(BF16).astype(F32)
    mid = (row - high).astype(BF16).astype(F32)
    low = row - high - mid
    which = lax.broadcasted_iota(jnp.int32, row.shape, 0)
    stat = jnp.where(which == 0, high, jnp.where(which == 1, mid, low)).astype(BF16)
    for (begin, end), out, sent in zip(cuts, outs, sents):
        out[:STAT_ROWS] = jnp.zeros((STAT_ROWS, end - begin), BF16)
        out[:STAT_ROWS, : stat.shape[1]] = stat
        for k in range(3):
            product = jnp.dot(normed[...], weight[0, k, :, begin:end], preferred_element_type=F32)
            top = STAT_ROWS + k * rows
            out[top : top + rows] = product[:rows].astype(BF16)
            kept[k, :, begin:end] = product[rows:]
            if apart:
                at = pl.ds(top, rows) if k else pl.ds(0, top + rows)
                copy(out.at[at], sent.at[at])
    for item in copies:
        item.wait()


def project(rows, place, four, gain, weight, cuts, apart, owns, estimate):
    width = four[0].shape[1]
    shapes = [(3 * rows + STAT_ROWS, end - begin) for begin, end in cuts]
    scratch = [pltpu.VMEM((2 * rows, 2 * width), BF16)]
    if apart:
        scratch += [pltpu.VMEM(shape, BF16) for shape in shapes]
    scratch.append(pltpu.SemaphoreType.DMA((3 * len(cuts) + len(owns),)))
    whole = (sum(own.shape[0] for own in owns), width)
    return pl.pallas_call(
        functools.partial(project_kernel, cuts, apart, len(owns)),
        in_specs=[smem_spec()] + [vmem_spec() for _ in range(6 + len(owns))],
        out_specs=[any_spec() if apart else vmem_spec() for _ in cuts]
        + [vmem_spec()] * 2
        + [any_spec()] * bool(owns),
        out_shape=[(pltpu.HBM if apart else pltpu.VMEM)(shape, BF16) for shape in shapes]
        + [pltpu.VMEM((3, rows, width), F32), pltpu.VMEM((rows, 1), F32)]
        + [pltpu.HBM(whole, BF16)] * bool(owns),
        scratch_shapes=scratch,
        compiler_params=pltpu.CompilerParams(vmem_limit_bytes=VMEM_BYTES),
        cost_estimate=cost(estimate),
        name="project",
    )(place, *four, gain, weight, *owns)


def mix(kept, received, kept_mean, earlier, pairs, put, first=0):
    rows = kept.shape[1]
    last = first + received.shape[1]
    stat = received[:STAT_ROWS, : rows + -rows % HD].astype(F32)
    mean_peer = to_column(stat[0:1] + stat[1:2] + stat[2:3], rows)
    mean_kept = kept_mean[...]
    inverse = lax.rsqrt((mean_kept + mean_peer) * 0.5 + EPS)
    scale_kept = inverse * jnp.sqrt(mean_kept + EPS)
    scale_peer = inverse * jnp.sqrt(mean_peer + EPS)
    start = sum(ref.shape[1] for ref in earlier)
    padding = -(start + rows) % HD
    shape = (rows, start + rows + padding)
    causal = lax.broadcasted_iota(jnp.int32, shape, 0) + start >= lax.broadcasted_iota(
        jnp.int32, shape, 1
    )

    def together(k, at, mine):
        pieces = [ref[k, :, at] for ref in earlier] + [mine]
        if padding:
            pieces.append(jnp.zeros((padding, HD), BF16))
        return jnp.concatenate(pieces) if len(pieces) > 1 else mine

    heads = [slice(begin, begin + HD) for begin in range(first, last, HD)]
    held, scores = [], []
    for at in heads:
        queries, keys, values = (
            (
                kept[k, :, at] * scale_kept
                + received[
                    STAT_ROWS + k * rows : STAT_ROWS + (k + 1) * rows,
                    at.start - first : at.stop - first,
                ].astype(F32)
                * scale_peer
            ).astype(BF16)
            for k in range(3)
        )
        if pairs is not None:
            pairs[0, :, at] = keys
            pairs[1, :, at] = values
        held.append(together(1, at, values))
        score = lax.dot_general(
            queries, together(0, at, keys), (((1,), (1,)), ((), ())), preferred_element_type=F32
        )
        scores.append(jnp.where(causal, score * (1.0 / math.sqrt(HD)), F32(-1e30)))
    tops = [jnp.max(score, axis=-1, keepdims=True) for score in scores]
    raised = [jnp.exp(score - top) for score, top in zip(scores, tops)]
    overs = [1.0 / jnp.sum(item, axis=-1, keepdims=True) for item in raised]
    for at, item, over, values in zip(heads, raised, overs, held):
        put(at, jnp.dot((item * over).astype(BF16), values, preferred_element_type=F32))


def attend_kernel(first, kept, received, kept_mean, block, *refs):
    earlier, out, pairs = ((), *refs) if first else (refs[:1], refs[1], None)

    def put(at, mixture):
        out[:, at] = (block[:, at].astype(F32) + mixture).astype(BF16)

    mix(kept, received, kept_mean, earlier, pairs, put)


def hold_kernel(kept, received, kept_mean, held, pairs):
    def put(at, mixture):
        held[:, at] = mixture

    mix(kept, received, kept_mean, (), pairs, put)


def part_kernel(kept, received, kept_mean, earlier, held):
    def put(at, mixture):
        held[:, at] = mixture

    mix(kept, received, kept_mean, (earlier,), None, put)


def settle_kernel(flag, held, part, before, own, out, rest, rest_own):
    rows, done = held.shape[0], part.shape[1]
    shadow = flag[0] == 1

    def settle(here, at, mixture):
        result = jnp.where(
            shadow, before[here, at].astype(F32) + mixture, own[here, at].astype(F32)
        )
        out[here, at] = result.astype(BF16)

    upper, lower = slice(0, rows), slice(rows, rows + part.shape[0])
    settle(upper, slice(None), held[...])
    settle(lower, slice(0, done), part[...])
    out[lower, done:] = own[lower, done:]
    rest[...] = before[lower, done:]
    rest_own[...] = own[lower, done:]


def final_kernel(
    flag, kept, received, kept_mean, earlier, rest, rest_own, settled, out, piece, semaphore
):
    rows, width = kept.shape[1:]
    done = width - rest.shape[1]
    shadow = flag[0] == 1

    def put(at, mixture):
        here = slice(at.start - done, at.stop - done)
        result = rest[:, here].astype(F32) + mixture
        piece[:, here] = jnp.where(shadow, result, rest_own[:, here].astype(F32)).astype(BF16)

    mix(kept, received, kept_mean, (earlier,), None, put, done)
    copy = pltpu.make_async_copy(
        piece, out.at[pl.ds(out.shape[0] - rows, rows), pl.ds(done, width - done)], semaphore
    )
    copy.start()
    copy.wait()


def call_attend(kernel, name, scalars, arrays, out_shape):
    return pl.pallas_call(
        kernel,
        in_specs=[smem_spec() for _ in scalars] + [vmem_spec() for _ in arrays],
        out_shape=out_shape,
        compiler_params=pltpu.CompilerParams(vmem_limit_bytes=VMEM_BYTES),
        cost_estimate=cost(250),
        name=name,
    )(*scalars, *arrays)


def solution(mesh):
    sections = mesh.shape["section"]

    def local(inputs, qkv_weight, norm_gain, preempted):
        d = lax.axis_index("dp")
        t = lax.axis_index("tensor")
        y, c = t // 2, t % 2
        place = jnp.stack([c, d, (d == y).astype(c.dtype)]).astype(jnp.int32)
        place, diagonal, weight = lax.optimization_barrier((place, d == y, qkv_weight))
        weight = stage(place, weight)

        def spread(crossed, ringed):
            return (
                crossed,
                ringed,
                permute(crossed, sections, sibling),
                permute(ringed, sections, sibling),
            )

        def partial(four, apart, estimate, cuts=None, owns=()):
            rows, width = four[0].shape
            cuts_in = cuts or [(0, width)]
            results = project(
                rows, place, four, norm_gain, weight, cuts_in, apart, owns, estimate
            )
            received = [permute(sent, sections, peer) for sent in results[: len(cuts_in)]]
            kept, kept_mean, *whole = results[len(cuts_in) :]
            return (kept, received if cuts else received[0], kept_mean, *whole)

        block = inputs[0, 0]
        above, below = chunk_rows(block.shape[0])
        parts = [block[:above], block[above:]]
        ringed = [permute(part, sections, ring) for part in parts]
        crossed = permute(parts[0], sections, cross)
        ringed[0], crossed, weight = lax.optimization_barrier((ringed[0], crossed, weight))
        weight = pltpu.with_memory_space_constraint(weight, pltpu.VMEM)
        sums = [partial(spread(crossed, ringed[0]), False, 3)]
        late, _ = lax.optimization_barrier((ringed[1], sums[0][2]))
        forwarded = permute(late, sections, forward)
        crossed = jnp.where(diagonal, parts[1], forwarded)
        sums.append(partial(spread(crossed, late), True, 0.001))
        width = block.shape[1]
        pairs_of = pltpu.VMEM((2, above, width), BF16)

        def attend(part, item, held):
            return call_attend(
                functools.partial(attend_kernel, not held),
                "attend",
                [],
                [*item, part, *held],
                [pltpu.VMEM(part.shape, BF16)] + [pairs_of] * (not held),
            )

        def carry(own):
            return permute(own, sections, onward(cross))

        first, pairs = attend(parts[0], sums[0], [])
        moved = [carry(first)]
        swapped = permute(moved[0], sections, swap)
        beside = permute(moved[0], sections, sibling)
        part = lax.optimization_barrier((parts[1], beside))[0]
        (second,) = attend(part, sums[1], [pairs])
        moved.append(carry(second))
        swapped, _ = lax.optimization_barrier((swapped, second))
        four = moved[0], swapped, beside, permute(swapped, sections, sibling)
        *upper, own = partial(four, False, 3, None, [first, second])
        crossed, _ = lax.optimization_barrier((moved[1], upper[2]))
        swapped = permute(crossed, sections, swap)
        cut = (width // HD + 1) // 2 * HD
        cuts = [(0, cut), (cut, width)]
        kept, received, kept_mean = partial(spread(crossed, swapped), True, 2, cuts)
        before = permute(own, sections, onward(direct))
        before, *upper = lax.optimization_barrier((before, *upper))
        mixture, pairs = call_attend(
            hold_kernel, "hold", [], upper, [pltpu.VMEM((above, width), F32), pairs_of]
        )
        (part,) = call_attend(
            part_kernel,
            "part",
            [],
            [kept, received[0], kept_mean, pairs],
            [pltpu.VMEM((below, cut), F32)],
        )
        rest_of = pltpu.VMEM((below, width - cut), BF16)
        out, *rest = call_attend(
            settle_kernel,
            "settle",
            [preempted],
            [mixture, part, before, own],
            [jax.ShapeDtypeStruct(block.shape, BF16), rest_of, rest_of],
        )
        last = [kept, received[1], kept_mean, pairs, *rest]
        out = pl.pallas_call(
            final_kernel,
            in_specs=[smem_spec()] + [vmem_spec() for _ in last] + [any_spec()],
            out_specs=any_spec(),
            out_shape=jax.ShapeDtypeStruct(block.shape, BF16),
            input_output_aliases={1 + len(last): 0},
            scratch_shapes=[
                pltpu.VMEM((below, width - cut), BF16),
                pltpu.SemaphoreType.DMA(()),
            ],
            compiler_params=pltpu.CompilerParams(vmem_limit_bytes=VMEM_BYTES),
            cost_estimate=cost(250),
            name="final",
        )(preempted, *last, out)
        return out[None, None]

    placed = (
        P("section", "dp", None, "tensor"),
        P("section", None, "dp", "tensor"),
        P("section", None),
        P("section"),
    )
    return jax.shard_map(
        local,
        mesh=mesh,
        in_specs=placed,
        out_specs=P("section", "dp", None, "tensor"),
        check_vma=False,
    )
```

```python
import functools
import math

import jax
import jax.numpy as jnp
from jax import lax
from jax.experimental import pallas as pl
from jax.experimental.pallas import tpu as pltpu
from jax.sharding import PartitionSpec as P

HD = 128
EPS = 1e-05
AXES = ("section", "dp", "tensor")
F32 = jnp.float32
BF16 = jnp.bfloat16
VMEM_BYTES = 16 * 1024 * 1024
STAT_ROWS = 16


def chunk_rows(length):
    first = length // 2
    return [first, length - first]


def permute(array, sections, hop):
    pairs = []
    for s in range(sections):
        for d in range(2):
            for y in range(2):
                for c in range(2):
                    to = hop(s, d, y, c)
                    if to is None or not 0 <= to[0] < sections:
                        continue
                    ts, td, ty, tc = to
                    pairs.append((s * 8 + d * 4 + y * 2 + c, ts * 8 + td * 4 + ty * 2 + tc))
    return lax.ppermute(array, AXES, pairs)


def ring(s, d, y, c):
    return (s, 1 - d, y, c) if d != y else (s, d, 1 - y, c)


def cross(s, d, y, c):
    return (s, 1 - d, 1 - y, c) if d != y else (s, d, y, c)


def direct(s, d, y, c):
    return (s, d, y, c)


def forward(s, d, y, c):
    return (s, d, 1 - y, c) if d == y else None


def swap(s, d, y, c):
    return (s, d, 1 - y, c)


def sibling(s, d, y, c):
    return (s, d, y, 1 - c)


def peer(s, d, y, c):
    return (s, 1 - d, y, c)


def onward(hop):
    def moved(s, d, y, c):
        to = hop(s, d, y, c)
        return None if to is None else (to[0] + 1, *to[1:])

    return moved


def cost(microseconds):
    return pl.CostEstimate(flops=int(microseconds * 1.15e9), bytes_accessed=1000, transcendentals=0)


def any_spec():
    return pl.BlockSpec(memory_space=pl.ANY)


def vmem_spec():
    return pl.BlockSpec(memory_space=pltpu.VMEM)


def smem_spec():
    return pl.BlockSpec(memory_space=pltpu.SMEM)


def stage_kernel(place, weight, staged, semaphore):
    copy = pltpu.make_async_copy(weight, staged, semaphore)
    copy.start()
    copy.wait()


def stage(place, weight):
    return pl.pallas_call(
        stage_kernel,
        in_specs=[smem_spec(), any_spec()],
        out_specs=vmem_spec(),
        out_shape=pltpu.VMEM(weight.shape, weight.dtype),
        scratch_shapes=[pltpu.SemaphoreType.DMA(())],
        compiler_params=pltpu.CompilerParams(vmem_limit_bytes=VMEM_BYTES),
        cost_estimate=cost(4),
        name="stage",
    )(place, pltpu.with_memory_space_constraint(weight, pltpu.HBM))


def to_lanes(column):
    rows = column.shape[0]
    wide = jnp.broadcast_to(column, (rows, HD))
    if rows % HD:
        wide = jnp.concatenate([wide, jnp.zeros((-rows % HD, HD), F32)])
    tiles = [jnp.transpose(wide[i : i + HD])[:STAT_ROWS] for i in range(0, wide.shape[0], HD)]
    return jnp.concatenate(tiles, axis=1) if len(tiles) > 1 else tiles[0]


def to_column(row, rows):
    tiles = [
        jnp.transpose(jnp.broadcast_to(row[:, i : i + HD], (HD, HD)))
        for i in range(0, row.shape[1], HD)
    ]
    column = jnp.concatenate(tiles) if len(tiles) > 1 else tiles[0]
    return column[:rows, :1]


def normalize(mine, theirs, place, gain, normed, at):
    width = mine.shape[1]
    half = 2 * width
    core, dp = place[0], place[1]
    pieces = [ref[...].astype(F32) for ref in (mine, theirs)]
    squares = sum(jnp.sum(piece * piece, axis=-1, keepdims=True) for piece in pieces)
    mean = squares * (1.0 / half)
    inverse = lax.rsqrt(mean + EPS)
    for piece, order in zip(pieces, (core, 1 - core)):
        gains = gain[:, pl.ds(pl.multiple_of(dp * half + order * width, HD), width)]
        normed[at, pl.ds(pl.multiple_of(order * width, HD), width)] = (
            piece * inverse * gains.astype(F32)
        ).astype(BF16)
    return mean


def statistics(mean):
    row = to_lanes(mean)
    high = row.astype(BF16).astype(F32)
    mid = (row - high).astype(BF16).astype(F32)
    low = row - high - mid
    which = lax.broadcasted_iota(jnp.int32, row.shape, 0)
    return jnp.where(which == 0, high, jnp.where(which == 1, mid, low)).astype(BF16)


def put_statistics(out, stat):
    out[:STAT_ROWS] = jnp.zeros((STAT_ROWS, out.shape[1]), BF16)
    out[:STAT_ROWS, : stat.shape[1]] = stat


class Copies:
    def __init__(self, semaphores):
        self.semaphores, self.started = semaphores, []

    def start(self, source, target):
        copy = pltpu.make_async_copy(source, target, self.semaphores.at[len(self.started)])
        copy.start()
        self.started.append(copy)

    def wait(self):
        for copy in self.started:
            copy.wait()


def piece_of(k, rows):
    top = STAT_ROWS + k * rows
    return pl.ds(top, rows) if k else pl.ds(0, top + rows)


def project_kernel(
    apart, place, crossed, ringed, sib_crossed, sib_ringed, gain, weight, sent, kept, kept_mean, *refs
):
    normed, *out, semaphores = refs
    rows = normed.shape[0] // 2
    diagonal = place[2]
    copies = Copies(semaphores)
    out = out[0] if apart else sent
    means = []
    for mine, theirs, offset in (
        (crossed, sib_crossed, diagonal),
        (ringed, sib_ringed, 1 - diagonal),
    ):
        at = pl.ds(pl.multiple_of(offset * rows, rows), rows)
        means.append(normalize(mine, theirs, place, gain, normed, at))
    kept_mean[...] = jnp.where(diagonal == 1, means[0], means[1])
    put_statistics(out, statistics(jnp.where(diagonal == 1, means[1], means[0])))
    for k in range(3):
        product = jnp.dot(normed[...], weight[0, k], preferred_element_type=F32)
        top = STAT_ROWS + k * rows
        out[top : top + rows] = product[:rows].astype(BF16)
        kept[k] = product[rows:]
        if apart:
            copies.start(out.at[piece_of(k, rows)], sent.at[piece_of(k, rows)])
    copies.wait()


def project(place, four, gain, weight, apart, estimate):
    rows, width = four[0].shape
    shape = (3 * rows + STAT_ROWS, width)
    return pl.pallas_call(
        functools.partial(project_kernel, apart),
        in_specs=[smem_spec()] + [vmem_spec()] * 6,
        out_specs=[any_spec() if apart else vmem_spec()] + [vmem_spec()] * 2,
        out_shape=[
            (pltpu.HBM if apart else pltpu.VMEM)(shape, BF16),
            pltpu.VMEM((3, rows, width), F32),
            pltpu.VMEM((rows, 1), F32),
        ],
        scratch_shapes=[pltpu.VMEM((2 * rows, 2 * width), BF16)]
        + [pltpu.VMEM(shape, BF16)] * apart
        + [pltpu.SemaphoreType.DMA((3,))],
        compiler_params=pltpu.CompilerParams(vmem_limit_bytes=VMEM_BYTES),
        cost_estimate=cost(estimate),
        name="project",
    )(place, *four, gain, weight)


def early_kernel(count, place, mine, theirs, gain, weight, *refs):
    owns, (product, mean), kept = refs[:count], refs[count : count + 2], refs[count + 2 : -2]
    normed, semaphores = refs[-2:]
    copies = Copies(semaphores)
    for source, target in zip(owns, kept):
        copies.start(source, target)
    mean[...] = normalize(mine, theirs, place, gain, normed, slice(None))
    for k in range(3):
        product[k] = jnp.dot(normed[...], weight[0, k], preferred_element_type=F32)
    copies.wait()


def early(place, mine, theirs, gain, weight, owns, estimate):
    rows, width = mine.shape
    return pl.pallas_call(
        functools.partial(early_kernel, len(owns)),
        in_specs=[smem_spec()] + [vmem_spec() for _ in range(4 + len(owns))],
        out_specs=[vmem_spec(), vmem_spec()] + [any_spec() for _ in owns],
        out_shape=[pltpu.VMEM((3, rows, width), F32), pltpu.VMEM((rows, 1), F32)]
        + [pltpu.HBM(own.shape, BF16) for own in owns],
        scratch_shapes=[
            pltpu.VMEM((rows, 2 * width), BF16),
            pltpu.SemaphoreType.DMA((max(len(owns), 1),)),
        ],
        compiler_params=pltpu.CompilerParams(vmem_limit_bytes=VMEM_BYTES),
        cost_estimate=cost(estimate),
        name="early",
    )(place, mine, theirs, gain, weight, *owns)


def late_kernel(cuts, apart, place, mine, theirs, gain, weight, product, mean, *refs):
    count = len(cuts)
    sents, (kept, kept_mean, normed) = refs[:count], refs[count : count + 3]
    outs, semaphores = refs[count + 3 : -1] if apart else sents, refs[-1]
    rows = normed.shape[0]
    diagonal = place[2] == 1
    copies = Copies(semaphores)
    swapped_mean = normalize(mine, theirs, place, gain, normed, slice(None))
    kept_mean[...] = jnp.where(diagonal, mean[...], swapped_mean)
    stat = statistics(jnp.where(diagonal, swapped_mean, mean[...]))
    for (begin, end), out, sent in zip(cuts, outs, sents):
        put_statistics(out, stat)
        for k in range(3):
            swapped = jnp.dot(normed[...], weight[0, k, :, begin:end], preferred_element_type=F32)
            crossed = product[k, :, begin:end]
            top = STAT_ROWS + k * rows
            out[top : top + rows] = jnp.where(diagonal, swapped, crossed).astype(BF16)
            kept[k, :, begin:end] = jnp.where(diagonal, crossed, swapped)
            if apart:
                copies.start(out.at[piece_of(k, rows)], sent.at[piece_of(k, rows)])
    copies.wait()


def late(place, mine, theirs, gain, weight, product, mean, cuts, apart, estimate):
    rows, width = mine.shape
    shapes = [(3 * rows + STAT_ROWS, end - begin) for begin, end in cuts]
    return pl.pallas_call(
        functools.partial(late_kernel, cuts, apart),
        in_specs=[smem_spec()] + [vmem_spec()] * 6,
        out_specs=[any_spec() if apart else vmem_spec() for _ in cuts] + [vmem_spec()] * 2,
        out_shape=[(pltpu.HBM if apart else pltpu.VMEM)(shape, BF16) for shape in shapes]
        + [pltpu.VMEM((3, rows, width), F32), pltpu.VMEM((rows, 1), F32)],
        scratch_shapes=[pltpu.VMEM((rows, 2 * width), BF16)]
        + [pltpu.VMEM(shape, BF16) for shape in shapes] * apart
        + [pltpu.SemaphoreType.DMA((3 * len(cuts),))],
        compiler_params=pltpu.CompilerParams(vmem_limit_bytes=VMEM_BYTES),
        cost_estimate=cost(estimate),
        name="late",
    )(place, mine, theirs, gain, weight, product, mean)


def mix(kept, received, kept_mean, earlier, pairs, put, first=0):
    rows = kept.shape[1]
    last = first + received.shape[1]
    stat = received[:STAT_ROWS, : rows + -rows % HD].astype(F32)
    mean_peer = to_column(stat[0:1] + stat[1:2] + stat[2:3], rows)
    mean_kept = kept_mean[...]
    inverse = lax.rsqrt((mean_kept + mean_peer) * 0.5 + EPS)
    scale_kept = inverse * jnp.sqrt(mean_kept + EPS)
    scale_peer = inverse * jnp.sqrt(mean_peer + EPS)
    start = sum(ref.shape[1] for ref in earlier)
    padding = -(start + rows) % HD
    shape = (rows, start + rows + padding)
    causal = lax.broadcasted_iota(jnp.int32, shape, 0) + start >= lax.broadcasted_iota(
        jnp.int32, shape, 1
    )

    def together(k, at, mine):
        pieces = [ref[k, :, at] for ref in earlier] + [mine]
        if padding:
            pieces.append(jnp.zeros((padding, HD), BF16))
        return jnp.concatenate(pieces) if len(pieces) > 1 else mine

    heads = [slice(begin, begin + HD) for begin in range(first, last, HD)]
    held, scores = [], []
    for at in heads:
        queries, keys, values = (
            (
                kept[k, :, at] * scale_kept
                + received[
                    STAT_ROWS + k * rows : STAT_ROWS + (k + 1) * rows,
                    at.start - first : at.stop - first,
                ].astype(F32)
                * scale_peer
            ).astype(BF16)
            for k in range(3)
        )
        if pairs is not None:
            pairs[0, :, at] = keys
            pairs[1, :, at] = values
        held.append(together(1, at, values))
        score = lax.dot_general(
            queries, together(0, at, keys), (((1,), (1,)), ((), ())), preferred_element_type=F32
        )
        scores.append(jnp.where(causal, score * (1.0 / math.sqrt(HD)), F32(-1e30)))
    tops = [jnp.max(score, axis=-1, keepdims=True) for score in scores]
    raised = [jnp.exp(score - top) for score, top in zip(scores, tops)]
    overs = [1.0 / jnp.sum(item, axis=-1, keepdims=True) for item in raised]
    for at, item, over, values in zip(heads, raised, overs, held):
        put(at, jnp.dot((item * over).astype(BF16), values, preferred_element_type=F32))


def attend_kernel(first, kept, received, kept_mean, block, *refs):
    earlier, out, pairs = ((), *refs) if first else (refs[:1], refs[1], None)

    def put(at, mixture):
        out[:, at] = (block[:, at].astype(F32) + mixture).astype(BF16)

    mix(kept, received, kept_mean, earlier, pairs, put)


def hold_kernel(kept, received, kept_mean, held, pairs):
    def put(at, mixture):
        held[:, at] = mixture

    mix(kept, received, kept_mean, (), pairs, put)


def part_kernel(kept, received, kept_mean, earlier, held):
    def put(at, mixture):
        held[:, at] = mixture

    mix(kept, received, kept_mean, (earlier,), None, put)


def settle_kernel(flag, held, part, before, before_last, own, own_last, out, rest, rest_own):
    rows, done = held.shape[0], part.shape[1]
    shadow = flag[0] == 1

    def settle(mixture, before, own):
        result = jnp.where(shadow, before.astype(F32) + mixture, own.astype(F32))
        return result.astype(BF16)

    out[:rows] = settle(held[...], before[...], own[...])
    out[rows:, :done] = settle(part[...], before_last[:, :done], own_last[:, :done])
    out[rows:, done:] = own_last[:, done:]
    rest[...] = before_last[:, done:]
    rest_own[...] = own_last[:, done:]


def final_kernel(
    flag, kept, received, kept_mean, earlier, rest, rest_own, settled, out, piece, semaphore
):
    rows, width = kept.shape[1:]
    done = width - rest.shape[1]
    shadow = flag[0] == 1

    def put(at, mixture):
        here = slice(at.start - done, at.stop - done)
        result = rest[:, here].astype(F32) + mixture
        piece[:, here] = jnp.where(shadow, result, rest_own[:, here].astype(F32)).astype(BF16)

    mix(kept, received, kept_mean, (earlier,), None, put, done)
    copy = pltpu.make_async_copy(
        piece, out.at[pl.ds(out.shape[0] - rows, rows), pl.ds(done, width - done)], semaphore
    )
    copy.start()
    copy.wait()


def call_attend(kernel, name, scalars, arrays, out_shape):
    return pl.pallas_call(
        kernel,
        in_specs=[smem_spec() for _ in scalars] + [vmem_spec() for _ in arrays],
        out_shape=out_shape,
        compiler_params=pltpu.CompilerParams(vmem_limit_bytes=VMEM_BYTES),
        cost_estimate=cost(250),
        name=name,
    )(*scalars, *arrays)


def solution(mesh):
    sections = mesh.shape["section"]

    def local(inputs, qkv_weight, norm_gain, preempted):
        d = lax.axis_index("dp")
        t = lax.axis_index("tensor")
        y, c = t // 2, t % 2
        place = jnp.stack([c, d, (d == y).astype(c.dtype)]).astype(jnp.int32)
        place, diagonal, weight = lax.optimization_barrier((place, d == y, qkv_weight))
        weight = stage(place, weight)

        def spread(crossed, ringed):
            return (
                crossed,
                ringed,
                permute(crossed, sections, sibling),
                permute(ringed, sections, sibling),
            )

        def partial(four, apart, estimate):
            sent, kept, kept_mean = project(place, four, norm_gain, weight, apart, estimate)
            return kept, permute(sent, sections, peer), kept_mean

        block = inputs[0, 0]
        above, below = chunk_rows(block.shape[0])
        parts = [block[:above], block[above:]]
        ringed = [permute(part, sections, ring) for part in parts]
        crossed = permute(parts[0], sections, cross)
        ringed[0], crossed, weight = lax.optimization_barrier((ringed[0], crossed, weight))
        weight = pltpu.with_memory_space_constraint(weight, pltpu.VMEM)
        sums = [partial(spread(crossed, ringed[0]), False, 3)]
        behind, _ = lax.optimization_barrier((ringed[1], sums[0][2]))
        forwarded = permute(behind, sections, forward)
        crossed = jnp.where(diagonal, parts[1], forwarded)
        sums.append(partial(spread(crossed, behind), True, 0.001))
        width = block.shape[1]
        pairs_of = pltpu.VMEM((2, above, width), BF16)

        def attend(part, item, held):
            return call_attend(
                functools.partial(attend_kernel, not held),
                "attend",
                [],
                [*item, part, *held],
                [pltpu.VMEM(part.shape, BF16)] + [pairs_of] * (not held),
            )

        def carry(own):
            return permute(own, sections, onward(cross))

        part, _ = lax.optimization_barrier((parts[0], sums[1][2]))
        first, pairs = attend(part, sums[0], [])
        crossed = carry(first)
        swapped = permute(crossed, sections, swap)
        beside = permute(crossed, sections, sibling)
        product, mean = early(place, crossed, beside, norm_gain, weight, [], 0.001)
        part, _ = lax.optimization_barrier((parts[1], mean))
        (second,) = attend(part, sums[1], [pairs])
        later = carry(second)
        swapped, _ = lax.optimization_barrier((swapped, second))
        sent, *upper = late(
            place,
            swapped,
            permute(swapped, sections, sibling),
            norm_gain,
            weight,
            product,
            mean,
            [(0, width)],
            False,
            3,
        )
        arrived = permute(sent, sections, peer)
        crossed, _ = lax.optimization_barrier((later, upper[1]))
        swapped = permute(crossed, sections, swap)
        beside = permute(crossed, sections, sibling)
        product, mean, own, own_last = early(
            place, crossed, beside, norm_gain, weight, [first, second], 3
        )
        cut = (width // HD + 1) // 2 * HD
        cuts = [(0, cut), (cut, width)]
        *sents, kept, kept_mean = late(
            place,
            swapped,
            permute(swapped, sections, sibling),
            norm_gain,
            weight,
            product,
            mean,
            cuts,
            True,
            1,
        )
        received = [permute(sent, sections, peer) for sent in sents]
        before = permute(first, sections, onward(direct))
        before, arrived, _ = lax.optimization_barrier((before, arrived, kept_mean))
        mixture, pairs = call_attend(
            hold_kernel,
            "hold",
            [],
            [upper[0], arrived, upper[1]],
            [pltpu.VMEM((above, width), F32), pairs_of],
        )
        own_last, _ = lax.optimization_barrier((own_last, arrived))
        before_last = permute(own_last, sections, onward(direct))
        (part,) = call_attend(
            part_kernel,
            "part",
            [],
            [kept, received[0], kept_mean, pairs],
            [pltpu.VMEM((below, cut), F32)],
        )
        rest_of = pltpu.VMEM((below, width - cut), BF16)
        out, *rest = call_attend(
            settle_kernel,
            "settle",
            [preempted],
            [mixture, part, before, before_last, own, own_last],
            [jax.ShapeDtypeStruct(block.shape, BF16), rest_of, rest_of],
        )
        last = [kept, received[1], kept_mean, pairs, *rest]
        out = pl.pallas_call(
            final_kernel,
            in_specs=[smem_spec()] + [vmem_spec() for _ in last] + [any_spec()],
            out_specs=any_spec(),
            out_shape=jax.ShapeDtypeStruct(block.shape, BF16),
            input_output_aliases={1 + len(last): 0},
            scratch_shapes=[
                pltpu.VMEM((below, width - cut), BF16),
                pltpu.SemaphoreType.DMA(()),
            ],
            compiler_params=pltpu.CompilerParams(vmem_limit_bytes=VMEM_BYTES),
            cost_estimate=cost(250),
            name="final",
        )(preempted, *last, out)
        return out[None, None]

    placed = (
        P("section", "dp", None, "tensor"),
        P("section", None, "dp", "tensor"),
        P("section", None),
        P("section"),
    )
    return jax.shard_map(
        local,
        mesh=mesh,
        in_specs=placed,
        out_specs=P("section", "dp", None, "tensor"),
        check_vma=False,
    )
```

```python
import functools
import math

import jax
import jax.numpy as jnp
from jax import lax
from jax.experimental import pallas as pl
from jax.experimental.pallas import tpu as pltpu
from jax.sharding import PartitionSpec as P

HD = 128
EPS = 1e-05
AXES = ("section", "dp", "tensor")
F32 = jnp.float32
BF16 = jnp.bfloat16
VMEM_BYTES = 16 * 1024 * 1024
STAT_ROWS = 16


def chunk_rows(length):
    first = length // 2
    return [first, length - first]


def permute(array, sections, hop):
    pairs = []
    for s in range(sections):
        for d in range(2):
            for y in range(2):
                for c in range(2):
                    to = hop(s, d, y, c)
                    if to is None or not 0 <= to[0] < sections:
                        continue
                    ts, td, ty, tc = to
                    pairs.append((s * 8 + d * 4 + y * 2 + c, ts * 8 + td * 4 + ty * 2 + tc))
    return lax.ppermute(array, AXES, pairs)


def ring(s, d, y, c):
    return (s, 1 - d, y, c) if d != y else (s, d, 1 - y, c)


def cross(s, d, y, c):
    return (s, 1 - d, 1 - y, c) if d != y else (s, d, y, c)


def direct(s, d, y, c):
    return (s, d, y, c)


def forward(s, d, y, c):
    return (s, d, 1 - y, c) if d == y else None


def swap(s, d, y, c):
    return (s, d, 1 - y, c)


def sibling(s, d, y, c):
    return (s, d, y, 1 - c)


def peer(s, d, y, c):
    return (s, 1 - d, y, c)


def onward(hop):
    def moved(s, d, y, c):
        to = hop(s, d, y, c)
        return None if to is None else (to[0] + 1, *to[1:])

    return moved


def cost(microseconds):
    return pl.CostEstimate(flops=int(microseconds * 1.15e9), bytes_accessed=1000, transcendentals=0)


def any_spec():
    return pl.BlockSpec(memory_space=pl.ANY)


def vmem_spec():
    return pl.BlockSpec(memory_space=pltpu.VMEM)


def smem_spec():
    return pl.BlockSpec(memory_space=pltpu.SMEM)


def stage_kernel(place, weight, staged, semaphore):
    copy = pltpu.make_async_copy(weight, staged, semaphore)
    copy.start()
    copy.wait()


def stage(place, weight):
    return pl.pallas_call(
        stage_kernel,
        in_specs=[smem_spec(), any_spec()],
        out_specs=vmem_spec(),
        out_shape=pltpu.VMEM(weight.shape, weight.dtype),
        scratch_shapes=[pltpu.SemaphoreType.DMA(())],
        compiler_params=pltpu.CompilerParams(vmem_limit_bytes=VMEM_BYTES),
        cost_estimate=cost(4),
        name="stage",
    )(place, pltpu.with_memory_space_constraint(weight, pltpu.HBM))


def to_lanes(column):
    rows = column.shape[0]
    wide = jnp.broadcast_to(column, (rows, HD))
    if rows % HD:
        wide = jnp.concatenate([wide, jnp.zeros((-rows % HD, HD), F32)])
    tiles = [jnp.transpose(wide[i : i + HD])[:STAT_ROWS] for i in range(0, wide.shape[0], HD)]
    return jnp.concatenate(tiles, axis=1) if len(tiles) > 1 else tiles[0]


def to_column(row, rows):
    tiles = [
        jnp.transpose(jnp.broadcast_to(row[:, i : i + HD], (HD, HD)))
        for i in range(0, row.shape[1], HD)
    ]
    column = jnp.concatenate(tiles) if len(tiles) > 1 else tiles[0]
    return column[:rows, :1]


def normalize(mine, theirs, place, gain, normed, at):
    width = mine.shape[1]
    half = 2 * width
    core, dp = place[0], place[1]
    pieces = [ref[...].astype(F32) for ref in (mine, theirs)]
    squares = sum(jnp.sum(piece * piece, axis=-1, keepdims=True) for piece in pieces)
    mean = squares * (1.0 / half)
    inverse = lax.rsqrt(mean + EPS)
    for piece, order in zip(pieces, (core, 1 - core)):
        gains = gain[:, pl.ds(pl.multiple_of(dp * half + order * width, HD), width)]
        normed[at, pl.ds(pl.multiple_of(order * width, HD), width)] = (
            piece * inverse * gains.astype(F32)
        ).astype(BF16)
    return mean


def statistics(mean):
    row = to_lanes(mean)
    high = row.astype(BF16).astype(F32)
    mid = (row - high).astype(BF16).astype(F32)
    low = row - high - mid
    which = lax.broadcasted_iota(jnp.int32, row.shape, 0)
    return jnp.where(which == 0, high, jnp.where(which == 1, mid, low)).astype(BF16)


def put_statistics(out, stat):
    out[:STAT_ROWS] = jnp.zeros((STAT_ROWS, out.shape[1]), BF16)
    out[:STAT_ROWS, : stat.shape[1]] = stat


class Copies:
    def __init__(self, semaphores):
        self.semaphores, self.started = semaphores, []

    def start(self, source, target):
        copy = pltpu.make_async_copy(source, target, self.semaphores.at[len(self.started)])
        copy.start()
        self.started.append(copy)

    def wait(self):
        for copy in self.started:
            copy.wait()


def piece_of(k, rows, top):
    return pl.ds(top + k * rows, rows) if k else pl.ds(0, top + rows)


def tops_of(cuts):
    return [STAT_ROWS] + [0] * (len(cuts) - 1)


def project_kernel(
    cuts, apart, place, crossed, ringed, sib_crossed, sib_ringed, gain, weight, *refs
):
    count = len(cuts)
    sents, (kept, kept_mean, normed) = refs[:count], refs[count : count + 3]
    outs, semaphores = refs[count + 3 : -1] if apart else sents, refs[-1]
    rows = normed.shape[0] // 2
    diagonal = place[2]
    copies = Copies(semaphores)
    means = []
    for mine, theirs, offset in (
        (crossed, sib_crossed, diagonal),
        (ringed, sib_ringed, 1 - diagonal),
    ):
        at = pl.ds(pl.multiple_of(offset * rows, rows), rows)
        means.append(normalize(mine, theirs, place, gain, normed, at))
    kept_mean[...] = jnp.where(diagonal == 1, means[0], means[1])
    put_statistics(outs[0], statistics(jnp.where(diagonal == 1, means[1], means[0])))
    for (begin, end), out, sent, top in zip(cuts, outs, sents, tops_of(cuts)):
        for k in range(3):
            product = jnp.dot(normed[...], weight[0, k, :, begin:end], preferred_element_type=F32)
            out[top + k * rows : top + (k + 1) * rows] = product[:rows].astype(BF16)
            kept[k, :, begin:end] = product[rows:]
            if apart:
                at = piece_of(k, rows, top)
                copies.start(out.at[at], sent.at[at])
    copies.wait()


def project(place, four, gain, weight, cuts, apart, estimate):
    rows, width = four[0].shape
    shapes = [(top + 3 * rows, end - begin) for (begin, end), top in zip(cuts, tops_of(cuts))]
    return pl.pallas_call(
        functools.partial(project_kernel, cuts, apart),
        in_specs=[smem_spec()] + [vmem_spec()] * 6,
        out_specs=[any_spec() if apart else vmem_spec() for _ in cuts] + [vmem_spec()] * 2,
        out_shape=[(pltpu.HBM if apart else pltpu.VMEM)(shape, BF16) for shape in shapes]
        + [pltpu.VMEM((3, rows, width), F32), pltpu.VMEM((rows, 1), F32)],
        scratch_shapes=[pltpu.VMEM((2 * rows, 2 * width), BF16)]
        + [pltpu.VMEM(shape, BF16) for shape in shapes] * apart
        + [pltpu.SemaphoreType.DMA((3 * len(cuts),))],
        compiler_params=pltpu.CompilerParams(vmem_limit_bytes=VMEM_BYTES),
        cost_estimate=cost(estimate),
        name="project",
    )(place, *four, gain, weight)


def early_kernel(count, place, mine, theirs, gain, weight, *refs):
    owns, (product, mean), kept = refs[:count], refs[count : count + 2], refs[count + 2 : -2]
    normed, semaphores = refs[-2:]
    copies = Copies(semaphores)
    for source, target in zip(owns, kept):
        copies.start(source, target)
    mean[...] = normalize(mine, theirs, place, gain, normed, slice(None))
    for k in range(3):
        product[k] = jnp.dot(normed[...], weight[0, k], preferred_element_type=F32)
    copies.wait()


def early(place, mine, theirs, gain, weight, owns, estimate):
    rows, width = mine.shape
    return pl.pallas_call(
        functools.partial(early_kernel, len(owns)),
        in_specs=[smem_spec()] + [vmem_spec() for _ in range(4 + len(owns))],
        out_specs=[vmem_spec(), vmem_spec()] + [any_spec() for _ in owns],
        out_shape=[pltpu.VMEM((3, rows, width), F32), pltpu.VMEM((rows, 1), F32)]
        + [pltpu.HBM(own.shape, BF16) for own in owns],
        scratch_shapes=[
            pltpu.VMEM((rows, 2 * width), BF16),
            pltpu.SemaphoreType.DMA((max(len(owns), 1),)),
        ],
        compiler_params=pltpu.CompilerParams(vmem_limit_bytes=VMEM_BYTES),
        cost_estimate=cost(estimate),
        name="early",
    )(place, mine, theirs, gain, weight, *owns)


def late_kernel(cuts, apart, place, mine, theirs, gain, weight, product, mean, *refs):
    count = len(cuts)
    sents, (kept, kept_mean, normed) = refs[:count], refs[count : count + 3]
    outs, semaphores = refs[count + 3 : -1] if apart else sents, refs[-1]
    rows = normed.shape[0]
    diagonal = place[2] == 1
    copies = Copies(semaphores)
    swapped_mean = normalize(mine, theirs, place, gain, normed, slice(None))
    kept_mean[...] = jnp.where(diagonal, mean[...], swapped_mean)
    stat = statistics(jnp.where(diagonal, swapped_mean, mean[...]))
    put_statistics(outs[0], stat)
    for (begin, end), out, sent, top in zip(cuts, outs, sents, tops_of(cuts)):
        for k in range(3):
            swapped = jnp.dot(normed[...], weight[0, k, :, begin:end], preferred_element_type=F32)
            crossed = product[k, :, begin:end]
            out[top + k * rows : top + (k + 1) * rows] = jnp.where(
                diagonal, swapped, crossed
            ).astype(BF16)
            kept[k, :, begin:end] = jnp.where(diagonal, crossed, swapped)
            if apart:
                at = piece_of(k, rows, top)
                copies.start(out.at[at], sent.at[at])
    copies.wait()


def late(place, mine, theirs, gain, weight, product, mean, cuts, apart, estimate):
    rows, width = mine.shape
    shapes = [(top + 3 * rows, end - begin) for (begin, end), top in zip(cuts, tops_of(cuts))]
    return pl.pallas_call(
        functools.partial(late_kernel, cuts, apart),
        in_specs=[smem_spec()] + [vmem_spec()] * 6,
        out_specs=[any_spec() if apart else vmem_spec() for _ in cuts] + [vmem_spec()] * 2,
        out_shape=[(pltpu.HBM if apart else pltpu.VMEM)(shape, BF16) for shape in shapes]
        + [pltpu.VMEM((3, rows, width), F32), pltpu.VMEM((rows, 1), F32)],
        scratch_shapes=[pltpu.VMEM((rows, 2 * width), BF16)]
        + [pltpu.VMEM(shape, BF16) for shape in shapes] * apart
        + [pltpu.SemaphoreType.DMA((3 * len(cuts),))],
        compiler_params=pltpu.CompilerParams(vmem_limit_bytes=VMEM_BYTES),
        cost_estimate=cost(estimate),
        name="late",
    )(place, mine, theirs, gain, weight, product, mean)


def scales_of(received, kept_mean):
    rows = kept_mean.shape[0]
    stat = received[:STAT_ROWS, : rows + -rows % HD].astype(F32)
    mean_peer = to_column(stat[0:1] + stat[1:2] + stat[2:3], rows)
    mean_kept = kept_mean[...]
    inverse = lax.rsqrt((mean_kept + mean_peer) * 0.5 + EPS)
    scale_kept = inverse * jnp.sqrt(mean_kept + EPS)
    scale_peer = inverse * jnp.sqrt(mean_peer + EPS)
    return scale_kept, scale_peer


def mix(kept, received, scales, earlier, pairs, put, first=0, top=STAT_ROWS):
    rows = kept.shape[1]
    last = first + received.shape[1]
    scale_kept, scale_peer = scales
    start = sum(ref.shape[1] for ref in earlier)
    padding = -(start + rows) % HD
    shape = (rows, start + rows + padding)
    causal = lax.broadcasted_iota(jnp.int32, shape, 0) + start >= lax.broadcasted_iota(
        jnp.int32, shape, 1
    )

    def together(k, at, mine):
        pieces = [ref[k, :, at] for ref in earlier] + [mine]
        if padding:
            pieces.append(jnp.zeros((padding, HD), BF16))
        return jnp.concatenate(pieces) if len(pieces) > 1 else mine

    heads = [slice(begin, begin + HD) for begin in range(first, last, HD)]
    held, scores = [], []
    for at in heads:
        queries, keys, values = (
            (
                kept[k, :, at] * scale_kept
                + received[
                    top + k * rows : top + (k + 1) * rows,
                    at.start - first : at.stop - first,
                ].astype(F32)
                * scale_peer
            ).astype(BF16)
            for k in range(3)
        )
        if pairs is not None:
            pairs[0, :, at] = keys
            pairs[1, :, at] = values
        held.append(together(1, at, values))
        score = lax.dot_general(
            queries, together(0, at, keys), (((1,), (1,)), ((), ())), preferred_element_type=F32
        )
        scores.append(jnp.where(causal, score * (1.0 / math.sqrt(HD)), F32(-1e30)))
    tops = [jnp.max(score, axis=-1, keepdims=True) for score in scores]
    raised = [jnp.exp(score - top) for score, top in zip(scores, tops)]
    overs = [1.0 / jnp.sum(item, axis=-1, keepdims=True) for item in raised]
    for at, item, over, values in zip(heads, raised, overs, held):
        put(at, jnp.dot((item * over).astype(BF16), values, preferred_element_type=F32))


def attend_kernel(kept, received, kept_mean, block, out, pairs):
    def put(at, mixture):
        out[:, at] = (block[:, at].astype(F32) + mixture).astype(BF16)

    mix(kept, received, scales_of(received, kept_mean), (), pairs, put)


def hold_kernel(kept, received, kept_mean, held, pairs):
    def put(at, mixture):
        held[:, at] = mixture

    mix(kept, received, scales_of(received, kept_mean), (), pairs, put)


def part_kernel(kept, received, kept_mean, earlier, held, *scales):
    def put(at, mixture):
        held[:, at] = mixture

    found = scales_of(received, kept_mean)
    for ref, scale in zip(scales, found):
        ref[...] = scale
    mix(kept, received, found, (earlier,), None, put)


def next_kernel(kept, received, kept_mean, block, earlier, out):
    def put(at, mixture):
        out[:, at] = (block[:, at].astype(F32) + mixture).astype(BF16)

    mix(kept, received, scales_of(received, kept_mean), (earlier,), None, put)


def settle_kernel(flag, held, part, before, before_last, own, own_last, out, rest, rest_own):
    rows, done = held.shape[0], part.shape[1]
    shadow = flag[0] == 1

    def settle(mixture, before, own):
        result = jnp.where(shadow, before.astype(F32) + mixture, own.astype(F32))
        return result.astype(BF16)

    out[:rows] = settle(held[...], before[...], own[...])
    out[rows:, :done] = settle(part[...], before_last[:, :done], own_last[:, :done])
    out[rows:, done:] = own_last[:, done:]
    rest[...] = before_last[:, done:]
    rest_own[...] = own_last[:, done:]


def final_kernel(
    flag,
    kept,
    received,
    scale_kept,
    scale_peer,
    earlier,
    rest,
    rest_own,
    settled,
    out,
    piece,
    semaphore,
):
    rows, width = kept.shape[1:]
    done = width - rest.shape[1]
    shadow = flag[0] == 1

    def put(at, mixture):
        here = slice(at.start - done, at.stop - done)
        result = rest[:, here].astype(F32) + mixture
        piece[:, here] = jnp.where(shadow, result, rest_own[:, here].astype(F32)).astype(BF16)

    mix(kept, received, (scale_kept[...], scale_peer[...]), (earlier,), None, put, done, 0)
    copy = pltpu.make_async_copy(
        piece, out.at[pl.ds(out.shape[0] - rows, rows), pl.ds(done, width - done)], semaphore
    )
    copy.start()
    copy.wait()


def call_attend(kernel, name, scalars, arrays, out_shape):
    return pl.pallas_call(
        kernel,
        in_specs=[smem_spec() for _ in scalars] + [vmem_spec() for _ in arrays],
        out_shape=out_shape,
        compiler_params=pltpu.CompilerParams(vmem_limit_bytes=VMEM_BYTES),
        cost_estimate=cost(250),
        name=name,
    )(*scalars, *arrays)


def solution(mesh):
    sections = mesh.shape["section"]

    def local(inputs, qkv_weight, norm_gain, preempted):
        d = lax.axis_index("dp")
        t = lax.axis_index("tensor")
        y, c = t // 2, t % 2
        place = jnp.stack([c, d, (d == y).astype(c.dtype)]).astype(jnp.int32)
        place, diagonal, weight = lax.optimization_barrier((place, d == y, qkv_weight))
        weight = stage(place, weight)

        def spread(crossed, ringed):
            return (
                crossed,
                ringed,
                permute(crossed, sections, sibling),
                permute(ringed, sections, sibling),
            )

        def send(sents):
            return [permute(sent, sections, peer) for sent in sents]

        block = inputs[0, 0]
        above, below = chunk_rows(block.shape[0])
        parts = [block[:above], block[above:]]
        ringed = [permute(part, sections, ring) for part in parts]
        crossed = permute(parts[0], sections, cross)
        ringed[0], crossed, weight = lax.optimization_barrier((ringed[0], crossed, weight))
        weight = pltpu.with_memory_space_constraint(weight, pltpu.VMEM)
        width = block.shape[1]
        heads = width // HD
        sent, *sums = project(
            place, spread(crossed, ringed[0]), norm_gain, weight, [(0, width)], False, 3
        )
        (received,) = send([sent])
        behind, _ = lax.optimization_barrier((ringed[1], sums[1]))
        forwarded = permute(behind, sections, forward)
        crossed = jnp.where(diagonal, parts[1], forwarded)
        sent, *behind_sums = project(
            place, spread(crossed, behind), norm_gain, weight, [(0, width)], True, 0.001
        )
        (received_behind,) = send([sent])

        def carry(own):
            return permute(own, sections, onward(cross))

        def start_part(kept, received, kept_mean, earlier, part):
            column = pltpu.VMEM((below, 1), F32)
            return call_attend(
                part_kernel,
                "part",
                [],
                [kept, received, kept_mean, earlier],
                [pltpu.VMEM((below, part), F32), column, column],
            )

        pairs_of = pltpu.VMEM((2, above, width), BF16)
        part, _ = lax.optimization_barrier((parts[0], behind_sums[1]))
        first, pairs = call_attend(
            attend_kernel,
            "attend",
            [],
            [sums[0], received, sums[1], part],
            [pltpu.VMEM(part.shape, BF16), pairs_of],
        )
        crossed = carry(first)
        swapped = permute(crossed, sections, swap)
        beside = permute(crossed, sections, sibling)
        product, mean = early(place, crossed, beside, norm_gain, weight, [], 0.001)
        part, _ = lax.optimization_barrier((parts[1], mean))
        (second,) = call_attend(
            next_kernel,
            "attend",
            [],
            [behind_sums[0], received_behind, behind_sums[1], part, pairs],
            [pltpu.VMEM(part.shape, BF16)],
        )
        later = carry(second)
        swapped, _ = lax.optimization_barrier((swapped, second))
        sent, *upper = late(
            place,
            swapped,
            permute(swapped, sections, sibling),
            norm_gain,
            weight,
            product,
            mean,
            [(0, width)],
            False,
            3,
        )
        arrived = permute(sent, sections, peer)
        crossed, _ = lax.optimization_barrier((later, upper[1]))
        swapped = permute(crossed, sections, swap)
        beside = permute(crossed, sections, sibling)
        product, mean, own, own_last = early(
            place, crossed, beside, norm_gain, weight, [first, second], 3
        )
        cut = (heads * 2 + 2) // 3 * HD
        cuts = [(0, cut), (cut, width)]
        *sents, kept, kept_mean = late(
            place,
            swapped,
            permute(swapped, sections, sibling),
            norm_gain,
            weight,
            product,
            mean,
            cuts,
            True,
            1,
        )
        received = send(sents)
        before = permute(first, sections, onward(direct))
        before, arrived, _ = lax.optimization_barrier((before, arrived, kept_mean))
        mixture, pairs = call_attend(
            hold_kernel,
            "hold",
            [],
            [upper[0], arrived, upper[1]],
            [pltpu.VMEM((above, width), F32), pairs_of],
        )
        own_last, _ = lax.optimization_barrier((own_last, arrived))
        before_last = permute(own_last, sections, onward(direct))
        part, *scales = start_part(kept, received[0], kept_mean, pairs, cut)
        rest_of = pltpu.VMEM((below, width - cut), BF16)
        out, *rest = call_attend(
            settle_kernel,
            "settle",
            [preempted],
            [mixture, part, before, before_last, own, own_last],
            [jax.ShapeDtypeStruct(block.shape, BF16), rest_of, rest_of],
        )
        last = [kept, received[1], *scales, pairs, *rest]
        out = pl.pallas_call(
            final_kernel,
            in_specs=[smem_spec()] + [vmem_spec() for _ in last] + [any_spec()],
            out_specs=any_spec(),
            out_shape=jax.ShapeDtypeStruct(block.shape, BF16),
            input_output_aliases={1 + len(last): 0},
            scratch_shapes=[
                pltpu.VMEM((below, width - cut), BF16),
                pltpu.SemaphoreType.DMA(()),
            ],
            compiler_params=pltpu.CompilerParams(vmem_limit_bytes=VMEM_BYTES),
            cost_estimate=cost(250),
            name="final",
        )(preempted, *last, out)
        return out[None, None]

    placed = (
        P("section", "dp", None, "tensor"),
        P("section", None, "dp", "tensor"),
        P("section", None),
        P("section"),
    )
    return jax.shard_map(
        local,
        mesh=mesh,
        in_specs=placed,
        out_specs=P("section", "dp", None, "tensor"),
        check_vma=False,
    )
```

```python
import functools
import math

import jax
import jax.numpy as jnp
from jax import lax
from jax.experimental import pallas as pl
from jax.experimental.pallas import tpu as pltpu
from jax.sharding import PartitionSpec as P

HD = 128
EPS = 1e-05
AXES = ("section", "dp", "tensor")
F32 = jnp.float32
BF16 = jnp.bfloat16
VMEM_BYTES = 16 * 1024 * 1024
STAT_ROWS = 16


def chunk_rows(length):
    first = length // 2
    return [first, length - first]


def permute(array, sections, hop):
    pairs = []
    for s in range(sections):
        for d in range(2):
            for y in range(2):
                for c in range(2):
                    to = hop(s, d, y, c)
                    if to is None or not 0 <= to[0] < sections:
                        continue
                    ts, td, ty, tc = to
                    pairs.append((s * 8 + d * 4 + y * 2 + c, ts * 8 + td * 4 + ty * 2 + tc))
    return lax.ppermute(array, AXES, pairs)


def ring(s, d, y, c):
    return (s, 1 - d, y, c) if d != y else (s, d, 1 - y, c)


def cross(s, d, y, c):
    return (s, 1 - d, 1 - y, c) if d != y else (s, d, y, c)


def direct(s, d, y, c):
    return (s, d, y, c)


def forward(s, d, y, c):
    return (s, d, 1 - y, c) if d == y else None


def swap(s, d, y, c):
    return (s, d, 1 - y, c)


def sibling(s, d, y, c):
    return (s, d, y, 1 - c)


def peer(s, d, y, c):
    return (s, 1 - d, y, c)


def onward(hop):
    def moved(s, d, y, c):
        to = hop(s, d, y, c)
        return None if to is None else (to[0] + 1, *to[1:])

    return moved


def cost(microseconds):
    return pl.CostEstimate(flops=int(microseconds * 1.15e9), bytes_accessed=1000, transcendentals=0)


def any_spec():
    return pl.BlockSpec(memory_space=pl.ANY)


def vmem_spec():
    return pl.BlockSpec(memory_space=pltpu.VMEM)


def smem_spec():
    return pl.BlockSpec(memory_space=pltpu.SMEM)


def stage_kernel(place, weight, staged, semaphore):
    copy = pltpu.make_async_copy(weight, staged, semaphore)
    copy.start()
    copy.wait()


def stage(place, weight):
    return pl.pallas_call(
        stage_kernel,
        in_specs=[smem_spec(), any_spec()],
        out_specs=vmem_spec(),
        out_shape=pltpu.VMEM(weight.shape, weight.dtype),
        scratch_shapes=[pltpu.SemaphoreType.DMA(())],
        compiler_params=pltpu.CompilerParams(vmem_limit_bytes=VMEM_BYTES),
        cost_estimate=cost(4),
        name="stage",
    )(place, pltpu.with_memory_space_constraint(weight, pltpu.HBM))


def to_lanes(column):
    rows = column.shape[0]
    wide = jnp.broadcast_to(column, (rows, HD))
    if rows % HD:
        wide = jnp.concatenate([wide, jnp.zeros((-rows % HD, HD), F32)])
    tiles = [jnp.transpose(wide[i : i + HD])[:STAT_ROWS] for i in range(0, wide.shape[0], HD)]
    return jnp.concatenate(tiles, axis=1) if len(tiles) > 1 else tiles[0]


def to_column(row, rows):
    tiles = [
        jnp.transpose(jnp.broadcast_to(row[:, i : i + HD], (HD, HD)))
        for i in range(0, row.shape[1], HD)
    ]
    column = jnp.concatenate(tiles) if len(tiles) > 1 else tiles[0]
    return column[:rows, :1]


def normalize(mine, theirs, place, gain, normed, at):
    width = mine.shape[1]
    half = 2 * width
    core, dp = place[0], place[1]
    pieces = [ref[...].astype(F32) for ref in (mine, theirs)]
    squares = sum(jnp.sum(piece * piece, axis=-1, keepdims=True) for piece in pieces)
    mean = squares * (1.0 / half)
    inverse = lax.rsqrt(mean + EPS)
    for piece, order in zip(pieces, (core, 1 - core)):
        gains = gain[:, pl.ds(pl.multiple_of(dp * half + order * width, HD), width)]
        normed[at, pl.ds(pl.multiple_of(order * width, HD), width)] = (
            piece * inverse * gains.astype(F32)
        ).astype(BF16)
    return mean


def statistics(mean):
    row = to_lanes(mean)
    high = row.astype(BF16).astype(F32)
    mid = (row - high).astype(BF16).astype(F32)
    low = row - high - mid
    which = lax.broadcasted_iota(jnp.int32, row.shape, 0)
    return jnp.where(which == 0, high, jnp.where(which == 1, mid, low)).astype(BF16)


def put_statistics(out, stat):
    out[:STAT_ROWS] = jnp.zeros((STAT_ROWS, out.shape[1]), BF16)
    out[:STAT_ROWS, : stat.shape[1]] = stat


class Copies:
    def __init__(self, semaphores):
        self.semaphores, self.started = semaphores, []

    def start(self, source, target):
        copy = pltpu.make_async_copy(source, target, self.semaphores.at[len(self.started)])
        copy.start()
        self.started.append(copy)

    def wait(self):
        for copy in self.started:
            copy.wait()


def piece_of(k, rows, top):
    return pl.ds(top + k * rows, rows) if k else pl.ds(0, top + rows)


def tops_of(cuts):
    return [STAT_ROWS] + [0] * (len(cuts) - 1)


def project_kernel(
    cuts, apart, place, crossed, ringed, sib_crossed, sib_ringed, gain, weight, *refs
):
    count = len(cuts)
    sents, (kept, kept_mean, normed) = refs[:count], refs[count : count + 3]
    outs, semaphores = refs[count + 3 : -1] if apart else sents, refs[-1]
    rows = normed.shape[0] // 2
    diagonal = place[2]
    copies = Copies(semaphores)
    means = []
    for mine, theirs, offset in (
        (crossed, sib_crossed, diagonal),
        (ringed, sib_ringed, 1 - diagonal),
    ):
        at = pl.ds(pl.multiple_of(offset * rows, rows), rows)
        means.append(normalize(mine, theirs, place, gain, normed, at))
    kept_mean[...] = jnp.where(diagonal == 1, means[0], means[1])
    put_statistics(outs[0], statistics(jnp.where(diagonal == 1, means[1], means[0])))
    for (begin, end), out, sent, top in zip(cuts, outs, sents, tops_of(cuts)):
        for k in range(3):
            product = jnp.dot(normed[...], weight[0, k, :, begin:end], preferred_element_type=F32)
            out[top + k * rows : top + (k + 1) * rows] = product[:rows].astype(BF16)
            kept[k, :, begin:end] = product[rows:]
            if apart:
                at = piece_of(k, rows, top)
                copies.start(out.at[at], sent.at[at])
    copies.wait()


def project(place, four, gain, weight, cuts, apart, estimate):
    rows, width = four[0].shape
    shapes = [(top + 3 * rows, end - begin) for (begin, end), top in zip(cuts, tops_of(cuts))]
    return pl.pallas_call(
        functools.partial(project_kernel, cuts, apart),
        in_specs=[smem_spec()] + [vmem_spec()] * 6,
        out_specs=[any_spec() if apart else vmem_spec() for _ in cuts] + [vmem_spec()] * 2,
        out_shape=[(pltpu.HBM if apart else pltpu.VMEM)(shape, BF16) for shape in shapes]
        + [pltpu.VMEM((3, rows, width), F32), pltpu.VMEM((rows, 1), F32)],
        scratch_shapes=[pltpu.VMEM((2 * rows, 2 * width), BF16)]
        + [pltpu.VMEM(shape, BF16) for shape in shapes] * apart
        + [pltpu.SemaphoreType.DMA((3 * len(cuts),))],
        compiler_params=pltpu.CompilerParams(vmem_limit_bytes=VMEM_BYTES),
        cost_estimate=cost(estimate),
        name="project",
    )(place, *four, gain, weight)


def half_kernel(
    own, place, crossed, ringed, sib_crossed, sib_ringed, gain, weight, out, mean, normed
):
    rows = normed.shape[0]

    def from_pair(mine, theirs):
        mean[...] = normalize(mine, theirs, place, gain, normed, slice(None))

    crossed_is_ours = place[2] == int(own)

    @pl.when(crossed_is_ours)
    def _():
        from_pair(crossed, sib_crossed)

    @pl.when(jnp.logical_not(crossed_is_ours))
    def _():
        from_pair(ringed, sib_ringed)

    if not own:
        put_statistics(out, statistics(mean[...]))
    for k in range(3):
        product = jnp.dot(normed[...], weight[0, k], preferred_element_type=F32)
        if own:
            out[k] = product
        else:
            out[STAT_ROWS + k * rows : STAT_ROWS + (k + 1) * rows] = product.astype(BF16)


def half(own, place, four, gain, weight, estimate):
    rows, width = four[0].shape
    sent = pltpu.VMEM((3 * rows + STAT_ROWS, width), BF16)
    return pl.pallas_call(
        functools.partial(half_kernel, own),
        in_specs=[smem_spec()] + [vmem_spec()] * 6,
        out_shape=[
            pltpu.VMEM((3, rows, width), F32) if own else sent,
            pltpu.VMEM((rows, 1), F32),
        ],
        scratch_shapes=[pltpu.VMEM((rows, 2 * width), BF16)],
        compiler_params=pltpu.CompilerParams(vmem_limit_bytes=VMEM_BYTES),
        cost_estimate=cost(estimate),
        name="half",
    )(place, *four, gain, weight)


def early_kernel(count, place, mine, theirs, gain, weight, *refs):
    owns, (product, mean), kept = refs[:count], refs[count : count + 2], refs[count + 2 : -2]
    normed, semaphores = refs[-2:]
    copies = Copies(semaphores)
    for source, target in zip(owns, kept):
        copies.start(source, target)
    mean[...] = normalize(mine, theirs, place, gain, normed, slice(None))
    for k in range(3):
        product[k] = jnp.dot(normed[...], weight[0, k], preferred_element_type=F32)
    copies.wait()


def early(place, mine, theirs, gain, weight, owns, estimate):
    rows, width = mine.shape
    return pl.pallas_call(
        functools.partial(early_kernel, len(owns)),
        in_specs=[smem_spec()] + [vmem_spec() for _ in range(4 + len(owns))],
        out_specs=[vmem_spec(), vmem_spec()] + [any_spec() for _ in owns],
        out_shape=[pltpu.VMEM((3, rows, width), F32), pltpu.VMEM((rows, 1), F32)]
        + [pltpu.HBM(own.shape, BF16) for own in owns],
        scratch_shapes=[
            pltpu.VMEM((rows, 2 * width), BF16),
            pltpu.SemaphoreType.DMA((max(len(owns), 1),)),
        ],
        compiler_params=pltpu.CompilerParams(vmem_limit_bytes=VMEM_BYTES),
        cost_estimate=cost(estimate),
        name="early",
    )(place, mine, theirs, gain, weight, *owns)


def late_kernel(cuts, apart, place, mine, theirs, gain, weight, product, mean, *refs):
    count = len(cuts)
    sents, (kept, kept_mean, normed) = refs[:count], refs[count : count + 3]
    outs, semaphores = refs[count + 3 : -1] if apart else sents, refs[-1]
    rows = normed.shape[0]
    diagonal = place[2] == 1
    copies = Copies(semaphores)
    swapped_mean = normalize(mine, theirs, place, gain, normed, slice(None))
    kept_mean[...] = jnp.where(diagonal, mean[...], swapped_mean)
    stat = statistics(jnp.where(diagonal, swapped_mean, mean[...]))
    put_statistics(outs[0], stat)
    for (begin, end), out, sent, top in zip(cuts, outs, sents, tops_of(cuts)):
        for k in range(3):
            swapped = jnp.dot(normed[...], weight[0, k, :, begin:end], preferred_element_type=F32)
            crossed = product[k, :, begin:end]
            out[top + k * rows : top + (k + 1) * rows] = jnp.where(
                diagonal, swapped, crossed
            ).astype(BF16)
            kept[k, :, begin:end] = jnp.where(diagonal, crossed, swapped)
            if apart:
                at = piece_of(k, rows, top)
                copies.start(out.at[at], sent.at[at])
    copies.wait()


def late(place, mine, theirs, gain, weight, product, mean, cuts, apart, estimate):
    rows, width = mine.shape
    shapes = [(top + 3 * rows, end - begin) for (begin, end), top in zip(cuts, tops_of(cuts))]
    return pl.pallas_call(
        functools.partial(late_kernel, cuts, apart),
        in_specs=[smem_spec()] + [vmem_spec()] * 6,
        out_specs=[any_spec() if apart else vmem_spec() for _ in cuts] + [vmem_spec()] * 2,
        out_shape=[(pltpu.HBM if apart else pltpu.VMEM)(shape, BF16) for shape in shapes]
        + [pltpu.VMEM((3, rows, width), F32), pltpu.VMEM((rows, 1), F32)],
        scratch_shapes=[pltpu.VMEM((rows, 2 * width), BF16)]
        + [pltpu.VMEM(shape, BF16) for shape in shapes] * apart
        + [pltpu.SemaphoreType.DMA((3 * len(cuts),))],
        compiler_params=pltpu.CompilerParams(vmem_limit_bytes=VMEM_BYTES),
        cost_estimate=cost(estimate),
        name="late",
    )(place, mine, theirs, gain, weight, product, mean)


def scales_of(received, kept_mean):
    rows = kept_mean.shape[0]
    stat = received[:STAT_ROWS, : rows + -rows % HD].astype(F32)
    mean_peer = to_column(stat[0:1] + stat[1:2] + stat[2:3], rows)
    mean_kept = kept_mean[...]
    inverse = lax.rsqrt((mean_kept + mean_peer) * 0.5 + EPS)
    scale_kept = inverse * jnp.sqrt(mean_kept + EPS)
    scale_peer = inverse * jnp.sqrt(mean_peer + EPS)
    return scale_kept, scale_peer


def mix(kept, received, scales, earlier, pairs, put, first=0, top=STAT_ROWS):
    rows = kept.shape[1]
    last = first + received.shape[1]
    scale_kept, scale_peer = scales
    start = sum(ref.shape[1] for ref in earlier)
    padding = -(start + rows) % HD
    shape = (rows, start + rows + padding)
    causal = lax.broadcasted_iota(jnp.int32, shape, 0) + start >= lax.broadcasted_iota(
        jnp.int32, shape, 1
    )

    def together(k, at, mine):
        pieces = [ref[k, :, at] for ref in earlier] + [mine]
        if padding:
            pieces.append(jnp.zeros((padding, HD), BF16))
        return jnp.concatenate(pieces) if len(pieces) > 1 else mine

    heads = [slice(begin, begin + HD) for begin in range(first, last, HD)]
    held, scores = [], []
    for at in heads:
        queries, keys, values = (
            (
                kept[k, :, at] * scale_kept
                + received[
                    top + k * rows : top + (k + 1) * rows,
                    at.start - first : at.stop - first,
                ].astype(F32)
                * scale_peer
            ).astype(BF16)
            for k in range(3)
        )
        if pairs is not None:
            pairs[0, :, at] = keys
            pairs[1, :, at] = values
        held.append(together(1, at, values))
        score = lax.dot_general(
            queries, together(0, at, keys), (((1,), (1,)), ((), ())), preferred_element_type=F32
        )
        scores.append(jnp.where(causal, score * (1.0 / math.sqrt(HD)), F32(-1e30)))
    tops = [jnp.max(score, axis=-1, keepdims=True) for score in scores]
    raised = [jnp.exp(score - top) for score, top in zip(scores, tops)]
    overs = [1.0 / jnp.sum(item, axis=-1, keepdims=True) for item in raised]
    for at, item, over, values in zip(heads, raised, overs, held):
        put(at, jnp.dot((item * over).astype(BF16), values, preferred_element_type=F32))


def attend_kernel(kept, received, kept_mean, block, out, pairs):
    def put(at, mixture):
        out[:, at] = (block[:, at].astype(F32) + mixture).astype(BF16)

    mix(kept, received, scales_of(received, kept_mean), (), pairs, put)


def hold_kernel(kept, received, kept_mean, held, pairs):
    def put(at, mixture):
        held[:, at] = mixture

    mix(kept, received, scales_of(received, kept_mean), (), pairs, put)


def part_kernel(kept, received, kept_mean, earlier, held, *scales):
    def put(at, mixture):
        held[:, at] = mixture

    found = scales_of(received, kept_mean)
    for ref, scale in zip(scales, found):
        ref[...] = scale
    mix(kept, received, found, (earlier,), None, put)


def next_kernel(kept, received, kept_mean, block, earlier, out):
    def put(at, mixture):
        out[:, at] = (block[:, at].astype(F32) + mixture).astype(BF16)

    mix(kept, received, scales_of(received, kept_mean), (earlier,), None, put)


def settle_kernel(flag, held, before, own, out, piece, semaphore):
    result = before[...].astype(F32) + held[...]
    piece[...] = jnp.where(flag[0] == 1, result, own[...].astype(F32)).astype(BF16)
    copy = pltpu.make_async_copy(piece, out.at[pl.ds(0, piece.shape[0])], semaphore)
    copy.start()
    copy.wait()


def final_kernel(
    flag,
    kept,
    received,
    scale_kept,
    scale_peer,
    earlier,
    part,
    before,
    own,
    settled,
    out,
    piece,
    semaphore,
):
    done = part.shape[1]

    def put(at, mixture):
        result = before[:, at].astype(F32) + mixture
        piece[:, at] = jnp.where(flag[0] == 1, result, own[:, at].astype(F32)).astype(BF16)

    put(slice(0, done), part[...])
    mix(kept, received, (scale_kept[...], scale_peer[...]), (earlier,), None, put, done, 0)
    rows = piece.shape[0]
    copy = pltpu.make_async_copy(piece, out.at[pl.ds(out.shape[0] - rows, rows)], semaphore)
    copy.start()
    copy.wait()


def call_attend(kernel, name, scalars, arrays, out_shape):
    return pl.pallas_call(
        kernel,
        in_specs=[smem_spec() for _ in scalars] + [vmem_spec() for _ in arrays],
        out_shape=out_shape,
        compiler_params=pltpu.CompilerParams(vmem_limit_bytes=VMEM_BYTES),
        cost_estimate=cost(250),
        name=name,
    )(*scalars, *arrays)


def solution(mesh):
    sections = mesh.shape["section"]

    def local(inputs, qkv_weight, norm_gain, preempted):
        d = lax.axis_index("dp")
        t = lax.axis_index("tensor")
        y, c = t // 2, t % 2
        place = jnp.stack([c, d, (d == y).astype(c.dtype)]).astype(jnp.int32)
        place, diagonal, weight = lax.optimization_barrier((place, d == y, qkv_weight))
        weight = stage(place, weight)

        def spread(crossed, ringed):
            return (
                crossed,
                ringed,
                permute(crossed, sections, sibling),
                permute(ringed, sections, sibling),
            )

        def send(sents):
            return [permute(sent, sections, peer) for sent in sents]

        block = inputs[0, 0]
        above, below = chunk_rows(block.shape[0])
        parts = [block[:above], block[above:]]
        ringed = [permute(part, sections, ring) for part in parts]
        crossed = permute(parts[0], sections, cross)
        ringed[0], crossed, weight = lax.optimization_barrier((ringed[0], crossed, weight))
        weight = pltpu.with_memory_space_constraint(weight, pltpu.VMEM)
        width = block.shape[1]
        heads = width // HD
        four = spread(crossed, ringed[0])
        sent, mean = half(False, place, four, norm_gain, weight, 3)
        (received,) = send([sent])
        *four, _ = lax.optimization_barrier((*four, mean))
        sums = half(True, place, four, norm_gain, weight, 0.001)
        behind, _ = lax.optimization_barrier((ringed[1], mean))
        forwarded = permute(behind, sections, forward)
        forwarded, _ = lax.optimization_barrier((forwarded, sums[1]))
        crossed = jnp.where(diagonal, parts[1], forwarded)
        four = spread(crossed, behind)
        sent, *behind_sums = project(
            place, four, norm_gain, weight, [(0, width)], True, 0.001
        )
        (received_behind,) = send([sent])

        def carry(own):
            return permute(own, sections, onward(cross))

        def start_part(kept, received, kept_mean, earlier, part):
            column = pltpu.VMEM((below, 1), F32)
            return call_attend(
                part_kernel,
                "part",
                [],
                [kept, received, kept_mean, earlier],
                [pltpu.VMEM((below, part), F32), column, column],
            )

        pairs_of = pltpu.VMEM((2, above, width), BF16)
        part, _ = lax.optimization_barrier((parts[0], behind_sums[1]))
        first, pairs = call_attend(
            attend_kernel,
            "attend",
            [],
            [sums[0], received, sums[1], part],
            [pltpu.VMEM(part.shape, BF16), pairs_of],
        )
        crossed = carry(first)
        swapped = permute(crossed, sections, swap)
        beside = permute(crossed, sections, sibling)
        product, mean = early(place, crossed, beside, norm_gain, weight, [], 0.001)
        part, _ = lax.optimization_barrier((parts[1], mean))
        (second,) = call_attend(
            next_kernel,
            "attend",
            [],
            [behind_sums[0], received_behind, behind_sums[1], part, pairs],
            [pltpu.VMEM(part.shape, BF16)],
        )
        later = carry(second)
        swapped, _ = lax.optimization_barrier((swapped, second))
        sent, *upper = late(
            place,
            swapped,
            permute(swapped, sections, sibling),
            norm_gain,
            weight,
            product,
            mean,
            [(0, width)],
            False,
            3,
        )
        arrived = permute(sent, sections, peer)
        crossed, _ = lax.optimization_barrier((later, upper[1]))
        swapped = permute(crossed, sections, swap)
        beside = permute(crossed, sections, sibling)
        product, mean, own, own_last = early(
            place, crossed, beside, norm_gain, weight, [first, second], 3
        )
        cut = (heads * 2 + 2) // 3 * HD
        cuts = [(0, cut), (cut, width)]
        *sents, kept, kept_mean = late(
            place,
            swapped,
            permute(swapped, sections, sibling),
            norm_gain,
            weight,
            product,
            mean,
            cuts,
            True,
            1,
        )
        received = send(sents)
        before = permute(first, sections, onward(direct))
        before, arrived, _ = lax.optimization_barrier((before, arrived, kept_mean))
        mixture, pairs = call_attend(
            hold_kernel,
            "hold",
            [],
            [upper[0], arrived, upper[1]],
            [pltpu.VMEM((above, width), F32), pairs_of],
        )
        own_last, _ = lax.optimization_barrier((own_last, arrived))
        before_last = permute(own_last, sections, onward(direct))
        def finish(kernel, name, arrays, rows, into):
            whole = [] if into is None else [into]
            return pl.pallas_call(
                kernel,
                in_specs=[smem_spec()] + [vmem_spec() for _ in arrays] + [any_spec() for _ in whole],
                out_specs=any_spec(),
                out_shape=jax.ShapeDtypeStruct(block.shape, BF16),
                input_output_aliases={1 + len(arrays): 0} if whole else {},
                scratch_shapes=[pltpu.VMEM((rows, width), BF16), pltpu.SemaphoreType.DMA(())],
                compiler_params=pltpu.CompilerParams(vmem_limit_bytes=VMEM_BYTES),
                cost_estimate=cost(250),
                name=name,
            )(preempted, *arrays, *whole)

        out = finish(settle_kernel, "settle", [mixture, before, own], above, None)
        first_piece, _ = lax.optimization_barrier((received[0], out))
        part, *scales = start_part(kept, first_piece, kept_mean, pairs, cut)
        last = [kept, received[1], *scales, pairs, part, before_last, own_last]
        out = finish(final_kernel, "final", last, below, out)
        return out[None, None]

    placed = (
        P("section", "dp", None, "tensor"),
        P("section", None, "dp", "tensor"),
        P("section", None),
        P("section"),
    )
    return jax.shard_map(
        local,
        mesh=mesh,
        in_specs=placed,
        out_specs=P("section", "dp", None, "tensor"),
        check_vma=False,
    )
```

```python
import functools
import math

import jax
import jax.numpy as jnp
from jax import lax
from jax.experimental import pallas as pl
from jax.experimental.pallas import tpu as pltpu
from jax.sharding import PartitionSpec as P

HD = 128
EPS = 1e-05
AXES = ("section", "dp", "tensor")
F32 = jnp.float32
BF16 = jnp.bfloat16
VMEM_BYTES = 16 * 1024 * 1024
STAT_ROWS = 16


def chunk_rows(length):
    first = length // 2
    return [first, length - first]


def permute(array, sections, hop):
    pairs = []
    for s in range(sections):
        for d in range(2):
            for y in range(2):
                for c in range(2):
                    to = hop(s, d, y, c)
                    if to is None or not 0 <= to[0] < sections:
                        continue
                    ts, td, ty, tc = to
                    pairs.append((s * 8 + d * 4 + y * 2 + c, ts * 8 + td * 4 + ty * 2 + tc))
    return lax.ppermute(array, AXES, pairs)


def ring(s, d, y, c):
    return (s, 1 - d, y, c) if d != y else (s, d, 1 - y, c)


def cross(s, d, y, c):
    return (s, 1 - d, 1 - y, c) if d != y else (s, d, y, c)


def direct(s, d, y, c):
    return (s, d, y, c)


def forward(s, d, y, c):
    return (s, d, 1 - y, c) if d == y else None


def swap(s, d, y, c):
    return (s, d, 1 - y, c)


def sibling(s, d, y, c):
    return (s, d, y, 1 - c)


def peer(s, d, y, c):
    return (s, 1 - d, y, c)


def onward(hop):
    def moved(s, d, y, c):
        to = hop(s, d, y, c)
        return None if to is None else (to[0] + 1, *to[1:])

    return moved


def cost(microseconds):
    return pl.CostEstimate(flops=int(microseconds * 1.15e9), bytes_accessed=1000, transcendentals=0)


def any_spec():
    return pl.BlockSpec(memory_space=pl.ANY)


def vmem_spec():
    return pl.BlockSpec(memory_space=pltpu.VMEM)


def smem_spec():
    return pl.BlockSpec(memory_space=pltpu.SMEM)


def stage_kernel(place, weight, staged, semaphore):
    copy = pltpu.make_async_copy(weight, staged, semaphore)
    copy.start()
    copy.wait()


def stage(place, weight):
    return pl.pallas_call(
        stage_kernel,
        in_specs=[smem_spec(), any_spec()],
        out_specs=vmem_spec(),
        out_shape=pltpu.VMEM(weight.shape, weight.dtype),
        scratch_shapes=[pltpu.SemaphoreType.DMA(())],
        compiler_params=pltpu.CompilerParams(vmem_limit_bytes=VMEM_BYTES),
        cost_estimate=cost(4),
        name="stage",
    )(place, pltpu.with_memory_space_constraint(weight, pltpu.HBM))


def to_lanes(column):
    rows = column.shape[0]
    wide = jnp.broadcast_to(column, (rows, HD))
    if rows % HD:
        wide = jnp.concatenate([wide, jnp.zeros((-rows % HD, HD), F32)])
    tiles = [jnp.transpose(wide[i : i + HD])[:STAT_ROWS] for i in range(0, wide.shape[0], HD)]
    return jnp.concatenate(tiles, axis=1) if len(tiles) > 1 else tiles[0]


def to_column(row, rows):
    tiles = [
        jnp.transpose(jnp.broadcast_to(row[:, i : i + HD], (HD, HD)))
        for i in range(0, row.shape[1], HD)
    ]
    column = jnp.concatenate(tiles) if len(tiles) > 1 else tiles[0]
    return column[:rows, :1]


def normalize(mine, theirs, place, gain, normed, at):
    width = mine.shape[1]
    half = 2 * width
    core, dp = place[0], place[1]
    pieces = [ref[...].astype(F32) for ref in (mine, theirs)]
    squares = sum(jnp.sum(piece * piece, axis=-1, keepdims=True) for piece in pieces)
    mean = squares * (1.0 / half)
    inverse = lax.rsqrt(mean + EPS)
    for piece, order in zip(pieces, (core, 1 - core)):
        gains = gain[:, pl.ds(pl.multiple_of(dp * half + order * width, HD), width)]
        normed[at, pl.ds(pl.multiple_of(order * width, HD), width)] = (
            piece * inverse * gains.astype(F32)
        ).astype(BF16)
    return mean


def statistics(mean):
    row = to_lanes(mean)
    high = row.astype(BF16).astype(F32)
    mid = (row - high).astype(BF16).astype(F32)
    low = row - high - mid
    which = lax.broadcasted_iota(jnp.int32, row.shape, 0)
    return jnp.where(which == 0, high, jnp.where(which == 1, mid, low)).astype(BF16)


def put_statistics(out, stat):
    out[:STAT_ROWS] = jnp.zeros((STAT_ROWS, out.shape[1]), BF16)
    out[:STAT_ROWS, : stat.shape[1]] = stat


class Copies:
    def __init__(self, semaphores):
        self.semaphores, self.started = semaphores, []

    def start(self, source, target):
        copy = pltpu.make_async_copy(source, target, self.semaphores.at[len(self.started)])
        copy.start()
        self.started.append(copy)

    def wait(self):
        for copy in self.started:
            copy.wait()


def piece_of(k, rows, top):
    return pl.ds(top + k * rows, rows) if k else pl.ds(0, top + rows)


def tops_of(cuts):
    return [STAT_ROWS] + [0] * (len(cuts) - 1)


def half_kernel(
    own, place, crossed, ringed, sib_crossed, sib_ringed, gain, weight, out, mean, normed
):
    rows = normed.shape[0]

    def from_pair(mine, theirs):
        mean[...] = normalize(mine, theirs, place, gain, normed, slice(None))

    crossed_is_ours = place[2] == int(own)

    @pl.when(crossed_is_ours)
    def _():
        from_pair(crossed, sib_crossed)

    @pl.when(jnp.logical_not(crossed_is_ours))
    def _():
        from_pair(ringed, sib_ringed)

    if not own:
        put_statistics(out, statistics(mean[...]))
    for k in range(3):
        product = jnp.dot(normed[...], weight[0, k], preferred_element_type=F32)
        if own:
            out[k] = product
        else:
            out[STAT_ROWS + k * rows : STAT_ROWS + (k + 1) * rows] = product.astype(BF16)


def half(own, place, four, gain, weight, estimate):
    rows, width = four[0].shape
    sent = pltpu.VMEM((3 * rows + STAT_ROWS, width), BF16)
    return pl.pallas_call(
        functools.partial(half_kernel, own),
        in_specs=[smem_spec()] + [vmem_spec()] * 6,
        out_shape=[
            pltpu.VMEM((3, rows, width), F32) if own else sent,
            pltpu.VMEM((rows, 1), F32),
        ],
        scratch_shapes=[pltpu.VMEM((rows, 2 * width), BF16)],
        compiler_params=pltpu.CompilerParams(vmem_limit_bytes=VMEM_BYTES),
        cost_estimate=cost(estimate),
        name="half",
    )(place, *four, gain, weight)


def early_kernel(count, place, mine, theirs, gain, weight, *refs):
    owns, (product, mean), kept = refs[:count], refs[count : count + 2], refs[count + 2 : -2]
    normed, semaphores = refs[-2:]
    copies = Copies(semaphores)
    for source, target in zip(owns, kept):
        copies.start(source, target)
    mean[...] = normalize(mine, theirs, place, gain, normed, slice(None))
    for k in range(3):
        product[k] = jnp.dot(normed[...], weight[0, k], preferred_element_type=F32)
    copies.wait()


def early(place, mine, theirs, gain, weight, owns, estimate):
    rows, width = mine.shape
    return pl.pallas_call(
        functools.partial(early_kernel, len(owns)),
        in_specs=[smem_spec()] + [vmem_spec() for _ in range(4 + len(owns))],
        out_specs=[vmem_spec(), vmem_spec()] + [any_spec() for _ in owns],
        out_shape=[pltpu.VMEM((3, rows, width), F32), pltpu.VMEM((rows, 1), F32)]
        + [pltpu.HBM(own.shape, BF16) for own in owns],
        scratch_shapes=[
            pltpu.VMEM((rows, 2 * width), BF16),
            pltpu.SemaphoreType.DMA((max(len(owns), 1),)),
        ],
        compiler_params=pltpu.CompilerParams(vmem_limit_bytes=VMEM_BYTES),
        cost_estimate=cost(estimate),
        name="early",
    )(place, mine, theirs, gain, weight, *owns)


def late_kernel(cuts, apart, place, mine, theirs, gain, weight, product, mean, *refs):
    count = len(cuts)
    sents, (kept, kept_mean, normed) = refs[:count], refs[count : count + 3]
    outs, semaphores = refs[count + 3 : -1] if apart else sents, refs[-1]
    rows = normed.shape[0]
    diagonal = place[2] == 1
    copies = Copies(semaphores)
    swapped_mean = normalize(mine, theirs, place, gain, normed, slice(None))
    kept_mean[...] = jnp.where(diagonal, mean[...], swapped_mean)
    stat = statistics(jnp.where(diagonal, swapped_mean, mean[...]))
    put_statistics(outs[0], stat)
    for (begin, end), out, sent, top in zip(cuts, outs, sents, tops_of(cuts)):
        for k in range(3):
            swapped = jnp.dot(normed[...], weight[0, k, :, begin:end], preferred_element_type=F32)
            crossed = product[k, :, begin:end]
            out[top + k * rows : top + (k + 1) * rows] = jnp.where(
                diagonal, swapped, crossed
            ).astype(BF16)
            kept[k, :, begin:end] = jnp.where(diagonal, crossed, swapped)
            if apart:
                at = piece_of(k, rows, top)
                copies.start(out.at[at], sent.at[at])
    copies.wait()


def late(place, mine, theirs, gain, weight, product, mean, cuts, apart, estimate):
    rows, width = mine.shape
    shapes = [(top + 3 * rows, end - begin) for (begin, end), top in zip(cuts, tops_of(cuts))]
    return pl.pallas_call(
        functools.partial(late_kernel, cuts, apart),
        in_specs=[smem_spec()] + [vmem_spec()] * 6,
        out_specs=[any_spec() if apart else vmem_spec() for _ in cuts] + [vmem_spec()] * 2,
        out_shape=[(pltpu.HBM if apart else pltpu.VMEM)(shape, BF16) for shape in shapes]
        + [pltpu.VMEM((3, rows, width), F32), pltpu.VMEM((rows, 1), F32)],
        scratch_shapes=[pltpu.VMEM((rows, 2 * width), BF16)]
        + [pltpu.VMEM(shape, BF16) for shape in shapes] * apart
        + [pltpu.SemaphoreType.DMA((3 * len(cuts),))],
        compiler_params=pltpu.CompilerParams(vmem_limit_bytes=VMEM_BYTES),
        cost_estimate=cost(estimate),
        name="late",
    )(place, mine, theirs, gain, weight, product, mean)


def scales_of(received, kept_mean):
    rows = kept_mean.shape[0]
    stat = received[:STAT_ROWS, : rows + -rows % HD].astype(F32)
    mean_peer = to_column(stat[0:1] + stat[1:2] + stat[2:3], rows)
    mean_kept = kept_mean[...]
    inverse = lax.rsqrt((mean_kept + mean_peer) * 0.5 + EPS)
    scale_kept = inverse * jnp.sqrt(mean_kept + EPS)
    scale_peer = inverse * jnp.sqrt(mean_peer + EPS)
    return scale_kept, scale_peer


def mix(kept, received, scales, earlier, pairs, put, first=0, top=STAT_ROWS):
    rows = kept.shape[1]
    last = first + received.shape[1]
    scale_kept, scale_peer = scales
    start = sum(ref.shape[1] for ref in earlier)
    padding = -(start + rows) % HD
    shape = (rows, start + rows + padding)
    causal = lax.broadcasted_iota(jnp.int32, shape, 0) + start >= lax.broadcasted_iota(
        jnp.int32, shape, 1
    )

    def together(k, at, mine):
        pieces = [ref[k, :, at] for ref in earlier] + [mine]
        if padding:
            pieces.append(jnp.zeros((padding, HD), BF16))
        return jnp.concatenate(pieces) if len(pieces) > 1 else mine

    heads = [slice(begin, begin + HD) for begin in range(first, last, HD)]
    held, scores = [], []
    for at in heads:
        queries, keys, values = (
            (
                kept[k, :, at] * scale_kept
                + received[
                    top + k * rows : top + (k + 1) * rows,
                    at.start - first : at.stop - first,
                ].astype(F32)
                * scale_peer
            ).astype(BF16)
            for k in range(3)
        )
        if pairs is not None:
            pairs[0, :, at] = keys
            pairs[1, :, at] = values
        held.append(together(1, at, values))
        score = lax.dot_general(
            queries, together(0, at, keys), (((1,), (1,)), ((), ())), preferred_element_type=F32
        )
        scores.append(jnp.where(causal, score * (1.0 / math.sqrt(HD)), F32(-1e30)))
    tops = [jnp.max(score, axis=-1, keepdims=True) for score in scores]
    raised = [jnp.exp(score - top) for score, top in zip(scores, tops)]
    overs = [1.0 / jnp.sum(item, axis=-1, keepdims=True) for item in raised]
    for at, item, over, values in zip(heads, raised, overs, held):
        put(at, jnp.dot((item * over).astype(BF16), values, preferred_element_type=F32))


def attend_kernel(kept, received, kept_mean, block, out, pairs):
    def put(at, mixture):
        out[:, at] = (block[:, at].astype(F32) + mixture).astype(BF16)

    mix(kept, received, scales_of(received, kept_mean), (), pairs, put)


def hold_kernel(kept, received, kept_mean, held, pairs):
    def put(at, mixture):
        held[:, at] = mixture

    mix(kept, received, scales_of(received, kept_mean), (), pairs, put)


def part_kernel(kept, received, kept_mean, earlier, held, *scales):
    def put(at, mixture):
        held[:, at] = mixture

    found = scales_of(received, kept_mean)
    for ref, scale in zip(scales, found):
        ref[...] = scale
    mix(kept, received, found, (earlier,), None, put)


def next_kernel(kept, received, kept_mean, block, earlier, out):
    def put(at, mixture):
        out[:, at] = (block[:, at].astype(F32) + mixture).astype(BF16)

    mix(kept, received, scales_of(received, kept_mean), (earlier,), None, put)


def settle_kernel(flag, held, before, own, out, piece, semaphore):
    result = before[...].astype(F32) + held[...]
    piece[...] = jnp.where(flag[0] == 1, result, own[...].astype(F32)).astype(BF16)
    copy = pltpu.make_async_copy(piece, out.at[pl.ds(0, piece.shape[0])], semaphore)
    copy.start()
    copy.wait()


def final_kernel(
    flag,
    kept,
    received,
    scale_kept,
    scale_peer,
    earlier,
    part,
    before,
    own,
    settled,
    out,
    piece,
    semaphore,
):
    done = part.shape[1]

    def put(at, mixture):
        result = before[:, at].astype(F32) + mixture
        piece[:, at] = jnp.where(flag[0] == 1, result, own[:, at].astype(F32)).astype(BF16)

    put(slice(0, done), part[...])
    mix(kept, received, (scale_kept[...], scale_peer[...]), (earlier,), None, put, done, 0)
    rows = piece.shape[0]
    copy = pltpu.make_async_copy(piece, out.at[pl.ds(out.shape[0] - rows, rows)], semaphore)
    copy.start()
    copy.wait()


def call_attend(kernel, name, scalars, arrays, out_shape):
    return pl.pallas_call(
        kernel,
        in_specs=[smem_spec() for _ in scalars] + [vmem_spec() for _ in arrays],
        out_shape=out_shape,
        compiler_params=pltpu.CompilerParams(vmem_limit_bytes=VMEM_BYTES),
        cost_estimate=cost(250),
        name=name,
    )(*scalars, *arrays)


def solution(mesh):
    sections = mesh.shape["section"]

    def local(inputs, qkv_weight, norm_gain, preempted):
        d = lax.axis_index("dp")
        t = lax.axis_index("tensor")
        y, c = t // 2, t % 2
        place = jnp.stack([c, d, (d == y).astype(c.dtype)]).astype(jnp.int32)
        place, diagonal, weight = lax.optimization_barrier((place, d == y, qkv_weight))
        weight = stage(place, weight)

        def spread(crossed, ringed):
            return (
                crossed,
                ringed,
                permute(crossed, sections, sibling),
                permute(ringed, sections, sibling),
            )

        def send(sents):
            return [permute(sent, sections, peer) for sent in sents]

        block = inputs[0, 0]
        above, below = chunk_rows(block.shape[0])
        parts = [block[:above], block[above:]]
        ringed = [permute(part, sections, ring) for part in parts]
        crossed = permute(parts[0], sections, cross)
        ringed[0], crossed, weight = lax.optimization_barrier((ringed[0], crossed, weight))
        weight = pltpu.with_memory_space_constraint(weight, pltpu.VMEM)
        width = block.shape[1]
        heads = width // HD
        four = spread(crossed, ringed[0])
        sent, mean = half(False, place, four, norm_gain, weight, 3)
        (received,) = send([sent])
        *four, _ = lax.optimization_barrier((*four, mean))
        sums = half(True, place, four, norm_gain, weight, 0.001)
        behind, _ = lax.optimization_barrier((ringed[1], mean))
        forwarded = permute(behind, sections, forward)
        forwarded, _ = lax.optimization_barrier((forwarded, sums[1]))
        crossed = jnp.where(diagonal, parts[1], forwarded)
        four = spread(crossed, behind)
        sent, mean = half(False, place, four, norm_gain, weight, 0.001)
        (received_behind,) = send([sent])

        def carry(own):
            return permute(own, sections, onward(cross))

        def start_part(kept, received, kept_mean, earlier, part):
            column = pltpu.VMEM((below, 1), F32)
            return call_attend(
                part_kernel,
                "part",
                [],
                [kept, received, kept_mean, earlier],
                [pltpu.VMEM((below, part), F32), column, column],
            )

        pairs_of = pltpu.VMEM((2, above, width), BF16)
        part, _ = lax.optimization_barrier((parts[0], mean))
        first, pairs = call_attend(
            attend_kernel,
            "attend",
            [],
            [sums[0], received, sums[1], part],
            [pltpu.VMEM(part.shape, BF16), pairs_of],
        )
        *four, _ = lax.optimization_barrier((*four, first))
        behind_sums = half(True, place, four, norm_gain, weight, 0.001)
        crossed, _ = lax.optimization_barrier((carry(first), behind_sums[1]))
        swapped = permute(crossed, sections, swap)
        beside = permute(crossed, sections, sibling)
        product, mean = early(place, crossed, beside, norm_gain, weight, [], 0.001)
        part, _ = lax.optimization_barrier((parts[1], mean))
        (second,) = call_attend(
            next_kernel,
            "attend",
            [],
            [behind_sums[0], received_behind, behind_sums[1], part, pairs],
            [pltpu.VMEM(part.shape, BF16)],
        )
        later = carry(second)
        swapped, _ = lax.optimization_barrier((swapped, second))
        sent, *upper = late(
            place,
            swapped,
            permute(swapped, sections, sibling),
            norm_gain,
            weight,
            product,
            mean,
            [(0, width)],
            False,
            3,
        )
        arrived = permute(sent, sections, peer)
        crossed, _ = lax.optimization_barrier((later, upper[1]))
        swapped = permute(crossed, sections, swap)
        beside = permute(crossed, sections, sibling)
        product, mean, own, own_last = early(
            place, crossed, beside, norm_gain, weight, [first, second], 3
        )
        cut = (heads * 2 + 2) // 3 * HD
        cuts = [(0, cut), (cut, width)]
        *sents, kept, kept_mean = late(
            place,
            swapped,
            permute(swapped, sections, sibling),
            norm_gain,
            weight,
            product,
            mean,
            cuts,
            True,
            1,
        )
        received = send(sents)
        before = permute(first, sections, onward(direct))
        before, arrived, _ = lax.optimization_barrier((before, arrived, kept_mean))
        mixture, pairs = call_attend(
            hold_kernel,
            "hold",
            [],
            [upper[0], arrived, upper[1]],
            [pltpu.VMEM((above, width), F32), pairs_of],
        )
        own_last, _ = lax.optimization_barrier((own_last, arrived))
        before_last = permute(own_last, sections, onward(direct))
        def finish(kernel, name, arrays, rows, into):
            whole = [] if into is None else [into]
            return pl.pallas_call(
                kernel,
                in_specs=[smem_spec()] + [vmem_spec() for _ in arrays] + [any_spec() for _ in whole],
                out_specs=any_spec(),
                out_shape=jax.ShapeDtypeStruct(block.shape, BF16),
                input_output_aliases={1 + len(arrays): 0} if whole else {},
                scratch_shapes=[pltpu.VMEM((rows, width), BF16), pltpu.SemaphoreType.DMA(())],
                compiler_params=pltpu.CompilerParams(vmem_limit_bytes=VMEM_BYTES),
                cost_estimate=cost(250),
                name=name,
            )(preempted, *arrays, *whole)

        out = finish(settle_kernel, "settle", [mixture, before, own], above, None)
        first_piece, _ = lax.optimization_barrier((received[0], out))
        part, *scales = start_part(kept, first_piece, kept_mean, pairs, cut)
        last = [kept, received[1], *scales, pairs, part, before_last, own_last]
        out = finish(final_kernel, "final", last, below, out)
        return out[None, None]

    placed = (
        P("section", "dp", None, "tensor"),
        P("section", None, "dp", "tensor"),
        P("section", None),
        P("section"),
    )
    return jax.shard_map(
        local,
        mesh=mesh,
        in_specs=placed,
        out_specs=P("section", "dp", None, "tensor"),
        check_vma=False,
    )
```

```python
import functools
import math

import jax
import jax.numpy as jnp
from jax import lax
from jax.experimental import pallas as pl
from jax.experimental.pallas import tpu as pltpu
from jax.sharding import PartitionSpec as P

HD = 128
EPS = 1e-05
AXES = ("section", "dp", "tensor")
F32 = jnp.float32
BF16 = jnp.bfloat16
VMEM_BYTES = 16 * 1024 * 1024
STAT_ROWS = 16


def chunk_rows(length):
    first = length // 2
    return [first, length - first]


def permute(array, sections, hop):
    pairs = []
    for s in range(sections):
        for d in range(2):
            for y in range(2):
                for c in range(2):
                    to = hop(s, d, y, c)
                    if to is None or not 0 <= to[0] < sections:
                        continue
                    ts, td, ty, tc = to
                    pairs.append((s * 8 + d * 4 + y * 2 + c, ts * 8 + td * 4 + ty * 2 + tc))
    return lax.ppermute(array, AXES, pairs)


def ring(s, d, y, c):
    return (s, 1 - d, y, c) if d != y else (s, d, 1 - y, c)


def cross(s, d, y, c):
    return (s, 1 - d, 1 - y, c) if d != y else (s, d, y, c)


def direct(s, d, y, c):
    return (s, d, y, c)


def forward(s, d, y, c):
    return (s, d, 1 - y, c) if d == y else None


def swap(s, d, y, c):
    return (s, d, 1 - y, c)


def sibling(s, d, y, c):
    return (s, d, y, 1 - c)


def peer(s, d, y, c):
    return (s, 1 - d, y, c)


def onward(hop):
    def moved(s, d, y, c):
        to = hop(s, d, y, c)
        return None if to is None else (to[0] + 1, *to[1:])

    return moved


def cost(microseconds):
    return pl.CostEstimate(flops=int(microseconds * 1.15e9), bytes_accessed=1000, transcendentals=0)


def any_spec():
    return pl.BlockSpec(memory_space=pl.ANY)


def vmem_spec():
    return pl.BlockSpec(memory_space=pltpu.VMEM)


def smem_spec():
    return pl.BlockSpec(memory_space=pltpu.SMEM)


def stage_kernel(place, weight, staged, semaphore):
    copy = pltpu.make_async_copy(weight, staged, semaphore)
    copy.start()
    copy.wait()


def stage(place, weight):
    return pl.pallas_call(
        stage_kernel,
        in_specs=[smem_spec(), any_spec()],
        out_specs=vmem_spec(),
        out_shape=pltpu.VMEM(weight.shape, weight.dtype),
        scratch_shapes=[pltpu.SemaphoreType.DMA(())],
        compiler_params=pltpu.CompilerParams(vmem_limit_bytes=VMEM_BYTES),
        cost_estimate=cost(4),
        name="stage",
    )(place, pltpu.with_memory_space_constraint(weight, pltpu.HBM))


def to_lanes(column):
    rows = column.shape[0]
    wide = jnp.broadcast_to(column, (rows, HD))
    if rows % HD:
        wide = jnp.concatenate([wide, jnp.zeros((-rows % HD, HD), F32)])
    tiles = [jnp.transpose(wide[i : i + HD])[:STAT_ROWS] for i in range(0, wide.shape[0], HD)]
    return jnp.concatenate(tiles, axis=1) if len(tiles) > 1 else tiles[0]


def to_column(row, rows):
    tiles = [
        jnp.transpose(jnp.broadcast_to(row[:, i : i + HD], (HD, HD)))
        for i in range(0, row.shape[1], HD)
    ]
    column = jnp.concatenate(tiles) if len(tiles) > 1 else tiles[0]
    return column[:rows, :1]


def normalize(mine, theirs, place, gain, normed, at):
    width = mine.shape[1]
    half = 2 * width
    core, dp = place[0], place[1]
    pieces = [ref[...].astype(F32) for ref in (mine, theirs)]
    squares = sum(jnp.sum(piece * piece, axis=-1, keepdims=True) for piece in pieces)
    mean = squares * (1.0 / half)
    inverse = lax.rsqrt(mean + EPS)
    for piece, order in zip(pieces, (core, 1 - core)):
        gains = gain[:, pl.ds(pl.multiple_of(dp * half + order * width, HD), width)]
        normed[at, pl.ds(pl.multiple_of(order * width, HD), width)] = (
            piece * inverse * gains.astype(F32)
        ).astype(BF16)
    return mean


def statistics(mean):
    row = to_lanes(mean)
    high = row.astype(BF16).astype(F32)
    mid = (row - high).astype(BF16).astype(F32)
    low = row - high - mid
    which = lax.broadcasted_iota(jnp.int32, row.shape, 0)
    return jnp.where(which == 0, high, jnp.where(which == 1, mid, low)).astype(BF16)


def put_statistics(out, stat):
    out[:STAT_ROWS] = jnp.zeros((STAT_ROWS, out.shape[1]), BF16)
    out[:STAT_ROWS, : stat.shape[1]] = stat


class Copies:
    def __init__(self, semaphores):
        self.semaphores, self.started = semaphores, []

    def start(self, source, target):
        copy = pltpu.make_async_copy(source, target, self.semaphores.at[len(self.started)])
        copy.start()
        self.started.append(copy)

    def wait(self):
        for copy in self.started:
            copy.wait()


def piece_of(k, rows, top):
    return pl.ds(top + k * rows, rows) if k else pl.ds(0, top + rows)


def tops_of(cuts):
    return [STAT_ROWS] + [0] * (len(cuts) - 1)


def half_kernel(
    own, apart, place, crossed, ringed, sib_crossed, sib_ringed, gain, weight, to, mean, normed, *more
):
    rows = normed.shape[0]
    out, copies = (more[0], Copies(more[1])) if apart else (to, Copies(None))

    def from_pair(mine, theirs):
        mean[...] = normalize(mine, theirs, place, gain, normed, slice(None))

    crossed_is_ours = place[2] == int(own)

    @pl.when(crossed_is_ours)
    def _():
        from_pair(crossed, sib_crossed)

    @pl.when(jnp.logical_not(crossed_is_ours))
    def _():
        from_pair(ringed, sib_ringed)

    if not own:
        put_statistics(out, statistics(mean[...]))
    for k in range(3):
        product = jnp.dot(normed[...], weight[0, k], preferred_element_type=F32)
        if own:
            out[k] = product
        else:
            out[STAT_ROWS + k * rows : STAT_ROWS + (k + 1) * rows] = product.astype(BF16)
        if apart:
            at = piece_of(k, rows, STAT_ROWS)
            copies.start(out.at[at], to.at[at])
    copies.wait()


def half(own, apart, place, four, gain, weight, estimate):
    rows, width = four[0].shape
    shape = (3 * rows + STAT_ROWS, width)
    sent = (pltpu.HBM if apart else pltpu.VMEM)(shape, BF16)
    return pl.pallas_call(
        functools.partial(half_kernel, own, apart),
        in_specs=[smem_spec()] + [vmem_spec()] * 6,
        out_specs=[any_spec() if apart else vmem_spec(), vmem_spec()],
        out_shape=[
            pltpu.VMEM((3, rows, width), F32) if own else sent,
            pltpu.VMEM((rows, 1), F32),
        ],
        scratch_shapes=[pltpu.VMEM((rows, 2 * width), BF16)]
        + [pltpu.VMEM(shape, BF16), pltpu.SemaphoreType.DMA((3,))] * apart,
        compiler_params=pltpu.CompilerParams(vmem_limit_bytes=VMEM_BYTES),
        cost_estimate=cost(estimate),
        name="half",
    )(place, *four, gain, weight)


def early_kernel(count, place, mine, theirs, gain, weight, *refs):
    owns, (product, mean), kept = refs[:count], refs[count : count + 2], refs[count + 2 : -2]
    normed, semaphores = refs[-2:]
    copies = Copies(semaphores)
    for source, target in zip(owns, kept):
        copies.start(source, target)
    mean[...] = normalize(mine, theirs, place, gain, normed, slice(None))
    for k in range(3):
        product[k] = jnp.dot(normed[...], weight[0, k], preferred_element_type=F32)
    copies.wait()


def early(place, mine, theirs, gain, weight, owns, estimate):
    rows, width = mine.shape
    return pl.pallas_call(
        functools.partial(early_kernel, len(owns)),
        in_specs=[smem_spec()] + [vmem_spec() for _ in range(4 + len(owns))],
        out_specs=[vmem_spec(), vmem_spec()] + [any_spec() for _ in owns],
        out_shape=[pltpu.VMEM((3, rows, width), F32), pltpu.VMEM((rows, 1), F32)]
        + [pltpu.HBM(own.shape, BF16) for own in owns],
        scratch_shapes=[
            pltpu.VMEM((rows, 2 * width), BF16),
            pltpu.SemaphoreType.DMA((max(len(owns), 1),)),
        ],
        compiler_params=pltpu.CompilerParams(vmem_limit_bytes=VMEM_BYTES),
        cost_estimate=cost(estimate),
        name="early",
    )(place, mine, theirs, gain, weight, *owns)


def late_kernel(cuts, apart, place, mine, theirs, gain, weight, product, mean, *refs):
    count = len(cuts)
    sents, (kept, kept_mean, normed) = refs[:count], refs[count : count + 3]
    outs, semaphores = refs[count + 3 : -1] if apart else sents, refs[-1]
    rows = normed.shape[0]
    diagonal = place[2] == 1
    copies = Copies(semaphores)
    swapped_mean = normalize(mine, theirs, place, gain, normed, slice(None))
    kept_mean[...] = jnp.where(diagonal, mean[...], swapped_mean)
    stat = statistics(jnp.where(diagonal, swapped_mean, mean[...]))
    put_statistics(outs[0], stat)
    for (begin, end), out, sent, top in zip(cuts, outs, sents, tops_of(cuts)):
        for k in range(3):
            swapped = jnp.dot(normed[...], weight[0, k, :, begin:end], preferred_element_type=F32)
            crossed = product[k, :, begin:end]
            out[top + k * rows : top + (k + 1) * rows] = jnp.where(
                diagonal, swapped, crossed
            ).astype(BF16)
            kept[k, :, begin:end] = jnp.where(diagonal, crossed, swapped)
            if apart:
                at = piece_of(k, rows, top)
                copies.start(out.at[at], sent.at[at])
    copies.wait()


def late(place, mine, theirs, gain, weight, product, mean, cuts, apart, estimate):
    rows, width = mine.shape
    shapes = [(top + 3 * rows, end - begin) for (begin, end), top in zip(cuts, tops_of(cuts))]
    return pl.pallas_call(
        functools.partial(late_kernel, cuts, apart),
        in_specs=[smem_spec()] + [vmem_spec()] * 6,
        out_specs=[any_spec() if apart else vmem_spec() for _ in cuts] + [vmem_spec()] * 2,
        out_shape=[(pltpu.HBM if apart else pltpu.VMEM)(shape, BF16) for shape in shapes]
        + [pltpu.VMEM((3, rows, width), F32), pltpu.VMEM((rows, 1), F32)],
        scratch_shapes=[pltpu.VMEM((rows, 2 * width), BF16)]
        + [pltpu.VMEM(shape, BF16) for shape in shapes] * apart
        + [pltpu.SemaphoreType.DMA((3 * len(cuts),))],
        compiler_params=pltpu.CompilerParams(vmem_limit_bytes=VMEM_BYTES),
        cost_estimate=cost(estimate),
        name="late",
    )(place, mine, theirs, gain, weight, product, mean)


def scales_of(received, kept_mean):
    rows = kept_mean.shape[0]
    stat = received[:STAT_ROWS, : rows + -rows % HD].astype(F32)
    mean_peer = to_column(stat[0:1] + stat[1:2] + stat[2:3], rows)
    mean_kept = kept_mean[...]
    inverse = lax.rsqrt((mean_kept + mean_peer) * 0.5 + EPS)
    scale_kept = inverse * jnp.sqrt(mean_kept + EPS)
    scale_peer = inverse * jnp.sqrt(mean_peer + EPS)
    return scale_kept, scale_peer


def mix(kept, received, scales, earlier, pairs, put, first=0, top=STAT_ROWS):
    rows = kept.shape[1]
    last = first + received.shape[1]
    scale_kept, scale_peer = scales
    start = sum(ref.shape[1] for ref in earlier)
    padding = -(start + rows) % HD
    shape = (rows, start + rows + padding)
    causal = lax.broadcasted_iota(jnp.int32, shape, 0) + start >= lax.broadcasted_iota(
        jnp.int32, shape, 1
    )

    def together(k, at, mine):
        pieces = [ref[k, :, at] for ref in earlier] + [mine]
        if padding:
            pieces.append(jnp.zeros((padding, HD), BF16))
        return jnp.concatenate(pieces) if len(pieces) > 1 else mine

    heads = [slice(begin, begin + HD) for begin in range(first, last, HD)]
    held, scores = [], []
    for at in heads:
        queries, keys, values = (
            (
                kept[k, :, at] * scale_kept
                + received[
                    top + k * rows : top + (k + 1) * rows,
                    at.start - first : at.stop - first,
                ].astype(F32)
                * scale_peer
            ).astype(BF16)
            for k in range(3)
        )
        if pairs is not None:
            pairs[0, :, at] = keys
            pairs[1, :, at] = values
        held.append(together(1, at, values))
        score = lax.dot_general(
            queries, together(0, at, keys), (((1,), (1,)), ((), ())), preferred_element_type=F32
        )
        scores.append(jnp.where(causal, score * (1.0 / math.sqrt(HD)), F32(-1e30)))
    tops = [jnp.max(score, axis=-1, keepdims=True) for score in scores]
    raised = [jnp.exp(score - top) for score, top in zip(scores, tops)]
    overs = [1.0 / jnp.sum(item, axis=-1, keepdims=True) for item in raised]
    for at, item, over, values in zip(heads, raised, overs, held):
        put(at, jnp.dot((item * over).astype(BF16), values, preferred_element_type=F32))


def attend_kernel(kept, received, kept_mean, block, out, pairs):
    def put(at, mixture):
        out[:, at] = (block[:, at].astype(F32) + mixture).astype(BF16)

    mix(kept, received, scales_of(received, kept_mean), (), pairs, put)


def hold_kernel(kept, received, kept_mean, held, pairs):
    def put(at, mixture):
        held[:, at] = mixture

    mix(kept, received, scales_of(received, kept_mean), (), pairs, put)


def part_kernel(kept, received, kept_mean, earlier, held, *scales):
    def put(at, mixture):
        held[:, at] = mixture

    found = scales_of(received, kept_mean)
    for ref, scale in zip(scales, found):
        ref[...] = scale
    mix(kept, received, found, (earlier,), None, put)


def next_kernel(kept, received, kept_mean, block, earlier, out):
    def put(at, mixture):
        out[:, at] = (block[:, at].astype(F32) + mixture).astype(BF16)

    mix(kept, received, scales_of(received, kept_mean), (earlier,), None, put)


def settle_kernel(flag, held, before, own, out, piece, semaphore):
    result = before[...].astype(F32) + held[...]
    piece[...] = jnp.where(flag[0] == 1, result, own[...].astype(F32)).astype(BF16)
    copy = pltpu.make_async_copy(piece, out.at[pl.ds(0, piece.shape[0])], semaphore)
    copy.start()
    copy.wait()


def final_kernel(
    flag,
    kept,
    received,
    scale_kept,
    scale_peer,
    earlier,
    part,
    before,
    own,
    settled,
    out,
    piece,
    semaphore,
):
    done = part.shape[1]

    def put(at, mixture):
        result = before[:, at].astype(F32) + mixture
        piece[:, at] = jnp.where(flag[0] == 1, result, own[:, at].astype(F32)).astype(BF16)

    put(slice(0, done), part[...])
    mix(kept, received, (scale_kept[...], scale_peer[...]), (earlier,), None, put, done, 0)
    rows = piece.shape[0]
    copy = pltpu.make_async_copy(piece, out.at[pl.ds(out.shape[0] - rows, rows)], semaphore)
    copy.start()
    copy.wait()


def call_attend(kernel, name, scalars, arrays, out_shape):
    return pl.pallas_call(
        kernel,
        in_specs=[smem_spec() for _ in scalars] + [vmem_spec() for _ in arrays],
        out_shape=out_shape,
        compiler_params=pltpu.CompilerParams(vmem_limit_bytes=VMEM_BYTES),
        cost_estimate=cost(250),
        name=name,
    )(*scalars, *arrays)


def solution(mesh):
    sections = mesh.shape["section"]

    def local(inputs, qkv_weight, norm_gain, preempted):
        d = lax.axis_index("dp")
        t = lax.axis_index("tensor")
        y, c = t // 2, t % 2
        place = jnp.stack([c, d, (d == y).astype(c.dtype)]).astype(jnp.int32)
        place, diagonal, weight = lax.optimization_barrier((place, d == y, qkv_weight))
        weight = stage(place, weight)

        def spread(crossed, ringed):
            return (
                crossed,
                ringed,
                permute(crossed, sections, sibling),
                permute(ringed, sections, sibling),
            )

        def send(sents):
            return [permute(sent, sections, peer) for sent in sents]

        block = inputs[0, 0]
        above, below = chunk_rows(block.shape[0])
        parts = [block[:above], block[above:]]
        ringed = [permute(part, sections, ring) for part in parts]
        crossed = permute(parts[0], sections, cross)
        ringed[0], crossed, weight = lax.optimization_barrier((ringed[0], crossed, weight))
        weight = pltpu.with_memory_space_constraint(weight, pltpu.VMEM)
        width = block.shape[1]
        heads = width // HD
        four = spread(crossed, ringed[0])
        sent, mean = half(False, False, place, four, norm_gain, weight, 3)
        (received,) = send([sent])
        *four, _ = lax.optimization_barrier((*four, mean))
        sums = half(True, False, place, four, norm_gain, weight, 0.001)
        behind, _ = lax.optimization_barrier((ringed[1], mean))
        forwarded = permute(behind, sections, forward)
        forwarded, _ = lax.optimization_barrier((forwarded, sums[1]))
        crossed = jnp.where(diagonal, parts[1], forwarded)
        four = spread(crossed, behind)
        sent, mean = half(False, True, place, four, norm_gain, weight, 0.001)
        (received_behind,) = send([sent])

        def carry(own):
            return permute(own, sections, onward(cross))

        def start_part(kept, received, kept_mean, earlier, part):
            column = pltpu.VMEM((below, 1), F32)
            return call_attend(
                part_kernel,
                "part",
                [],
                [kept, received, kept_mean, earlier],
                [pltpu.VMEM((below, part), F32), column, column],
            )

        pairs_of = pltpu.VMEM((2, above, width), BF16)
        part, _ = lax.optimization_barrier((parts[0], mean))
        first, pairs = call_attend(
            attend_kernel,
            "attend",
            [],
            [sums[0], received, sums[1], part],
            [pltpu.VMEM(part.shape, BF16), pairs_of],
        )
        *four, _ = lax.optimization_barrier((*four, first))
        behind_sums = half(True, False, place, four, norm_gain, weight, 0.001)
        crossed, _ = lax.optimization_barrier((carry(first), behind_sums[1]))
        swapped = permute(crossed, sections, swap)
        beside = permute(crossed, sections, sibling)
        product, mean = early(place, crossed, beside, norm_gain, weight, [], 0.001)
        part, _ = lax.optimization_barrier((parts[1], mean))
        (second,) = call_attend(
            next_kernel,
            "attend",
            [],
            [behind_sums[0], received_behind, behind_sums[1], part, pairs],
            [pltpu.VMEM(part.shape, BF16)],
        )
        later = carry(second)
        swapped, _ = lax.optimization_barrier((swapped, second))
        sent, *upper = late(
            place,
            swapped,
            permute(swapped, sections, sibling),
            norm_gain,
            weight,
            product,
            mean,
            [(0, width)],
            False,
            3,
        )
        arrived = permute(sent, sections, peer)
        crossed, _ = lax.optimization_barrier((later, upper[1]))
        swapped = permute(crossed, sections, swap)
        beside = permute(crossed, sections, sibling)
        product, mean, own, own_last = early(
            place, crossed, beside, norm_gain, weight, [first, second], 3
        )
        cut = (heads * 2 + 2) // 3 * HD
        cuts = [(0, cut), (cut, width)]
        *sents, kept, kept_mean = late(
            place,
            swapped,
            permute(swapped, sections, sibling),
            norm_gain,
            weight,
            product,
            mean,
            cuts,
            True,
            1,
        )
        received = send(sents)
        before = permute(first, sections, onward(direct))
        before, arrived, _ = lax.optimization_barrier((before, arrived, kept_mean))
        mixture, pairs = call_attend(
            hold_kernel,
            "hold",
            [],
            [upper[0], arrived, upper[1]],
            [pltpu.VMEM((above, width), F32), pairs_of],
        )
        own_last, _ = lax.optimization_barrier((own_last, arrived))
        before_last = permute(own_last, sections, onward(direct))
        def finish(kernel, name, arrays, rows, into):
            whole = [] if into is None else [into]
            return pl.pallas_call(
                kernel,
                in_specs=[smem_spec()] + [vmem_spec() for _ in arrays] + [any_spec() for _ in whole],
                out_specs=any_spec(),
                out_shape=jax.ShapeDtypeStruct(block.shape, BF16),
                input_output_aliases={1 + len(arrays): 0} if whole else {},
                scratch_shapes=[pltpu.VMEM((rows, width), BF16), pltpu.SemaphoreType.DMA(())],
                compiler_params=pltpu.CompilerParams(vmem_limit_bytes=VMEM_BYTES),
                cost_estimate=cost(250),
                name=name,
            )(preempted, *arrays, *whole)

        out = finish(settle_kernel, "settle", [mixture, before, own], above, None)
        first_piece, _ = lax.optimization_barrier((received[0], out))
        part, *scales = start_part(kept, first_piece, kept_mean, pairs, cut)
        last = [kept, received[1], *scales, pairs, part, before_last, own_last]
        out = finish(final_kernel, "final", last, below, out)
        return out[None, None]

    placed = (
        P("section", "dp", None, "tensor"),
        P("section", None, "dp", "tensor"),
        P("section", None),
        P("section"),
    )
    return jax.shard_map(
        local,
        mesh=mesh,
        in_specs=placed,
        out_specs=P("section", "dp", None, "tensor"),
        check_vma=False,
    )
```

```python
import functools
import math

import jax
import jax.numpy as jnp
from jax import lax
from jax.experimental import pallas as pl
from jax.experimental.pallas import tpu as pltpu
from jax.sharding import PartitionSpec as P

HD = 128
EPS = 1e-05
AXES = ("section", "dp", "tensor")
F32 = jnp.float32
BF16 = jnp.bfloat16
VMEM_BYTES = 16 * 1024 * 1024
STAT_ROWS = 16


def chunk_rows(length):
    first = length // 2
    return [first, length - first]


def permute(array, sections, hop):
    pairs = []
    for s in range(sections):
        for d in range(2):
            for y in range(2):
                for c in range(2):
                    to = hop(s, d, y, c)
                    if to is None or not 0 <= to[0] < sections:
                        continue
                    ts, td, ty, tc = to
                    pairs.append((s * 8 + d * 4 + y * 2 + c, ts * 8 + td * 4 + ty * 2 + tc))
    return lax.ppermute(array, AXES, pairs)


def ring(s, d, y, c):
    return (s, 1 - d, y, c) if d != y else (s, d, 1 - y, c)


def cross(s, d, y, c):
    return (s, 1 - d, 1 - y, c) if d != y else (s, d, y, c)


def direct(s, d, y, c):
    return (s, d, y, c)


def forward(s, d, y, c):
    return (s, d, 1 - y, c) if d == y else None


def swap(s, d, y, c):
    return (s, d, 1 - y, c)


def sibling(s, d, y, c):
    return (s, d, y, 1 - c)


def peer(s, d, y, c):
    return (s, 1 - d, y, c)


def onward(hop):
    def moved(s, d, y, c):
        to = hop(s, d, y, c)
        return None if to is None else (to[0] + 1, *to[1:])

    return moved


def cost(microseconds):
    return pl.CostEstimate(flops=int(microseconds * 1.15e9), bytes_accessed=1000, transcendentals=0)


def any_spec():
    return pl.BlockSpec(memory_space=pl.ANY)


def vmem_spec():
    return pl.BlockSpec(memory_space=pltpu.VMEM)


def smem_spec():
    return pl.BlockSpec(memory_space=pltpu.SMEM)


def stage_kernel(place, weight, staged, semaphore):
    copy = pltpu.make_async_copy(weight, staged, semaphore)
    copy.start()
    copy.wait()


def stage(place, weight):
    return pl.pallas_call(
        stage_kernel,
        in_specs=[smem_spec(), any_spec()],
        out_specs=vmem_spec(),
        out_shape=pltpu.VMEM(weight.shape, weight.dtype),
        scratch_shapes=[pltpu.SemaphoreType.DMA(())],
        compiler_params=pltpu.CompilerParams(vmem_limit_bytes=VMEM_BYTES),
        cost_estimate=cost(4),
        name="stage",
    )(place, pltpu.with_memory_space_constraint(weight, pltpu.HBM))


def to_lanes(column):
    rows = column.shape[0]
    wide = jnp.broadcast_to(column, (rows, HD))
    if rows % HD:
        wide = jnp.concatenate([wide, jnp.zeros((-rows % HD, HD), F32)])
    tiles = [jnp.transpose(wide[i : i + HD])[:STAT_ROWS] for i in range(0, wide.shape[0], HD)]
    return jnp.concatenate(tiles, axis=1) if len(tiles) > 1 else tiles[0]


def to_column(row, rows):
    tiles = [
        jnp.transpose(jnp.broadcast_to(row[:, i : i + HD], (HD, HD)))
        for i in range(0, row.shape[1], HD)
    ]
    column = jnp.concatenate(tiles) if len(tiles) > 1 else tiles[0]
    return column[:rows, :1]


def normalize(mine, theirs, place, gain, normed, at):
    width = mine.shape[1]
    half = 2 * width
    core, dp = place[0], place[1]
    pieces = [ref[...].astype(F32) for ref in (mine, theirs)]
    squares = sum(jnp.sum(piece * piece, axis=-1, keepdims=True) for piece in pieces)
    mean = squares * (1.0 / half)
    inverse = lax.rsqrt(mean + EPS)
    for piece, order in zip(pieces, (core, 1 - core)):
        gains = gain[:, pl.ds(pl.multiple_of(dp * half + order * width, HD), width)]
        normed[at, pl.ds(pl.multiple_of(order * width, HD), width)] = (
            piece * inverse * gains.astype(F32)
        ).astype(BF16)
    return mean


def statistics(mean):
    row = to_lanes(mean)
    high = row.astype(BF16).astype(F32)
    mid = (row - high).astype(BF16).astype(F32)
    low = row - high - mid
    which = lax.broadcasted_iota(jnp.int32, row.shape, 0)
    return jnp.where(which == 0, high, jnp.where(which == 1, mid, low)).astype(BF16)


def put_statistics(out, stat):
    out[:STAT_ROWS] = jnp.zeros((STAT_ROWS, out.shape[1]), BF16)
    out[:STAT_ROWS, : stat.shape[1]] = stat


class Copies:
    def __init__(self, semaphores):
        self.semaphores, self.started = semaphores, []

    def start(self, source, target):
        copy = pltpu.make_async_copy(source, target, self.semaphores.at[len(self.started)])
        copy.start()
        self.started.append(copy)

    def wait(self):
        for copy in self.started:
            copy.wait()


def piece_of(k, rows, top):
    return pl.ds(top + k * rows, rows) if k else pl.ds(0, top + rows)


def tops_of(cuts):
    return [STAT_ROWS] + [0] * (len(cuts) - 1)


def half_kernel(
    own, place, crossed, ringed, sib_crossed, sib_ringed, gain, weight, out, mean, normed
):
    rows = normed.shape[0]

    def from_pair(mine, theirs):
        mean[...] = normalize(mine, theirs, place, gain, normed, slice(None))

    crossed_is_ours = place[2] == int(own)

    @pl.when(crossed_is_ours)
    def _():
        from_pair(crossed, sib_crossed)

    @pl.when(jnp.logical_not(crossed_is_ours))
    def _():
        from_pair(ringed, sib_ringed)

    if not own:
        put_statistics(out, statistics(mean[...]))
    for k in range(3):
        product = jnp.dot(normed[...], weight[0, k], preferred_element_type=F32)
        if own:
            out[k] = product
        else:
            out[STAT_ROWS + k * rows : STAT_ROWS + (k + 1) * rows] = product.astype(BF16)


def half(own, place, four, gain, weight, estimate):
    rows, width = four[0].shape
    sent = pltpu.VMEM((3 * rows + STAT_ROWS, width), BF16)
    return pl.pallas_call(
        functools.partial(half_kernel, own),
        in_specs=[smem_spec()] + [vmem_spec()] * 6,
        out_shape=[
            pltpu.VMEM((3, rows, width), F32) if own else sent,
            pltpu.VMEM((rows, 1), F32),
        ],
        scratch_shapes=[pltpu.VMEM((rows, 2 * width), BF16)],
        compiler_params=pltpu.CompilerParams(vmem_limit_bytes=VMEM_BYTES),
        cost_estimate=cost(estimate),
        name="half",
    )(place, *four, gain, weight)


def early_kernel(count, place, mine, theirs, gain, weight, *refs):
    owns, (product, mean), kept = refs[:count], refs[count : count + 2], refs[count + 2 : -2]
    normed, semaphores = refs[-2:]
    copies = Copies(semaphores)
    for source, target in zip(owns, kept):
        copies.start(source, target)
    mean[...] = normalize(mine, theirs, place, gain, normed, slice(None))
    for k in range(3):
        product[k] = jnp.dot(normed[...], weight[0, k], preferred_element_type=F32)
    copies.wait()


def early(place, mine, theirs, gain, weight, owns, estimate):
    rows, width = mine.shape
    return pl.pallas_call(
        functools.partial(early_kernel, len(owns)),
        in_specs=[smem_spec()] + [vmem_spec() for _ in range(4 + len(owns))],
        out_specs=[vmem_spec(), vmem_spec()] + [any_spec() for _ in owns],
        out_shape=[pltpu.VMEM((3, rows, width), F32), pltpu.VMEM((rows, 1), F32)]
        + [pltpu.HBM(own.shape, BF16) for own in owns],
        scratch_shapes=[
            pltpu.VMEM((rows, 2 * width), BF16),
            pltpu.SemaphoreType.DMA((max(len(owns), 1),)),
        ],
        compiler_params=pltpu.CompilerParams(vmem_limit_bytes=VMEM_BYTES),
        cost_estimate=cost(estimate),
        name="early",
    )(place, mine, theirs, gain, weight, *owns)


def late_kernel(cuts, apart, place, mine, theirs, gain, weight, product, mean, *refs):
    count = len(cuts)
    sents, (kept, kept_mean, normed) = refs[:count], refs[count : count + 3]
    outs, semaphores = refs[count + 3 : -1] if apart else sents, refs[-1]
    rows = normed.shape[0]
    diagonal = place[2] == 1
    copies = Copies(semaphores)
    swapped_mean = normalize(mine, theirs, place, gain, normed, slice(None))
    kept_mean[...] = jnp.where(diagonal, mean[...], swapped_mean)
    stat = statistics(jnp.where(diagonal, swapped_mean, mean[...]))
    put_statistics(outs[0], stat)
    for (begin, end), out, sent, top in zip(cuts, outs, sents, tops_of(cuts)):
        for k in range(3):
            swapped = jnp.dot(normed[...], weight[0, k, :, begin:end], preferred_element_type=F32)
            crossed = product[k, :, begin:end]
            out[top + k * rows : top + (k + 1) * rows] = jnp.where(
                diagonal, swapped, crossed
            ).astype(BF16)
            kept[k, :, begin:end] = jnp.where(diagonal, crossed, swapped)
            if apart:
                at = piece_of(k, rows, top)
                copies.start(out.at[at], sent.at[at])
    copies.wait()


def late(place, mine, theirs, gain, weight, product, mean, cuts, apart, estimate):
    rows, width = mine.shape
    shapes = [(top + 3 * rows, end - begin) for (begin, end), top in zip(cuts, tops_of(cuts))]
    return pl.pallas_call(
        functools.partial(late_kernel, cuts, apart),
        in_specs=[smem_spec()] + [vmem_spec()] * 6,
        out_specs=[any_spec() if apart else vmem_spec() for _ in cuts] + [vmem_spec()] * 2,
        out_shape=[(pltpu.HBM if apart else pltpu.VMEM)(shape, BF16) for shape in shapes]
        + [pltpu.VMEM((3, rows, width), F32), pltpu.VMEM((rows, 1), F32)],
        scratch_shapes=[pltpu.VMEM((rows, 2 * width), BF16)]
        + [pltpu.VMEM(shape, BF16) for shape in shapes] * apart
        + [pltpu.SemaphoreType.DMA((3 * len(cuts),))],
        compiler_params=pltpu.CompilerParams(vmem_limit_bytes=VMEM_BYTES),
        cost_estimate=cost(estimate),
        name="late",
    )(place, mine, theirs, gain, weight, product, mean)


def scales_of(received, kept_mean):
    rows = kept_mean.shape[0]
    stat = received[:STAT_ROWS, : rows + -rows % HD].astype(F32)
    mean_peer = to_column(stat[0:1] + stat[1:2] + stat[2:3], rows)
    mean_kept = kept_mean[...]
    inverse = lax.rsqrt((mean_kept + mean_peer) * 0.5 + EPS)
    scale_kept = inverse * jnp.sqrt(mean_kept + EPS)
    scale_peer = inverse * jnp.sqrt(mean_peer + EPS)
    return scale_kept, scale_peer


def mix(kept, received, scales, earlier, pairs, put, first=0, top=STAT_ROWS):
    rows = kept.shape[1]
    last = first + received.shape[1]
    scale_kept, scale_peer = scales
    start = sum(ref.shape[1] for ref in earlier)
    padding = -(start + rows) % HD
    shape = (rows, start + rows + padding)
    causal = lax.broadcasted_iota(jnp.int32, shape, 0) + start >= lax.broadcasted_iota(
        jnp.int32, shape, 1
    )

    def together(k, at, mine):
        pieces = [ref[k, :, at] for ref in earlier] + [mine]
        if padding:
            pieces.append(jnp.zeros((padding, HD), BF16))
        return jnp.concatenate(pieces) if len(pieces) > 1 else mine

    heads = [slice(begin, begin + HD) for begin in range(first, last, HD)]
    held, scores = [], []
    for at in heads:
        queries, keys, values = (
            (
                kept[k, :, at] * scale_kept
                + received[
                    top + k * rows : top + (k + 1) * rows,
                    at.start - first : at.stop - first,
                ].astype(F32)
                * scale_peer
            ).astype(BF16)
            for k in range(3)
        )
        if pairs is not None:
            pairs[0, :, at] = keys
            pairs[1, :, at] = values
        held.append(together(1, at, values))
        score = lax.dot_general(
            queries, together(0, at, keys), (((1,), (1,)), ((), ())), preferred_element_type=F32
        )
        scores.append(jnp.where(causal, score * (1.0 / math.sqrt(HD)), F32(-1e30)))
    tops = [jnp.max(score, axis=-1, keepdims=True) for score in scores]
    raised = [jnp.exp(score - top) for score, top in zip(scores, tops)]
    overs = [1.0 / jnp.sum(item, axis=-1, keepdims=True) for item in raised]
    for at, item, over, values in zip(heads, raised, overs, held):
        put(at, jnp.dot((item * over).astype(BF16), values, preferred_element_type=F32))


def attend_kernel(kept, received, kept_mean, block, out, pairs):
    def put(at, mixture):
        out[:, at] = (block[:, at].astype(F32) + mixture).astype(BF16)

    mix(kept, received, scales_of(received, kept_mean), (), pairs, put)


def hold_kernel(kept, received, kept_mean, held, pairs):
    def put(at, mixture):
        held[:, at] = mixture

    mix(kept, received, scales_of(received, kept_mean), (), pairs, put)


def part_kernel(kept, received, kept_mean, earlier, held, *scales):
    def put(at, mixture):
        held[:, at] = mixture

    found = scales_of(received, kept_mean)
    for ref, scale in zip(scales, found):
        ref[...] = scale
    mix(kept, received, found, (earlier,), None, put)


def next_kernel(kept, received, kept_mean, block, earlier, out):
    def put(at, mixture):
        out[:, at] = (block[:, at].astype(F32) + mixture).astype(BF16)

    mix(kept, received, scales_of(received, kept_mean), (earlier,), None, put)


def settle_kernel(flag, held, before, own, out, piece, semaphore):
    result = before[...].astype(F32) + held[...]
    piece[...] = jnp.where(flag[0] == 1, result, own[...].astype(F32)).astype(BF16)
    copy = pltpu.make_async_copy(piece, out.at[pl.ds(0, piece.shape[0])], semaphore)
    copy.start()
    copy.wait()


def final_kernel(
    flag,
    kept,
    received,
    scale_kept,
    scale_peer,
    earlier,
    part,
    before,
    own,
    settled,
    out,
    piece,
    semaphore,
):
    done = part.shape[1]

    def put(at, mixture):
        result = before[:, at].astype(F32) + mixture
        piece[:, at] = jnp.where(flag[0] == 1, result, own[:, at].astype(F32)).astype(BF16)

    put(slice(0, done), part[...])
    mix(kept, received, (scale_kept[...], scale_peer[...]), (earlier,), None, put, done, 0)
    rows = piece.shape[0]
    copy = pltpu.make_async_copy(piece, out.at[pl.ds(out.shape[0] - rows, rows)], semaphore)
    copy.start()
    copy.wait()


def call_attend(kernel, name, scalars, arrays, out_shape):
    return pl.pallas_call(
        kernel,
        in_specs=[smem_spec() for _ in scalars] + [vmem_spec() for _ in arrays],
        out_shape=out_shape,
        compiler_params=pltpu.CompilerParams(vmem_limit_bytes=VMEM_BYTES),
        cost_estimate=cost(250),
        name=name,
    )(*scalars, *arrays)


def solution(mesh):
    sections = mesh.shape["section"]

    def local(inputs, qkv_weight, norm_gain, preempted):
        d = lax.axis_index("dp")
        t = lax.axis_index("tensor")
        y, c = t // 2, t % 2
        place = jnp.stack([c, d, (d == y).astype(c.dtype)]).astype(jnp.int32)
        place, diagonal, weight = lax.optimization_barrier((place, d == y, qkv_weight))
        weight = stage(place, weight)

        def spread(crossed, ringed):
            return (
                crossed,
                ringed,
                permute(crossed, sections, sibling),
                permute(ringed, sections, sibling),
            )

        def send(sents):
            return [permute(sent, sections, peer) for sent in sents]

        block = inputs[0, 0]
        above, below = chunk_rows(block.shape[0])
        parts = [block[:above], block[above:]]
        ringed = [permute(part, sections, ring) for part in parts]
        crossed = permute(parts[0], sections, cross)
        ringed[0], crossed, weight = lax.optimization_barrier((ringed[0], crossed, weight))
        weight = pltpu.with_memory_space_constraint(weight, pltpu.VMEM)
        width = block.shape[1]
        heads = width // HD
        four = spread(crossed, ringed[0])
        sent, mean = half(False, place, four, norm_gain, weight, 3)
        (received,) = send([sent])
        *four, _ = lax.optimization_barrier((*four, mean))
        sums = half(True, place, four, norm_gain, weight, 0.001)
        behind, _ = lax.optimization_barrier((ringed[1], mean))
        forwarded = permute(behind, sections, forward)
        forwarded, _ = lax.optimization_barrier((forwarded, sums[1]))
        crossed = jnp.where(diagonal, parts[1], forwarded)
        four = spread(crossed, behind)
        sent, mean = half(False, place, four, norm_gain, weight, 0.001)
        (received_behind,) = send([sent])

        def carry(own):
            return permute(own, sections, onward(cross))

        def start_part(kept, received, kept_mean, earlier, part):
            column = pltpu.VMEM((below, 1), F32)
            return call_attend(
                part_kernel,
                "part",
                [],
                [kept, received, kept_mean, earlier],
                [pltpu.VMEM((below, part), F32), column, column],
            )

        pairs_of = pltpu.VMEM((2, above, width), BF16)
        part, _ = lax.optimization_barrier((parts[0], mean))
        first, pairs = call_attend(
            attend_kernel,
            "attend",
            [],
            [sums[0], received, sums[1], part],
            [pltpu.VMEM(part.shape, BF16), pairs_of],
        )
        *four, _ = lax.optimization_barrier((*four, first))
        behind_sums = half(True, place, four, norm_gain, weight, 0.001)
        crossed, _ = lax.optimization_barrier((carry(first), behind_sums[1]))
        swapped = permute(crossed, sections, swap)
        beside = permute(crossed, sections, sibling)
        product, mean = early(place, crossed, beside, norm_gain, weight, [], 0.001)
        part, _ = lax.optimization_barrier((parts[1], mean))
        (second,) = call_attend(
            next_kernel,
            "attend",
            [],
            [behind_sums[0], received_behind, behind_sums[1], part, pairs],
            [pltpu.VMEM(part.shape, BF16)],
        )
        later = carry(second)
        swapped, _ = lax.optimization_barrier((swapped, second))
        sent, *upper = late(
            place,
            swapped,
            permute(swapped, sections, sibling),
            norm_gain,
            weight,
            product,
            mean,
            [(0, width)],
            False,
            3,
        )
        arrived = permute(sent, sections, peer)
        crossed, _ = lax.optimization_barrier((later, upper[1]))
        swapped = permute(crossed, sections, swap)
        beside = permute(crossed, sections, sibling)
        product, mean, own, own_last = early(
            place, crossed, beside, norm_gain, weight, [first, second], 3
        )
        cut = (heads * 2 + 2) // 3 * HD
        cuts = [(0, cut), (cut, width)]
        *sents, kept, kept_mean = late(
            place,
            swapped,
            permute(swapped, sections, sibling),
            norm_gain,
            weight,
            product,
            mean,
            cuts,
            True,
            1,
        )
        received = send(sents)
        arrived, _ = lax.optimization_barrier((arrived, kept_mean))
        mixture, pairs = call_attend(
            hold_kernel,
            "hold",
            [],
            [upper[0], arrived, upper[1]],
            [pltpu.VMEM((above, width), F32), pairs_of],
        )
        own, own_last, _ = lax.optimization_barrier((own, own_last, arrived))
        before = permute(own, sections, onward(direct))
        before_last = permute(own_last, sections, onward(direct))
        def finish(kernel, name, arrays, rows, into):
            whole = [] if into is None else [into]
            return pl.pallas_call(
                kernel,
                in_specs=[smem_spec()] + [vmem_spec() for _ in arrays] + [any_spec() for _ in whole],
                out_specs=any_spec(),
                out_shape=jax.ShapeDtypeStruct(block.shape, BF16),
                input_output_aliases={1 + len(arrays): 0} if whole else {},
                scratch_shapes=[pltpu.VMEM((rows, width), BF16), pltpu.SemaphoreType.DMA(())],
                compiler_params=pltpu.CompilerParams(vmem_limit_bytes=VMEM_BYTES),
                cost_estimate=cost(250),
                name=name,
            )(preempted, *arrays, *whole)

        out = finish(settle_kernel, "settle", [mixture, before, own], above, None)
        first_piece, _ = lax.optimization_barrier((received[0], out))
        part, *scales = start_part(kept, first_piece, kept_mean, pairs, cut)
        last = [kept, received[1], *scales, pairs, part, before_last, own_last]
        out = finish(final_kernel, "final", last, below, out)
        return out[None, None]

    placed = (
        P("section", "dp", None, "tensor"),
        P("section", None, "dp", "tensor"),
        P("section", None),
        P("section"),
    )
    return jax.shard_map(
        local,
        mesh=mesh,
        in_specs=placed,
        out_specs=P("section", "dp", None, "tensor"),
        check_vma=False,
    )
```
